256 devices in a mesh: ctx: 64 (over y, z_hi, x, core), rep: 4 (over z_lo).
Axes of the slice: x: 4, y: 4, z: 8 (z_hi: 2, z_lo: 4; z = z_hi * 4 + z_lo), core: 2. Of those that a mesh axis runs over, the one named last changes fastest.
Arguments:
- features: bfloat16 [3, 16, 512, 8192], P(None, 'rep', None, 'ctx'), may hold values from -6 to 6
- short_taps: float32 [3, 16, 512, 3], P(None, 'rep'), may hold values from -3.5 to 3.5
- skip_gain: float32 [16, 512], P('rep', 'ctx'), may hold values from -4 to 4
- filters: float32 [512, 8192], P('ctx'), may hold values from -4 to 4
- cotangent: bfloat16 [16, 512, 8192], P('rep', None, 'ctx'), may hold values from -16 to 16
Outputs:
- d_features: bfloat16 [3, 16, 512, 8192], P(None, 'rep', None, 'ctx')
- d_short: float32 [3, 16, 512, 3], P(None, 'rep', 'ctx')
- d_skip: float32 [16, 512], P('rep', 'ctx')
- d_filter: float32 [512, 8192], P('ctx', 'rep')
The draws below stay inside these ranges and needn't reach their ends.
All inputs are finite; a program needn't handle non-finite values.
Results may differ from the reference program's by a relative error of at most 0.014.
Values may be sent and summed in bfloat16 or wider, within the bound.
A program may use at most 256 MiB of HBM per device.

```python
import math
import jax
import jax.numpy as jnp
from jax import lax

GRP = 16
NF = 512
TOKENS = 8192


def draw_filters(key, part):
    key = jax.random.fold_in(key, 11)
    rate_key, noise_key = jax.random.split(key)
    lowest = math.log(0.5 / TOKENS)
    highest = math.log(1.0 / 30.0)
    rate = jnp.exp(jax.random.uniform(rate_key, (NF, 1), jnp.float32, lowest, highest))
    places = jnp.arange(TOKENS, dtype=jnp.float32)[None, :]
    envelope = jnp.exp(-rate * places)
    energy = (1.0 - jnp.exp(-2.0 * rate * TOKENS)) / (1.0 - jnp.exp(-2.0 * rate))
    noise = jax.random.truncated_normal(noise_key, -4.0, 4.0, (NF, TOKENS), jnp.float32)
    return noise * envelope / jnp.sqrt(energy)


def draw_cotangent(key, part):
    key = jax.random.fold_in(key, 23)
    noise_key = jax.random.fold_in(key, 0)
    ramp = jnp.exp(math.log(3.0) * jnp.arange(TOKENS, dtype=jnp.float32) / max(TOKENS - 1, 1))
    noise = jax.random.truncated_normal(noise_key, -4.0, 4.0, (GRP, NF, TOKENS), jnp.float32)
    return (noise * ramp).astype(jnp.bfloat16)


def levels(own_key, extent, pieces, low, largest):
    gain = 1.0
    for dim, parts in pieces:
        draws = jax.random.uniform(jax.random.fold_in(jax.random.fold_in(own_key, 6), dim), (parts,), jnp.float32, low / len(pieces), largest / len(pieces))
        gain = gain * jnp.repeat(jnp.exp(draws), extent[dim] // parts).reshape((-1,) + (1,) * (len(extent) - 1 - dim))
    return gain


def centred(key, shape, scale, limit, shards=(), kind=jnp.bfloat16):
    array = jax.random.normal(key, shape, jnp.float32) * scale
    if len(shards) > 0:
        array = levels(key, shape, shards, -0.22, 0.18) * array
    return jnp.clip(array, min=-limit, max=limit).astype(kind)


def setup_inputs(seed: int = 0) -> dict:
    keys = jax.random.split(jax.random.key(seed), 6)
    features = centred(keys[0], (3, GRP, NF, TOKENS), 1.0, 6.0, ((1, 4), (3, 64)))
    short_taps = centred(keys[1], (3, GRP, NF, 3), 3 ** -0.5, 3.5, ((1, 4),), jnp.float32)
    skip_gain = centred(keys[2], (GRP, NF), 1.0, 4.0, ((0, 4), (1, 64)), jnp.float32)
    filters = draw_filters(jax.random.fold_in(keys[5], 71), 0)
    cotangent = draw_cotangent(jax.random.fold_in(keys[5], 71), 0)
    return dict(features=features, short_taps=short_taps, skip_gain=skip_gain, filters=filters, cotangent=cotangent)


def short_forward(signal, taps):
    length = signal.shape[-1]
    padded = jnp.pad(signal, [(0, 0)] * (signal.ndim - 1) + [(2, 0)])
    return taps[..., 0:1] * signal + taps[..., 1:2] * padded[..., 1:1 + length] + taps[..., 2:3] * padded[..., 0:length]

def short_backward(grads, taps):
    length = grads.shape[-1]
    padded = jnp.pad(grads, [(0, 0)] * (grads.ndim - 1) + [(0, 2)])
    return taps[..., 0:1] * grads + taps[..., 1:2] * padded[..., 1:1 + length] + taps[..., 2:3] * padded[..., 2:2 + length]

def short_taps_grad(grads, signal):
    length = signal.shape[-1]
    padded = jnp.pad(signal, [(0, 0)] * (signal.ndim - 1) + [(2, 0)])
    return jnp.stack([lax.optimization_barrier(jnp.sum(grads * signal, axis=-1)), lax.optimization_barrier(jnp.sum(grads * padded[..., 1:1 + length], axis=-1)), lax.optimization_barrier(jnp.sum(grads * padded[..., 0:length], axis=-1))], axis=-1)

def reference(features, short_taps, skip_gain, filters, cotangent):
    signal = features.astype(jnp.float32)
    length = signal.shape[-1]
    size = 2 * length
    mixed = short_forward(signal, short_taps)
    cot_full = cotangent.astype(jnp.float32)
    product = lax.optimization_barrier((mixed[1] * mixed[2]).astype(jnp.bfloat16)).astype(jnp.float32)
    gated = lax.optimization_barrier((cot_full * mixed[0]).astype(jnp.bfloat16)).astype(jnp.float32)
    filter_spec = jnp.fft.rfft(filters, size, axis=-1)

    def one_group(carry, pair):
        value_row, grad_row = pair
        value_spec = jnp.fft.rfft(value_row, size, axis=-1)
        grad_spec = jnp.fft.rfft(grad_row, size, axis=-1)
        forward_out = jnp.fft.irfft(filter_spec * value_spec, size, axis=-1)[:, :length]
        backward_out = jnp.fft.irfft(jnp.conj(filter_spec) * grad_spec, size, axis=-1)[:, :length]
        return (carry + grad_spec * jnp.conj(value_spec), (forward_out, backward_out))
    lag_spec, outs = lax.scan(one_group, jnp.zeros_like(filter_spec), (product, gated))
    conv_out, conv_grad = outs
    skip_col = skip_gain[..., None]
    conv_full = lax.optimization_barrier((conv_out + skip_col * product).astype(jnp.bfloat16)).astype(jnp.float32)
    value_grad = lax.optimization_barrier((conv_grad + skip_col * gated).astype(jnp.bfloat16)).astype(jnp.float32)
    d_filter = jnp.fft.irfft(lag_spec, size, axis=-1)[:, :length]
    d_skip = lax.optimization_barrier(jnp.sum(gated * product, axis=-1))
    grads = jnp.stack([cot_full * conv_full, value_grad * mixed[2], value_grad * mixed[1]])
    d_features = short_backward(grads, short_taps).astype(jnp.bfloat16)
    d_short = short_taps_grad(grads, signal)
    return (d_features, d_short, d_skip, d_filter)
```

```python
import math

import jax
import jax.numpy as jnp
from jax import lax
from jax.sharding import PartitionSpec as P

dft_mode = lax.Precision.HIGH


def shifted(block, axis, distance):
    devices = range(lax.axis_size(axis))
    route = [(i - distance, i) for i in devices if i - distance in devices]
    return lax.ppermute(block, axis, route)


def square_table(count):
    index = jnp.arange(count, dtype=jnp.int32)
    angle = (index[:, None] * index[None, :] % count).astype(jnp.float32) * (2.0 * math.pi / count)
    return (jnp.cos(angle), jnp.sin(angle))


def make_plan(length):
    total = 2 * length
    outer = min(128, total)
    inner = total // outer
    outer_cos, outer_sin = square_table(outer)
    inner_cos, inner_sin = square_table(inner)
    rows_index = jnp.arange(outer, dtype=jnp.int32)[:, None]
    cols_index = jnp.arange(inner, dtype=jnp.int32)[None, :]
    angle = (rows_index * cols_index % total).astype(jnp.float32) * (2.0 * math.pi / total)
    return (
        outer_cos,
        outer_sin,
        jnp.cos(angle),
        jnp.sin(angle),
        inner_cos,
        inner_sin,
        outer,
        inner,
    )


def spectrum(signal, plan):
    outer_cos, outer_sin, twist_cos, twist_sin, inner_cos, inner_sin, outer, inner = plan
    half = outer // 2
    grid = signal.reshape(-1, half, inner)
    first_re = jnp.einsum("kn,bnq->bkq", outer_cos[:, :half], grid, precision=dft_mode)
    first_im = -jnp.einsum("kn,bnq->bkq", outer_sin[:, :half], grid, precision=dft_mode)
    turned_re = (first_re * twist_cos + first_im * twist_sin).reshape(-1, inner)
    turned_im = (first_im * twist_cos - first_re * twist_sin).reshape(-1, inner)
    out_re = jnp.dot(turned_re, inner_cos, precision=dft_mode) + jnp.dot(
        turned_im, inner_sin, precision=dft_mode
    )
    out_im = jnp.dot(turned_im, inner_cos, precision=dft_mode) - jnp.dot(
        turned_re, inner_sin, precision=dft_mode
    )
    return (out_re.reshape(-1, outer, inner), out_im.reshape(-1, outer, inner))


def signal_back(spec_re, spec_im, plan):
    outer_cos, outer_sin, twist_cos, twist_sin, inner_cos, inner_sin, outer, inner = plan
    half = outer // 2
    flat_re = spec_re.reshape(-1, inner)
    flat_im = spec_im.reshape(-1, inner)
    mid_re = (
        jnp.dot(flat_re, inner_cos, precision=dft_mode)
        - jnp.dot(flat_im, inner_sin, precision=dft_mode)
    ).reshape(-1, outer, inner)
    mid_im = (
        jnp.dot(flat_im, inner_cos, precision=dft_mode)
        + jnp.dot(flat_re, inner_sin, precision=dft_mode)
    ).reshape(-1, outer, inner)
    turned_re = mid_re * twist_cos - mid_im * twist_sin
    turned_im = mid_im * twist_cos + mid_re * twist_sin
    grid = jnp.einsum("nk,bkq->bnq", outer_cos[:half], turned_re, precision=dft_mode) - jnp.einsum(
        "nk,bkq->bnq", outer_sin[:half], turned_im, precision=dft_mode
    )
    return grid.reshape(-1, half * inner) / (outer * inner)


def short_forward(signal, taps):
    zeros = jnp.zeros(signal.shape[:-1] + (2,), jnp.float32)
    padded = jnp.concatenate([zeros, signal], axis=-1)
    length = signal.shape[-1]
    return (
        taps[..., 0:1] * signal
        + taps[..., 1:2] * padded[..., 1 : 1 + length]
        + taps[..., 2:3] * padded[..., 0:length]
    )


def short_backward(grads, taps):
    zeros = jnp.zeros(grads.shape[:-1] + (2,), jnp.float32)
    padded = jnp.concatenate([grads, zeros], axis=-1)
    length = grads.shape[-1]
    return (
        taps[..., 0:1] * grads
        + taps[..., 1:2] * padded[..., 1 : 1 + length]
        + taps[..., 2:3] * padded[..., 2 : 2 + length]
    )


def short_taps_grad(grads, signal):
    zeros = jnp.zeros(signal.shape[:-1] + (2,), jnp.float32)
    padded = jnp.concatenate([zeros, signal], axis=-1)
    length = signal.shape[-1]
    return jnp.stack(
        [
            jnp.sum(grads * signal, axis=-1),
            jnp.sum(grads * padded[..., 1 : 1 + length], axis=-1),
            jnp.sum(grads * padded[..., 0:length], axis=-1),
        ],
        axis=-1,
    )


def channel_work(product, gated_part, filters, skip_gain, plan):
    groups_here, filt_here, length = product.shape
    outer, inner = (plan[6], plan[7])
    value_sig = product.astype(jnp.float32)
    grad_sig = gated_part.astype(jnp.float32)
    filt_re, filt_im = spectrum(filters, plan)
    val_re, val_im = spectrum(value_sig.reshape(-1, length), plan)
    grd_re, grd_im = spectrum(grad_sig.reshape(-1, length), plan)
    shape_four = (groups_here, filt_here, outer, inner)
    val_re = val_re.reshape(shape_four)
    val_im = val_im.reshape(shape_four)
    grd_re = grd_re.reshape(shape_four)
    grd_im = grd_im.reshape(shape_four)
    conv_re = filt_re * val_re - filt_im * val_im
    conv_im = filt_re * val_im + filt_im * val_re
    corr_re = filt_re * grd_re + filt_im * grd_im
    corr_im = filt_re * grd_im - filt_im * grd_re
    skip_col = skip_gain[..., None]
    conv_back = signal_back(conv_re, conv_im, plan).reshape(groups_here, filt_here, length)
    corr_back = signal_back(corr_re, corr_im, plan).reshape(groups_here, filt_here, length)
    conv_full = lax.optimization_barrier((conv_back + skip_col * value_sig).astype(jnp.bfloat16))
    value_grad = lax.optimization_barrier((corr_back + skip_col * grad_sig).astype(jnp.bfloat16))
    lag_re = jnp.sum(grd_re * val_re + grd_im * val_im, axis=0)
    lag_im = jnp.sum(grd_im * val_re - grd_re * val_im, axis=0)
    skip_grad = jnp.sum(grad_sig * value_sig, axis=-1)
    return (conv_full, value_grad, lag_re, lag_im, skip_grad)


def per_device(features, short_taps, skip_gain, filters, cotangent):
    shards = lax.axis_size("ctx")
    tok_here = features.shape[3]
    filt_here = features.shape[2] // shards
    length = tok_here * shards
    plan = make_plan(length)
    cot_full = cotangent.astype(jnp.float32)
    taps_local = lax.dynamic_slice_in_dim(
        short_taps, lax.axis_index("ctx") * filt_here, filt_here, 2
    )
    front = features[0:1]
    front_taps = short_taps[0:1]
    before = shifted(front[..., tok_here - 2 :], "ctx", 1)
    front_ext = jnp.concatenate([before, front], axis=-1).astype(jnp.float32)
    front_mixed = (
        front_taps[..., 0:1] * front_ext[..., 2:]
        + front_taps[..., 1:2] * front_ext[..., 1 : tok_here + 1]
        + front_taps[..., 2:3] * front_ext[..., 0:tok_here]
    )
    gated = lax.optimization_barrier((cot_full * front_mixed[0]).astype(jnp.bfloat16))
    key_part, value_part, gated_part = (
        lax.all_to_all(features[1], "ctx", split_axis=1, concat_axis=2, tiled=True),
        lax.all_to_all(features[2], "ctx", split_axis=1, concat_axis=2, tiled=True),
        lax.all_to_all(gated, "ctx", split_axis=1, concat_axis=2, tiled=True),
    )
    key_sig = key_part.astype(jnp.float32)
    value_sig = value_part.astype(jnp.float32)
    key_mixed = short_forward(key_sig, taps_local[1])
    value_mixed = short_forward(value_sig, taps_local[2])
    product = lax.optimization_barrier((key_mixed * value_mixed).astype(jnp.bfloat16))
    conv_full, value_grad, lag_re, lag_im, skip_grad = channel_work(
        product, gated_part, filters, skip_gain, plan
    )
    grad_wide = value_grad.astype(jnp.float32)
    key_grad = grad_wide * value_mixed
    value_grad_ch = grad_wide * key_mixed
    taps_kv = jnp.stack(
        [short_taps_grad(key_grad, key_sig), short_taps_grad(value_grad_ch, value_sig)]
    )
    key_back = short_backward(key_grad, taps_local[1]).astype(jnp.bfloat16)
    value_back = short_backward(value_grad_ch, taps_local[2]).astype(jnp.bfloat16)
    conv_seq, key_seq, value_seq = (
        lax.all_to_all(conv_full, "ctx", split_axis=2, concat_axis=1, tiled=True),
        lax.all_to_all(key_back, "ctx", split_axis=2, concat_axis=1, tiled=True),
        lax.all_to_all(value_back, "ctx", split_axis=2, concat_axis=1, tiled=True),
    )
    grads = (cot_full * conv_seq.astype(jnp.float32))[None]
    after = shifted(grads[..., 0:2], "ctx", -1)
    grad_ext = jnp.concatenate([grads, after], axis=-1)
    front_back = (
        front_taps[..., 0:1] * grads
        + front_taps[..., 1:2] * grad_ext[..., 1 : tok_here + 1]
        + front_taps[..., 2:3] * grad_ext[..., 2 : tok_here + 2]
    )
    tap_terms = jnp.stack(
        [
            jnp.sum(grads * front_ext[..., 2:], axis=-1),
            jnp.sum(grads * front_ext[..., 1 : tok_here + 1], axis=-1),
            jnp.sum(grads * front_ext[..., 0:tok_here], axis=-1),
        ],
        axis=-1,
    )
    tap_rows = tap_terms[0].reshape(-1, shards, filt_here, 3).transpose(1, 3, 0, 2)
    tap_rows = tap_rows.reshape(shards, -1)
    tap_rows = lax.all_to_all(tap_rows, "ctx", split_axis=0, concat_axis=0, tiled=True)
    tap_share = jnp.sum(tap_rows, axis=0).reshape(3, -1, filt_here).transpose(1, 2, 0)[None]
    d_short = jnp.concatenate([tap_share, taps_kv], axis=0)
    d_features = jnp.stack([front_back[0].astype(jnp.bfloat16), key_seq, value_seq])
    lag_terms = signal_back(lag_re, lag_im, plan)
    d_filter = lax.psum_scatter(
        lag_terms.astype(jnp.bfloat16), "rep", scatter_dimension=1, tiled=True
    ).astype(jnp.float32)
    return (d_features, d_short, skip_grad, d_filter)


def solution(mesh):
    placed = (
        P(None, "rep", None, "ctx"),
        P(None, "rep", None, None),
        P("rep", "ctx"),
        P("ctx", None),
        P("rep", None, "ctx"),
    )
    return jax.shard_map(
        per_device,
        mesh=mesh,
        in_specs=placed,
        out_specs=(
            P(None, "rep", None, "ctx"),
            P(None, "rep", "ctx", None),
            P("rep", "ctx"),
            P("ctx", "rep"),
        ),
        check_vma=False,
    )
```

```python
import functools

import jax
import jax.numpy as jnp
from jax import lax
from jax.experimental import pallas as pl
from jax.experimental.pallas import tpu as pltpu
from jax.sharding import PartitionSpec as P

MESH = pl.DeviceIdType.MESH
F32 = jnp.float32
BF16 = jnp.bfloat16

SHARDS = 64
REPS = 4
LANES = 128
CHUNKS = 2
QUAD = 4
GROUP = 8
LAGS = 64


def lane_ids():
    return lax.broadcasted_iota(jnp.int32, (8, LANES), 1)


def row_ids():
    return lax.broadcasted_iota(jnp.int32, (8, LANES), 0)


def swap_halves(first, second):
    upper = row_ids() < QUAD
    return (
        jnp.where(upper, first, pltpu.roll(second, QUAD, 0)),
        jnp.where(upper, pltpu.roll(first, QUAD, 0), second),
    )


def flip_matrix():
    rows = lax.broadcasted_iota(jnp.int32, (LANES, LANES), 0)
    cols = lax.broadcasted_iota(jnp.int32, (LANES, LANES), 1)
    return jnp.where(rows + cols == LANES - 1, 1.0, 0.0).astype(BF16)


def column(tile, lane):
    return jnp.broadcast_to(tile[:, lane : lane + 1], (8, LANES))


def kernel(
    feat, cot, taps, skip, filt,
    d_feat, d_short, d_skip, d_filt,
    sig, mixed, wts, tcol, strip, base, front, front_in,
    send_in, recv_in, send_out, recv_out,
    spread, prod_nat, grad_nat, xs, conv, merged,
    shifted, prod_t, cross, low, high, lagrow, lag_send, lag_recv,
    grads, back, back_in, tap_send, tap_recv,
    front_sem, in_sem, out_sem, back_sem, tap_sem, lag_sem,
):
    me = lax.axis_index("ctx")
    rep = lax.axis_index("rep")
    lane = lane_ids()

    barrier = pltpu.get_barrier_semaphore()

    def greet(k, _):
        pl.semaphore_signal(
            barrier, inc=1, device_id=(lax.rem(me + k, SHARDS), rep), device_id_type=MESH
        )
        return 0

    lax.fori_loop(1, SHARDS, greet, 0)
    for k in range(1, REPS):
        pl.semaphore_signal(
            barrier, inc=1, device_id=(me, lax.rem(rep + k, REPS)), device_id_type=MESH
        )

    def arrange(step, packed):
        packed = list(packed)
        for half in range(4):
            pair = step * 4 + half
            rows = pl.ds(pl.multiple_of(pair * 16, 16), 16)
            for j in range(4):
                wide = []
                for g in range(4):
                    block = feat[j, g, rows, :] if j < 3 else cot[g, rows, :]
                    wide.append(block.astype(F32))
                for u in range(2):
                    shard = pair * 2 + u
                    for gp in range(2):
                        tiles = swap_halves(
                            wide[2 * gp][8 * u : 8 * u + 8], wide[2 * gp + 1][8 * u : 8 * u + 8]
                        )
                        for c in range(CHUNKS):
                            sig[j, c, shard, 8 * gp : 8 * gp + 8, :] = tiles[c]
                            if j < 3:
                                at = (c * 3 + j) * 2 + gp
                                moved = pltpu.roll(tiles[c], lax.rem(2 * shard + 2, LANES), 1)
                                packed[at] = jnp.where(lane // 2 == shard, moved, packed[at])
        return tuple(packed)

    zero = jnp.zeros((8, LANES), F32)
    packed = lax.fori_loop(0, SHARDS // 8, arrange, (zero,) * 12)
    for at in range(12):
        front[8 * at : 8 * at + 8, :] = packed[at]

    @pl.when(me == 0)
    def _():
        front_in[...] = jnp.zeros(front_in.shape, F32)

    @pl.when(me == SHARDS - 1)
    def _():
        back_in[...] = jnp.zeros(back_in.shape, F32)

    pl.semaphore_wait(barrier, SHARDS - 1 + REPS - 1)

    def front_copy():
        return pltpu.make_async_remote_copy(
            src_ref=front, dst_ref=front_in, send_sem=front_sem.at[0], recv_sem=front_sem.at[1],
            device_id=(lax.rem(me + 1, SHARDS), rep), device_id_type=MESH,
        )

    @pl.when(me < SHARDS - 1)
    def _():
        front_copy().start()

    for part in range(4):
        cols = slice(part * LANES, (part + 1) * LANES)
        tcol[cols, :] = jnp.concatenate(
            [taps[:, cols], jnp.zeros((LANES - 40, LANES), F32)], axis=0
        ).T

    def arrange_taps(step, _):
        for u in range(8):
            shard = step * 8 + u
            tile = tcol[pl.ds(pl.multiple_of(shard * 8, 8), 8), :]
            for gp in range(2):
                first = tile if gp == 0 else pltpu.roll(tile, LANES - 18 * gp, 1)
                second = pltpu.roll(tile, LANES - 18 * gp - 9, 1)
                both = swap_halves(first, second)
                for c in range(CHUNKS):
                    wts[c, shard, 8 * gp : 8 * gp + 8, :] = both[c]
        return 0

    lax.fori_loop(0, SHARDS // 8, arrange_taps, 0)

    for q in range(QUAD):
        for u in range(2):
            xs[q, u, 0:256, :] = jnp.zeros((256, 256), BF16)
        for e in range(2):
            for k in range(4):
                shifted[q, e, k, 128:256, :] = jnp.zeros((128, LANES), BF16)
        high[q, LAGS] = zero
    for e in range(2):
        grad_nat[e, 512:576, :] = jnp.zeros((64, LANES), F32)

    @pl.when(me > 0)
    def _():
        front_copy().wait_recv()

    @pl.when(me < SHARDS - 1)
    def _():
        front_copy().wait_send()

    def block_copy(src, dst, sems, c, peer):
        return pltpu.make_async_remote_copy(
            src_ref=src.at[c, peer], dst_ref=dst.at[c, me], send_sem=sems.at[0, c],
            recv_sem=sems.at[1, c], device_id=(peer, rep), device_id_type=MESH,
        )

    def all_copies(src, dst, sems, c):
        others = pl.ds(0, SHARDS - 1)
        return pltpu.make_async_remote_copy(
            src_ref=src.at[c, others], dst_ref=dst.at[c, others], send_sem=sems.at[0, c],
            recv_sem=sems.at[1, c], device_id=(lax.rem(me + 1, SHARDS), rep), device_id_type=MESH,
        )

    def send_all(src, dst, sems, c):
        def one(k, _):
            block_copy(src, dst, sems, c, lax.rem(me + k, SHARDS)).start()
            return 0

        lax.fori_loop(1, SHARDS, one, 0)
        dst[c, me] = src[c, me]

    def short_conv(c, step, _):
        for u in range(GROUP):
            shard = lax.rem(me + step * GROUP + u, SHARDS)
            made = []
            for gp in range(2):
                rows = slice(8 * gp, 8 * gp + 8)
                weight = wts[c, shard, rows, :]
                mix = []
                for j in range(3):
                    here = sig[j, c, shard, rows, :]
                    at = (c * 3 + j) * 2 + gp
                    before = pltpu.roll(front_in[8 * at : 8 * at + 8, :], 126 - 2 * shard, 1)
                    one = pltpu.roll(jnp.where(lane == 127, before, here), 1, 1)
                    two = pltpu.roll(jnp.where(lane >= 126, before, here), 2, 1)
                    mix.append(
                        column(weight, 3 * j) * here
                        + column(weight, 3 * j + 1) * one
                        + column(weight, 3 * j + 2) * two
                    )
                mixed[0, c, shard, rows, :] = mix[1]
                mixed[1, c, shard, rows, :] = mix[2]
                made.append((mix[1] * mix[2], sig[3, c, shard, rows, :] * mix[0]))
            for a in range(2):
                send_in[c, shard, 16 * a : 16 * a + 16, :] = jnp.concatenate(
                    [made[0][a], made[1][a]], axis=0
                ).astype(BF16)
        for u in range(GROUP):
            shard = lax.rem(me + step * GROUP + u, SHARDS)

            @pl.when(shard != me)
            def _():
                block_copy(send_in, recv_in, in_sem, c, shard).start()

        return 0

    for c in range(CHUNKS):
        lax.fori_loop(0, SHARDS // GROUP, functools.partial(short_conv, c), 0)
        recv_in[c, me] = send_in[c, me]

    strip[:, :, 0:LANES] = jnp.zeros((8, LANES, LANES), BF16)
    base[:, 0:LANES] = zero

    def make_strip(f, _):
        row = filt[pl.ds(f, 1), :]
        for part in range(8):
            cols = slice(LANES + part * 1024, LANES + part * 1024 + 1024)
            base[:, cols] = jnp.broadcast_to(row[:, part * 1024 : part * 1024 + 1024], (8, 1024))
        for part in reversed(range(8)):
            wide = base[:, part * 1024 : part * 1024 + 1152]
            base[:, LANES + part * 1024 : LANES + part * 1024 + 1024] = pltpu.roll(
                wide, 0, 1, stride=1, stride_axis=0
            )[:, LANES:]
        for part in range(8):
            wide = base[:, part * 1024 : part * 1024 + 1152]
            for k in range(8):
                upper = wide if k == 0 else pltpu.roll(wide, 16 * k, 1)
                lower = pltpu.roll(wide, 16 * k + 8, 1)
                strip[f, 16 * k : 16 * k + 16, LANES + part * 1024 : LANES + part * 1024 + 1024] = (
                    jnp.concatenate([upper[:, LANES:], lower[:, LANES:]], axis=0).astype(BF16)
                )
        return 0

    lax.fori_loop(0, 8, make_strip, 0)

    flip = flip_matrix()
    sign_row = lax.broadcasted_iota(jnp.int32, (8, 256), 0) % 4

    def unpack(c, step, total):
        back_rows = jnp.concatenate(
            [recv_in[c, step * 8 + u, 16:32, :] for u in range(8)], axis=0
        )
        turned = jnp.dot(back_rows, flip, preferred_element_type=F32)
        for u in range(8):
            shard = step * 8 + u
            place = step * 4 + u // 2
            e = u % 2
            product = recv_in[c, shard, 0:16, :].astype(F32)
            gated = recv_in[c, shard, 16:32, :].astype(F32)
            total = total + product * gated
            spread[e, pl.ds(pl.multiple_of(place * 32, 32), 16), :] = product
            prod_nat[e, pl.ds(pl.multiple_of(place * 16, 16), 16), :] = product
            reverse = turned[16 * u : 16 * u + 16]
            mirror = 31 - place
            spread[1 - e, pl.ds(pl.multiple_of(mirror * 32 + 16, 16), 16), :] = reverse
            grad_nat[e, pl.ds(pl.multiple_of(place * 16, 16), 16), :] = reverse
        return total

    def long_conv(c, q, _):
        f = QUAD * c + q
        for group in range(4):
            skip_rows = 64 * group
            acc = jnp.zeros((256 - skip_rows, 256), F32)
            for lag in range(8 * group, 8 * group + 8):
                even = lag - lag % 2
                lhs = xs[q, lag % 2, 256 + skip_rows - 8 * even : 512 - 8 * even, :]
                at = LANES + 256 * lag
                rhs = jnp.concatenate(
                    [strip[f, :, at : at + 256], strip[f, :, at - LANES : at + LANES]], axis=0
                )
                acc = acc + jnp.dot(lhs, rhs, preferred_element_type=F32)
            if group == 0:
                conv[q] = acc
            else:
                conv[q, skip_rows:256, :] += acc
        gain = jnp.where(
            sign_row == 0,
            skip[0, f],
            jnp.where(sign_row == 1, skip[1, f], jnp.where(sign_row == 2, skip[2, f], skip[3, f])),
        )
        for part in range(4):
            rows = slice(64 * part, 64 * part + 64)
            own = xs[q, 0, 256 + 64 * part : 320 + 64 * part, :].astype(F32)
            conv[q, rows, :] += own * jnp.concatenate([gain] * 8, axis=0)
        return 0

    def pack(c, step, _):
        turned = jnp.concatenate(
            [
                merged[u % 2, pl.ds(pl.multiple_of((step * 4 + u // 2) * 32 + 16, 16), 16), :]
                for u in range(8)
            ],
            axis=0,
        ).astype(BF16)
        turned = jnp.dot(turned, flip, preferred_element_type=F32).astype(BF16)
        for u in range(8):
            shard = step * 8 + u
            place = step * 4 + u // 2
            send_out[c, shard, 0:16, :] = merged[
                u % 2, pl.ds(pl.multiple_of(place * 32, 32), 16), :
            ].astype(BF16)
            send_out[c, SHARDS - 1 - shard, 16:32, :] = turned[16 * u : 16 * u + 16]
        return 0

    def owner_conv(c):
        all_copies(send_in, recv_in, in_sem, c).wait_recv()
        total = lax.fori_loop(0, 8, functools.partial(unpack, c), jnp.zeros((16, LANES), F32))
        d_skip[16 * c : 16 * c + 16, :] = jnp.broadcast_to(
            jnp.sum(total, axis=1, keepdims=True), (16, LANES)
        )
        for q in range(QUAD):
            tile = jnp.concatenate(
                [spread[e, pl.ds(q, 256, stride=4), :] for e in range(2)], axis=1
            )
            xs[q, 0, 256:512, :] = tile.astype(BF16)
            xs[q, 1, 256:512, :] = jnp.concatenate(
                [jnp.zeros((8, 256), F32), tile[0:248]], axis=0
            ).astype(BF16)
        lax.fori_loop(0, QUAD, functools.partial(long_conv, c), 0)
        for q in range(QUAD):
            for e in range(2):
                merged[e, pl.ds(q, 256, stride=4), :] = conv[q, :, LANES * e : LANES * e + LANES]
        lax.fori_loop(0, 8, functools.partial(pack, c), 0)
        send_all(send_out, recv_out, out_sem, c)

    def cross_dots(q, m, slot):
        for pair in range(4):
            sides = []
            for odd in range(2):
                lag = 2 * pair + odd
                half = pair
                parts = []
                for e in range(2):
                    carry = half + (1 if e == 1 and odd == 1 else 0)
                    at = pl.multiple_of(16 * m + 16 * (carry // 4), 16)
                    parts.append(shifted[q, (e + odd) % 2, carry % 4, pl.ds(at, 128), :])
                sides.append(jnp.concatenate(parts, axis=0))
            cross[slot, pair] = jnp.dot(
                prod_t[q], jnp.concatenate(sides, axis=1), preferred_element_type=F32
            )

    def diagonals(q, m, slot):
        for lag in range(8):
            cols = slice((lag % 2) * LANES, (lag % 2) * LANES + LANES)
            total = cross[slot, lag // 2, 0:8, cols]
            kept = total
            for k in range(1, 16):
                moved = pltpu.roll(cross[slot, lag // 2, 8 * k : 8 * k + 8, cols], 8 * k, 1)
                total = total + moved
                kept = kept + jnp.where(lane >= 8 * k, moved, 0.0)
            low[q, 8 * m + lag] = kept
            high[q, 8 * m + lag] = total - kept

    def owner_lags(c):
        for q in range(QUAD):
            for e in range(2):
                prod_t[q, :, LANES * e : LANES * e + LANES] = (
                    prod_nat[e, pl.ds(q, 128, stride=4), :].T.astype(BF16)
                )
                for k in range(4):
                    shifted[q, e, k, 0:128, :] = grad_nat[
                        e, pl.ds(q + 16 * k, 128, stride=4), :
                    ].astype(BF16)
        cross_dots(0, 0, 0)

        def two(step, _):
            q = step // 4
            m = 2 * (step % 4)
            cross_dots(q, m + 1, 1)
            diagonals(q, m, 0)
            later = jnp.minimum(step + 1, 15)
            cross_dots(later // 4, 2 * (later % 4), 0)
            diagonals(q, m + 1, 1)
            return 0

        lax.fori_loop(0, 16, two, 0)

        def turn(step, _):
            q = step // 4
            first = 16 * (step % 4)
            rolled = []
            for k in range(17):
                at = jnp.minimum(first + k, LAGS - 1)
                tile = low[q, at] + high[q, at + 1]
                rolled.append(pltpu.roll(tile, 0, 1, stride=1, stride_axis=0))
            rolled[16] = jnp.where(first == 48, 0.0, rolled[16])
            rows = [
                jnp.sum(jnp.where(lane >= row_ids(), rolled[k], rolled[k + 1]), axis=0, keepdims=True)
                for k in range(16)
            ]
            lagrow[q, step % 4] = jnp.concatenate(rows, axis=0)
            return 0

        lax.fori_loop(0, 16, turn, 0)
        for q in range(QUAD):
            turned = jnp.dot(
                jnp.concatenate([lagrow[q, r] for r in range(4)], axis=0).astype(BF16),
                flip,
                preferred_element_type=F32,
            ).astype(BF16)
            for r in range(REPS):
                lag_send[r, QUAD * c + q] = turned[16 * r : 16 * r + 16]

    owner_conv(0)
    owner_lags(0)
    owner_conv(1)
    owner_lags(1)

    def lag_copy(peer):
        return pltpu.make_async_remote_copy(
            src_ref=lag_send.at[peer], dst_ref=lag_recv.at[rep], send_sem=lag_sem.at[0],
            recv_sem=lag_sem.at[1], device_id=(me, peer), device_id_type=MESH,
        )

    for k in range(1, REPS):
        lag_copy(lax.rem(rep + k, REPS)).start()
    lag_recv[rep] = lag_send[rep]

    def make_grads(c, step, packed):
        packed = list(packed)
        for u in range(GROUP):
            shard = step * GROUP + u
            conv_rows = recv_out[c, shard, 0:16, :].astype(F32)
            grad_rows = recv_out[c, shard, 16:32, :].astype(F32)
            for gp in range(2):
                rows = slice(8 * gp, 8 * gp + 8)
                value = grad_rows[rows]
                three = (
                    sig[3, c, shard, rows, :] * conv_rows[rows],
                    value * mixed[1, c, shard, rows, :],
                    value * mixed[0, c, shard, rows, :],
                )
                for j in range(3):
                    grads[c, j, shard, rows, :] = three[j]
                    moved = pltpu.roll(three[j], 2 * shard, 1)
                    packed[2 * j + gp] = jnp.where(lane // 2 == shard, moved, packed[2 * j + gp])
        return tuple(packed)

    def back_copy(c):
        return pltpu.make_async_remote_copy(
            src_ref=back.at[c], dst_ref=back_in.at[c], send_sem=back_sem.at[0, c],
            recv_sem=back_sem.at[1, c],
            device_id=(lax.rem(me + SHARDS - 1, SHARDS), rep), device_id_type=MESH,
        )

    def post_first(c):
        all_copies(send_out, recv_out, out_sem, c).wait_recv()
        packed = lax.fori_loop(
            0, SHARDS // GROUP, functools.partial(make_grads, c), (zero,) * 6
        )
        for at in range(6):
            back[c, 8 * at : 8 * at + 8, :] = packed[at]

        @pl.when(me > 0)
        def _():
            back_copy(c).start()

    def short_back(c, step, _):
        for u in range(GROUP):
            shard = step * GROUP + u
            sums = tap_send[shard] if c == 1 else zero
            for gp in range(2):
                rows = slice(8 * gp, 8 * gp + 8)
                weight = wts[c, shard, rows, :]
                for j in range(3):
                    here = grads[c, j, shard, rows, :]
                    at = 2 * j + gp
                    after = pltpu.roll(
                        back_in[c, 8 * at : 8 * at + 8, :], lax.rem(LANES - 2 * shard, LANES), 1
                    )
                    one = pltpu.roll(jnp.where(lane == 0, after, here), LANES - 1, 1)
                    two = pltpu.roll(jnp.where(lane < 2, after, here), LANES - 2, 1)
                    grads[c, j, shard, rows, :] = (
                        column(weight, 3 * j) * here
                        + column(weight, 3 * j + 1) * one
                        + column(weight, 3 * j + 2) * two
                    )
                    signal = sig[j, c, shard, rows, :]
                    for i, moved in enumerate((here, one, two)):
                        share = jnp.sum(moved * signal, axis=1, keepdims=True)
                        sums = jnp.where(lane == c * 18 + gp * 9 + 3 * j + i, share, sums)
            tap_send[shard] = sums
        return 0

    def post_second(c):
        @pl.when(me < SHARDS - 1)
        def _():
            back_copy(c).wait_recv()

        lax.fori_loop(0, SHARDS // GROUP, functools.partial(short_back, c), 0)

    post_first(0)
    post_first(1)
    post_second(0)
    post_second(1)

    def tap_copy(peer):
        return pltpu.make_async_remote_copy(
            src_ref=tap_send.at[peer], dst_ref=tap_recv.at[me], send_sem=tap_sem.at[0],
            recv_sem=tap_sem.at[1], device_id=(peer, rep), device_id_type=MESH,
        )

    def send_taps(k, _):
        tap_copy(lax.rem(me + k, SHARDS)).start()
        return 0

    lax.fori_loop(1, SHARDS, send_taps, 0)
    tap_recv[me] = tap_send[me]

    def put_back(step, _):
        for half in range(4):
            pair = step * 4 + half
            rows = pl.ds(pl.multiple_of(pair * 16, 16), 16)
            for j in range(3):
                for gp in range(2):
                    tiles = [
                        swap_halves(
                            grads[0, j, pair * 2 + u, 8 * gp : 8 * gp + 8, :],
                            grads[1, j, pair * 2 + u, 8 * gp : 8 * gp + 8, :],
                        )
                        for u in range(2)
                    ]
                    for g in range(2):
                        d_feat[j, 2 * gp + g, rows, :] = jnp.concatenate(
                            [tiles[0][g], tiles[1][g]], axis=0
                        ).astype(BF16)
        return 0

    lax.fori_loop(0, SHARDS // 8, put_back, 0)

    lag_all = pltpu.make_async_remote_copy(
        src_ref=lag_send.at[pl.ds(0, REPS - 1)], dst_ref=lag_recv.at[pl.ds(0, REPS - 1)],
        send_sem=lag_sem.at[0], recv_sem=lag_sem.at[1],
        device_id=(me, lax.rem(rep + 1, REPS)), device_id_type=MESH,
    )
    lag_all.wait_recv()
    for f in range(8):
        d_filt[f] = (
            lag_recv[0, f].astype(F32)
            + lag_recv[1, f].astype(F32)
            + lag_recv[2, f].astype(F32)
            + lag_recv[3, f].astype(F32)
        )

    tap_all = pltpu.make_async_remote_copy(
        src_ref=tap_send.at[pl.ds(0, SHARDS - 1)], dst_ref=tap_recv.at[pl.ds(0, SHARDS - 1)],
        send_sem=tap_sem.at[0], recv_sem=tap_sem.at[1],
        device_id=(lax.rem(me + 1, SHARDS), rep), device_id_type=MESH,
    )
    tap_all.wait_recv()
    d_short[...] = jnp.sum(tap_recv[...], axis=0)

    for c in range(CHUNKS):
        all_copies(send_in, recv_in, in_sem, c).wait_send()
        all_copies(send_out, recv_out, out_sem, c).wait_send()

        @pl.when(me > 0)
        def _():
            back_copy(c).wait_send()

    lag_all.wait_send()
    tap_all.wait_send()


def per_device(features, short_taps, skip_gain, filters, cotangent):
    tap_rows = jnp.transpose(short_taps, (1, 0, 3, 2)).reshape(36, 512)
    tap_rows = jnp.pad(tap_rows, ((0, 4), (0, 0)))
    vmem = pl.BlockSpec(memory_space=pltpu.VMEM)
    message = pltpu.VMEM((CHUNKS, SHARDS, 32, LANES), BF16)
    d_feat, d_short, d_skip, d_filt = pl.pallas_call(
        kernel,
        out_shape=(
            jax.ShapeDtypeStruct((3, 4, 512, LANES), BF16),
            jax.ShapeDtypeStruct((8, LANES), F32),
            jax.ShapeDtypeStruct((32, LANES), F32),
            jax.ShapeDtypeStruct((8, 16, LANES), F32),
        ),
        in_specs=[vmem, vmem, vmem, pl.BlockSpec(memory_space=pltpu.SMEM), vmem],
        out_specs=(vmem,) * 4,
        scratch_shapes=[
            pltpu.VMEM((4, CHUNKS, SHARDS, 16, LANES), F32),
            pltpu.VMEM((2, CHUNKS, SHARDS, 16, LANES), F32),
            pltpu.VMEM((CHUNKS, SHARDS, 16, LANES), F32),
            pltpu.VMEM((512, LANES), F32),
            pltpu.VMEM((8, LANES, LANES + 8192), BF16),
            pltpu.VMEM((8, LANES + 8192), F32),
            pltpu.VMEM((96, LANES), F32),
            pltpu.VMEM((96, LANES), F32),
            message, message, message, message,
            pltpu.VMEM((2, 1024, LANES), F32),
            pltpu.VMEM((2, 512, LANES), F32),
            pltpu.VMEM((2, 576, LANES), F32),
            pltpu.VMEM((QUAD, 2, 512, 256), BF16),
            pltpu.VMEM((QUAD, 256, 256), F32),
            pltpu.VMEM((2, 1024, LANES), F32),
            pltpu.VMEM((QUAD, 2, 4, 256, LANES), BF16),
            pltpu.VMEM((QUAD, LANES, 256), BF16),
            pltpu.VMEM((2, 4, LANES, 256), F32),
            pltpu.VMEM((QUAD, LAGS, 8, LANES), F32),
            pltpu.VMEM((QUAD, LAGS + 1, 8, LANES), F32),
            pltpu.VMEM((QUAD, 4, 16, LANES), F32),
            pltpu.VMEM((REPS, 8, 16, LANES), BF16),
            pltpu.VMEM((REPS, 8, 16, LANES), BF16),
            pltpu.VMEM((CHUNKS, 3, SHARDS, 16, LANES), F32),
            pltpu.VMEM((CHUNKS, 48, LANES), F32),
            pltpu.VMEM((CHUNKS, 48, LANES), F32),
            pltpu.VMEM((SHARDS, 8, LANES), F32),
            pltpu.VMEM((SHARDS, 8, LANES), F32),
            pltpu.SemaphoreType.DMA((2,)),
            pltpu.SemaphoreType.DMA((2, CHUNKS)),
            pltpu.SemaphoreType.DMA((2, CHUNKS)),
            pltpu.SemaphoreType.DMA((2, CHUNKS)),
            pltpu.SemaphoreType.DMA((2,)),
            pltpu.SemaphoreType.DMA((2,)),
        ],
        compiler_params=pltpu.CompilerParams(
            collective_id=0, has_side_effects=True, vmem_limit_bytes=60 * 2**20
        ),
    )(features, cotangent, tap_rows, skip_gain, filters)
    short = d_short[:, :36].reshape(2, 4, 2, 2, 3, 3)
    short = jnp.transpose(short, (4, 3, 0, 2, 1, 5)).reshape(3, 4, 8, 3)
    skips = jnp.transpose(d_skip[:, 0].reshape(2, 4, 4), (1, 0, 2)).reshape(4, 8)
    return (d_feat, short, skips, d_filt.reshape(8, 2048))


def solution(mesh):
    placed = (
        P(None, "rep", None, "ctx"),
        P(None, "rep", None, None),
        P("rep", "ctx"),
        P("ctx", None),
        P("rep", None, "ctx"),
    )
    return jax.shard_map(
        per_device,
        mesh=mesh,
        in_specs=placed,
        out_specs=(
            P(None, "rep", None, "ctx"),
            P(None, "rep", "ctx", None),
            P("rep", "ctx"),
            P("ctx", "rep"),
        ),
        check_vma=False,
    )
```

```python
import functools

import jax
import jax.numpy as jnp
from jax import lax
from jax.experimental import pallas as pl
from jax.experimental.pallas import tpu as pltpu
from jax.sharding import PartitionSpec as P

MESH = pl.DeviceIdType.MESH
F32 = jnp.float32
BF16 = jnp.bfloat16

SHARDS = 64
REPS = 4
LANES = 128
CHUNKS = 2
QUAD = 4
GROUP = 8
LAGS = 64


def lane_ids():
    return lax.broadcasted_iota(jnp.int32, (8, LANES), 1)


def row_ids():
    return lax.broadcasted_iota(jnp.int32, (8, LANES), 0)


def swap_halves(first, second):
    upper = row_ids() < QUAD
    return (
        jnp.where(upper, first, pltpu.roll(second, QUAD, 0)),
        jnp.where(upper, pltpu.roll(first, QUAD, 0), second),
    )


def flip_matrix():
    rows = lax.broadcasted_iota(jnp.int32, (LANES, LANES), 0)
    cols = lax.broadcasted_iota(jnp.int32, (LANES, LANES), 1)
    return jnp.where(rows + cols == LANES - 1, 1.0, 0.0).astype(BF16)


def ids(rows, cols):
    shape = (rows, cols)
    return (
        lax.broadcasted_iota(jnp.int32, shape, 0),
        lax.broadcasted_iota(jnp.int32, shape, 1),
    )


def ones_where(condition):
    return jnp.where(condition, 1.0, 0.0).astype(BF16)


def halves(wide):
    high = wide.astype(BF16)
    return jnp.concatenate([high, (wide - high.astype(F32)).astype(BF16)], axis=1)


def product_of(left, right):
    return jnp.dot(left, right, preferred_element_type=F32)


def kernel(
    feat, cot, taps, skip, filt,
    d_feat, d_short, d_skip, d_filt,
    sig, mixed, wts, tcol, strip, base, front, front_in, halo,
    m_early, m_col, m_late, m_next, m_first, m_sum,
    send_in, recv_in, send_out, recv_out,
    spread, prod_nat, grad_nat, xs, conv, merged,
    shifted, prod_t, cross, low, high, lagrow, lag_send, lag_recv,
    grads, d_rows, back, back_in, tap_send, tap_recv,
    front_sem, in_sem, out_sem, back_sem, tap_sem, lag_sem,
):
    me = lax.axis_index("ctx")
    rep = lax.axis_index("rep")
    lane = lane_ids()

    barrier = pltpu.get_barrier_semaphore()

    def greet(k, _):
        pl.semaphore_signal(
            barrier, inc=1, device_id=(lax.rem(me + k, SHARDS), rep), device_id_type=MESH
        )
        return 0

    lax.fori_loop(1, SHARDS, greet, 0)
    for k in range(1, REPS):
        pl.semaphore_signal(
            barrier, inc=1, device_id=(me, lax.rem(rep + k, REPS)), device_id_type=MESH
        )

    row, col = ids(LANES, LANES)
    m_early[0:LANES, 0:LANES] = ones_where(col == row + 1)
    m_early[0:LANES, LANES:] = ones_where(col == row + 2)
    m_early[LANES:, 0:LANES] = ones_where((col == 0) & (row % 2 == 1))
    m_early[LANES:, LANES:] = ones_where((col < 2) & (col == row % 2))
    for k in range(2):
        rows = slice(k * LANES, (k + 1) * LANES)
        m_late[rows, 0:LANES] = ones_where(col == row - 1)
        m_late[rows, LANES:] = ones_where(col == row - 2)
        m_next[rows, 0:LANES] = ones_where((col == LANES - 1) & (row % 2 == 0))
        m_next[rows, LANES:] = ones_where((col >= LANES - 2) & (col % 2 == row % 2))
        m_first[rows, :] = ones_where(row == col % 2)
    last = ones_where(row - (LANES - 2) == col % 2)
    for k in range(9):
        m_col[:, k * LANES : (k + 1) * LANES] = ones_where((row < 27) & (row % 9 == k))
        m_sum[2 * k * LANES : 2 * (k + 1) * LANES, :] = ones_where(ids(256, LANES)[1] == k)

    def arrange(step, _):
        for half in range(4):
            pair = step * 4 + half
            rows = pl.ds(pl.multiple_of(pair * 16, 16), 16)
            for j in range(4):
                wide = []
                for g in range(4):
                    block = feat[j, g, rows, :] if j < 3 else cot[g, rows, :]
                    wide.append(block.astype(F32))
                for u in range(2):
                    both = [
                        swap_halves(
                            wide[2 * gp][8 * u : 8 * u + 8], wide[2 * gp + 1][8 * u : 8 * u + 8]
                        )
                        for gp in range(2)
                    ]
                    for c in range(CHUNKS):
                        sig[j, c, pair * 2 + u] = jnp.concatenate(
                            [both[0][c], both[1][c]], axis=0
                        ).astype(BF16)
        return 0

    zero = jnp.zeros((8, LANES), F32)
    lax.fori_loop(0, SHARDS // 8, arrange, 0)

    def eight(ref, *at):
        return ref[at].reshape(8 * 16, LANES)

    def own_lanes(step):
        rows, cols = ids(8 * 16, LANES)
        return cols // 2 == step * 8 + rows // 16

    def gather(values):
        total = values[0:16]
        for u in range(1, 8):
            total = total + values[16 * u : 16 * u + 16]
        return total

    def pack_front(step, _):
        mine = own_lanes(step)
        shards = pl.ds(pl.multiple_of(step * 8, 8), 8)
        for c in range(CHUNKS):
            for j in range(3):
                spread_out = product_of(eight(sig, j, c, shards), last)
                halo[c * 3 + j] += gather(jnp.where(mine, spread_out, 0.0))
        return 0

    halo[...] = jnp.zeros(halo.shape, F32)
    lax.fori_loop(0, SHARDS // 8, pack_front, 0)
    for at in range(6):
        front[at] = halo[at].astype(BF16)

    @pl.when(me == 0)
    def _():
        front_in[...] = jnp.zeros(front_in.shape, BF16)

    @pl.when(me == SHARDS - 1)
    def _():
        back_in[...] = jnp.zeros(back_in.shape, F32)

    pl.semaphore_wait(barrier, SHARDS - 1 + REPS - 1)

    def front_copy():
        return pltpu.make_async_remote_copy(
            src_ref=front, dst_ref=front_in, send_sem=front_sem.at[0], recv_sem=front_sem.at[1],
            device_id=(lax.rem(me + 1, SHARDS), rep), device_id_type=MESH,
        )

    @pl.when(me < SHARDS - 1)
    def _():
        front_copy().start()

    for part in range(4):
        cols = slice(part * LANES, (part + 1) * LANES)
        tcol[cols, :] = jnp.concatenate(
            [taps[:, cols], jnp.zeros((LANES - 40, LANES), F32)], axis=0
        ).T

    def arrange_taps(step, _):
        for u in range(8):
            shard = step * 8 + u
            tile = tcol[pl.ds(pl.multiple_of(shard * 8, 8), 8), :]
            made = ([], [])
            for gp in range(2):
                first = tile if gp == 0 else pltpu.roll(tile, LANES - 18 * gp, 1)
                second = pltpu.roll(tile, LANES - 18 * gp - 9, 1)
                for c, weight in enumerate(swap_halves(first, second)):
                    high_part = weight.astype(BF16).astype(F32)
                    rest = weight - high_part
                    mid_part = rest.astype(BF16).astype(F32)
                    rest = rest - mid_part
                    three = jnp.where(
                        lane < 9,
                        high_part,
                        jnp.where(lane < 18, pltpu.roll(mid_part, 9, 1), pltpu.roll(rest, 18, 1)),
                    )
                    made[c].append(jnp.where(lane < 27, three, 0.0))
            for c in range(CHUNKS):
                wts[c, shard] = jnp.concatenate(made[c], axis=0).astype(BF16)
        return 0

    lax.fori_loop(0, SHARDS // 8, arrange_taps, 0)

    for q in range(QUAD):
        for u in range(2):
            xs[q, u, 0:256, :] = jnp.zeros((256, 256), BF16)
        for e in range(2):
            for k in range(4):
                shifted[q, e, k, 128:256, :] = jnp.zeros((128, LANES), BF16)
        high[q, LAGS] = zero
    for e in range(2):
        grad_nat[e, 512:576, :] = jnp.zeros((64, LANES), F32)

    @pl.when(me > 0)
    def _():
        front_copy().wait_recv()

    @pl.when(me < SHARDS - 1)
    def _():
        front_copy().wait_send()

    def block_copy(src, dst, sems, c, peer):
        return pltpu.make_async_remote_copy(
            src_ref=src.at[c, peer], dst_ref=dst.at[c, me], send_sem=sems.at[0, c],
            recv_sem=sems.at[1, c], device_id=(peer, rep), device_id_type=MESH,
        )

    def all_copies(src, dst, sems, c):
        others = pl.ds(0, SHARDS - 1)
        return pltpu.make_async_remote_copy(
            src_ref=src.at[c, others], dst_ref=dst.at[c, others], send_sem=sems.at[0, c],
            recv_sem=sems.at[1, c], device_id=(lax.rem(me + 1, SHARDS), rep), device_id_type=MESH,
        )

    def send_all(src, dst, sems, c):
        def one(k, _):
            block_copy(src, dst, sems, c, lax.rem(me + k, SHARDS)).start()
            return 0

        lax.fori_loop(1, SHARDS, one, 0)
        dst[c, me] = src[c, me]

    def short_conv(c, step, _):
        group = lax.rem(me // GROUP + step, SHARDS // GROUP)
        shards = pl.ds(pl.multiple_of(group * GROUP, GROUP), GROUP)
        mine = own_lanes(group)
        weight = product_of(eight(wts, c, shards), m_col[...])
        mix = []
        for j in range(3):
            here = eight(sig, j, c, shards)
            before = jnp.concatenate([front_in[c * 3 + j].astype(F32)] * 8, axis=0)
            before = jnp.where(mine, before, 0.0).astype(BF16)
            moved = product_of(jnp.concatenate([here, before], axis=1), m_early[...])
            three = [weight[:, (3 * j + i) * LANES : (3 * j + i + 1) * LANES] for i in range(3)]
            mix.append(
                three[0] * here.astype(F32)
                + three[1] * moved[:, 0:LANES]
                + three[2] * moved[:, LANES:]
            )
        mixed[0, c, shards] = mix[1].reshape(8, 16, LANES)
        mixed[1, c, shards] = mix[2].reshape(8, 16, LANES)
        send_in[c, shards, 0:16, :] = (mix[1] * mix[2]).astype(BF16).reshape(8, 16, LANES)
        gated = eight(sig, 3, c, shards).astype(F32) * mix[0]
        send_in[c, shards, 16:32, :] = gated.astype(BF16).reshape(8, 16, LANES)
        for u in range(GROUP):
            shard = group * GROUP + lax.rem(me + u, GROUP)

            @pl.when(shard != me)
            def _():
                block_copy(send_in, recv_in, in_sem, c, shard).start()

        return 0

    for c in range(CHUNKS):
        lax.fori_loop(0, SHARDS // GROUP, functools.partial(short_conv, c), 0)
        recv_in[c, me] = send_in[c, me]

    strip[:, :, 0:LANES] = jnp.zeros((8, LANES, LANES), BF16)
    base[:, 0:LANES] = zero

    def make_strip(f, _):
        row = filt[pl.ds(f, 1), :]
        for part in range(8):
            cols = slice(LANES + part * 1024, LANES + part * 1024 + 1024)
            base[:, cols] = jnp.broadcast_to(row[:, part * 1024 : part * 1024 + 1024], (8, 1024))
        for part in reversed(range(8)):
            wide = base[:, part * 1024 : part * 1024 + 1152]
            base[:, LANES + part * 1024 : LANES + part * 1024 + 1024] = pltpu.roll(
                wide, 0, 1, stride=1, stride_axis=0
            )[:, LANES:]
        for part in range(8):
            wide = base[:, part * 1024 : part * 1024 + 1152]
            for k in range(8):
                upper = wide if k == 0 else pltpu.roll(wide, 16 * k, 1)
                lower = pltpu.roll(wide, 16 * k + 8, 1)
                strip[f, 16 * k : 16 * k + 16, LANES + part * 1024 : LANES + part * 1024 + 1024] = (
                    jnp.concatenate([upper[:, LANES:], lower[:, LANES:]], axis=0).astype(BF16)
                )
        return 0

    lax.fori_loop(0, 8, make_strip, 0)

    flip = flip_matrix()
    sign_row = lax.broadcasted_iota(jnp.int32, (8, 256), 0) % 4

    def unpack(c, step, total):
        back_rows = jnp.concatenate(
            [recv_in[c, step * 8 + u, 16:32, :] for u in range(8)], axis=0
        )
        turned = jnp.dot(back_rows, flip, preferred_element_type=F32)
        for u in range(8):
            shard = step * 8 + u
            place = step * 4 + u // 2
            e = u % 2
            product = recv_in[c, shard, 0:16, :].astype(F32)
            gated = recv_in[c, shard, 16:32, :].astype(F32)
            total = total + product * gated
            spread[e, pl.ds(pl.multiple_of(place * 32, 32), 16), :] = product
            prod_nat[e, pl.ds(pl.multiple_of(place * 16, 16), 16), :] = product
            reverse = turned[16 * u : 16 * u + 16]
            mirror = 31 - place
            spread[1 - e, pl.ds(pl.multiple_of(mirror * 32 + 16, 16), 16), :] = reverse
            grad_nat[e, pl.ds(pl.multiple_of(place * 16, 16), 16), :] = reverse
        return total

    def long_conv(c, q, _):
        f = QUAD * c + q
        for group in range(4):
            skip_rows = 64 * group
            acc = jnp.zeros((256 - skip_rows, 256), F32)
            for lag in range(8 * group, 8 * group + 8):
                even = lag - lag % 2
                lhs = xs[q, lag % 2, 256 + skip_rows - 8 * even : 512 - 8 * even, :]
                at = LANES + 256 * lag
                rhs = jnp.concatenate(
                    [strip[f, :, at : at + 256], strip[f, :, at - LANES : at + LANES]], axis=0
                )
                acc = acc + jnp.dot(lhs, rhs, preferred_element_type=F32)
            if group == 0:
                conv[q] = acc
            else:
                conv[q, skip_rows:256, :] += acc
        gain = jnp.where(
            sign_row == 0,
            skip[0, f],
            jnp.where(sign_row == 1, skip[1, f], jnp.where(sign_row == 2, skip[2, f], skip[3, f])),
        )
        for part in range(4):
            rows = slice(64 * part, 64 * part + 64)
            own = xs[q, 0, 256 + 64 * part : 320 + 64 * part, :].astype(F32)
            conv[q, rows, :] += own * jnp.concatenate([gain] * 8, axis=0)
        return 0

    def pack(c, step, _):
        turned = jnp.concatenate(
            [
                merged[u % 2, pl.ds(pl.multiple_of((step * 4 + u // 2) * 32 + 16, 16), 16), :]
                for u in range(8)
            ],
            axis=0,
        ).astype(BF16)
        turned = jnp.dot(turned, flip, preferred_element_type=F32).astype(BF16)
        for u in range(8):
            shard = step * 8 + u
            place = step * 4 + u // 2
            send_out[c, shard, 0:16, :] = merged[
                u % 2, pl.ds(pl.multiple_of(place * 32, 32), 16), :
            ].astype(BF16)
            send_out[c, SHARDS - 1 - shard, 16:32, :] = turned[16 * u : 16 * u + 16]
        return 0

    def owner_conv(c):
        all_copies(send_in, recv_in, in_sem, c).wait_recv()
        total = lax.fori_loop(0, 8, functools.partial(unpack, c), jnp.zeros((16, LANES), F32))
        d_skip[16 * c : 16 * c + 16, :] = jnp.broadcast_to(
            jnp.sum(total, axis=1, keepdims=True), (16, LANES)
        )
        for q in range(QUAD):
            tile = jnp.concatenate(
                [spread[e, pl.ds(q, 256, stride=4), :] for e in range(2)], axis=1
            )
            xs[q, 0, 256:512, :] = tile.astype(BF16)
            xs[q, 1, 256:512, :] = jnp.concatenate(
                [jnp.zeros((8, 256), F32), tile[0:248]], axis=0
            ).astype(BF16)
        lax.fori_loop(0, QUAD, functools.partial(long_conv, c), 0)
        for q in range(QUAD):
            for e in range(2):
                merged[e, pl.ds(q, 256, stride=4), :] = conv[q, :, LANES * e : LANES * e + LANES]
        lax.fori_loop(0, 8, functools.partial(pack, c), 0)
        send_all(send_out, recv_out, out_sem, c)

    def cross_dots(q, m, slot):
        for pair in range(4):
            sides = []
            for odd in range(2):
                lag = 2 * pair + odd
                half = pair
                parts = []
                for e in range(2):
                    carry = half + (1 if e == 1 and odd == 1 else 0)
                    at = pl.multiple_of(16 * m + 16 * (carry // 4), 16)
                    parts.append(shifted[q, (e + odd) % 2, carry % 4, pl.ds(at, 128), :])
                sides.append(jnp.concatenate(parts, axis=0))
            cross[slot, pair] = jnp.dot(
                prod_t[q], jnp.concatenate(sides, axis=1), preferred_element_type=F32
            )

    def diagonals(q, m, slot):
        for lag in range(8):
            cols = slice((lag % 2) * LANES, (lag % 2) * LANES + LANES)
            total = cross[slot, lag // 2, 0:8, cols]
            kept = total
            for k in range(1, 16):
                moved = pltpu.roll(cross[slot, lag // 2, 8 * k : 8 * k + 8, cols], 8 * k, 1)
                total = total + moved
                kept = kept + jnp.where(lane >= 8 * k, moved, 0.0)
            low[q, 8 * m + lag] = kept
            high[q, 8 * m + lag] = total - kept

    def owner_lags(c):
        for q in range(QUAD):
            for e in range(2):
                prod_t[q, :, LANES * e : LANES * e + LANES] = (
                    prod_nat[e, pl.ds(q, 128, stride=4), :].T.astype(BF16)
                )
                for k in range(4):
                    shifted[q, e, k, 0:128, :] = grad_nat[
                        e, pl.ds(q + 16 * k, 128, stride=4), :
                    ].astype(BF16)
        cross_dots(0, 0, 0)

        def two(step, _):
            q = step // 4
            m = 2 * (step % 4)
            cross_dots(q, m + 1, 1)
            diagonals(q, m, 0)
            later = jnp.minimum(step + 1, 15)
            cross_dots(later // 4, 2 * (later % 4), 0)
            diagonals(q, m + 1, 1)
            return 0

        lax.fori_loop(0, 16, two, 0)

        def turn(step, _):
            q = step // 4
            first = 16 * (step % 4)
            rolled = []
            for k in range(17):
                at = jnp.minimum(first + k, LAGS - 1)
                tile = low[q, at] + high[q, at + 1]
                rolled.append(pltpu.roll(tile, 0, 1, stride=1, stride_axis=0))
            rolled[16] = jnp.where(first == 48, 0.0, rolled[16])
            rows = [
                jnp.sum(jnp.where(lane >= row_ids(), rolled[k], rolled[k + 1]), axis=0, keepdims=True)
                for k in range(16)
            ]
            lagrow[q, step % 4] = jnp.concatenate(rows, axis=0)
            return 0

        lax.fori_loop(0, 16, turn, 0)
        for q in range(QUAD):
            turned = jnp.dot(
                jnp.concatenate([lagrow[q, r] for r in range(4)], axis=0).astype(BF16),
                flip,
                preferred_element_type=F32,
            ).astype(BF16)
            for r in range(REPS):
                lag_send[r, QUAD * c + q] = turned[16 * r : 16 * r + 16]

    owner_conv(0)
    owner_lags(0)
    owner_conv(1)
    owner_lags(1)

    def lag_copy(peer):
        return pltpu.make_async_remote_copy(
            src_ref=lag_send.at[peer], dst_ref=lag_recv.at[rep], send_sem=lag_sem.at[0],
            recv_sem=lag_sem.at[1], device_id=(me, peer), device_id_type=MESH,
        )

    for k in range(1, REPS):
        lag_copy(lax.rem(rep + k, REPS)).start()
    lag_recv[rep] = lag_send[rep]

    def make_grads(c, step, _):
        shards = pl.ds(pl.multiple_of(step * 8, 8), 8)
        mine = own_lanes(step)
        value = recv_out[c, shards, 16:32, :].astype(F32)
        three = (
            sig[3, c, shards].astype(F32) * recv_out[c, shards, 0:16, :].astype(F32),
            value * mixed[1, c, shards],
            value * mixed[0, c, shards],
        )
        for j in range(3):
            grads[c, j, shards] = three[j]
            spread_out = product_of(halves(three[j].reshape(8 * 16, LANES)), m_first[...])
            back[c, j] += gather(jnp.where(mine, spread_out, 0.0))
        return 0

    def back_copy(c):
        return pltpu.make_async_remote_copy(
            src_ref=back.at[c], dst_ref=back_in.at[c], send_sem=back_sem.at[0, c],
            recv_sem=back_sem.at[1, c],
            device_id=(lax.rem(me + SHARDS - 1, SHARDS), rep), device_id_type=MESH,
        )

    def post_first(c):
        all_copies(send_out, recv_out, out_sem, c).wait_recv()
        back[c] = jnp.zeros(back.shape[1:], F32)
        lax.fori_loop(0, SHARDS // GROUP, functools.partial(make_grads, c), 0)

        @pl.when(me > 0)
        def _():
            back_copy(c).start()

    def short_back(c, step, _):
        shards = pl.ds(pl.multiple_of(step * 8, 8), 8)
        mine = own_lanes(step)
        weight = product_of(eight(wts, c, shards), m_col[...])
        sums = jnp.zeros((8 * 16, LANES), F32)
        for j in range(3):
            here = eight(grads, c, j, shards)
            after = jnp.where(mine, jnp.concatenate([back_in[c, j]] * 8, axis=0), 0.0)
            moved = product_of(halves(here), m_late[...]) + product_of(halves(after), m_next[...])
            three = (here, moved[:, 0:LANES], moved[:, LANES:])
            signal = eight(sig, j, c, shards).astype(F32)
            total = None
            for i in range(3):
                k = 3 * j + i
                term = weight[:, k * LANES : (k + 1) * LANES] * three[i]
                total = term if i == 0 else total + term
                sums = sums + product_of(
                    halves(three[i] * signal), m_sum[2 * k * LANES : 2 * (k + 1) * LANES, :]
                )
            d_rows[c, j, shards] = total.astype(BF16).reshape(8, 16, LANES)
        for u in range(8):
            first = sums[16 * u : 16 * u + 8]
            second = pltpu.roll(sums[16 * u + 8 : 16 * u + 16], 18 * c + 9, 1)
            if c == 0:
                tap_send[step * 8 + u] = first + second
            else:
                tap_send[step * 8 + u] += pltpu.roll(first, 18 * c, 1) + second
        return 0

    def post_second(c):
        @pl.when(me < SHARDS - 1)
        def _():
            back_copy(c).wait_recv()

        lax.fori_loop(0, SHARDS // GROUP, functools.partial(short_back, c), 0)

    post_first(0)
    post_first(1)
    post_second(0)
    post_second(1)

    def tap_copy(peer):
        return pltpu.make_async_remote_copy(
            src_ref=tap_send.at[peer], dst_ref=tap_recv.at[me], send_sem=tap_sem.at[0],
            recv_sem=tap_sem.at[1], device_id=(peer, rep), device_id_type=MESH,
        )

    def send_taps(k, _):
        tap_copy(lax.rem(me + k, SHARDS)).start()
        return 0

    lax.fori_loop(1, SHARDS, send_taps, 0)
    tap_recv[me] = tap_send[me]

    def put_back(step, _):
        for half in range(4):
            pair = step * 4 + half
            rows = pl.ds(pl.multiple_of(pair * 16, 16), 16)
            for j in range(3):
                chunk = [
                    [d_rows[c, j, pair * 2 + u].astype(F32) for u in range(2)]
                    for c in range(CHUNKS)
                ]
                for gp in range(2):
                    tiles = [
                        swap_halves(
                            chunk[0][u][8 * gp : 8 * gp + 8], chunk[1][u][8 * gp : 8 * gp + 8]
                        )
                        for u in range(2)
                    ]
                    for g in range(2):
                        d_feat[j, 2 * gp + g, rows, :] = jnp.concatenate(
                            [tiles[0][g], tiles[1][g]], axis=0
                        ).astype(BF16)
        return 0

    lax.fori_loop(0, SHARDS // 8, put_back, 0)

    lag_all = pltpu.make_async_remote_copy(
        src_ref=lag_send.at[pl.ds(0, REPS - 1)], dst_ref=lag_recv.at[pl.ds(0, REPS - 1)],
        send_sem=lag_sem.at[0], recv_sem=lag_sem.at[1],
        device_id=(me, lax.rem(rep + 1, REPS)), device_id_type=MESH,
    )
    lag_all.wait_recv()
    for f in range(8):
        d_filt[f] = (
            lag_recv[0, f].astype(F32)
            + lag_recv[1, f].astype(F32)
            + lag_recv[2, f].astype(F32)
            + lag_recv[3, f].astype(F32)
        )

    tap_all = pltpu.make_async_remote_copy(
        src_ref=tap_send.at[pl.ds(0, SHARDS - 1)], dst_ref=tap_recv.at[pl.ds(0, SHARDS - 1)],
        send_sem=tap_sem.at[0], recv_sem=tap_sem.at[1],
        device_id=(lax.rem(me + 1, SHARDS), rep), device_id_type=MESH,
    )
    tap_all.wait_recv()
    d_short[...] = jnp.sum(tap_recv[...], axis=0)

    for c in range(CHUNKS):
        all_copies(send_in, recv_in, in_sem, c).wait_send()
        all_copies(send_out, recv_out, out_sem, c).wait_send()

        @pl.when(me > 0)
        def _():
            back_copy(c).wait_send()

    lag_all.wait_send()
    tap_all.wait_send()


def per_device(features, short_taps, skip_gain, filters, cotangent):
    tap_rows = jnp.transpose(short_taps, (1, 0, 3, 2)).reshape(36, 512)
    tap_rows = jnp.pad(tap_rows, ((0, 4), (0, 0)))
    vmem = pl.BlockSpec(memory_space=pltpu.VMEM)
    message = pltpu.VMEM((CHUNKS, SHARDS, 32, LANES), BF16)
    d_feat, d_short, d_skip, d_filt = pl.pallas_call(
        kernel,
        out_shape=(
            jax.ShapeDtypeStruct((3, 4, 512, LANES), BF16),
            jax.ShapeDtypeStruct((8, LANES), F32),
            jax.ShapeDtypeStruct((32, LANES), F32),
            jax.ShapeDtypeStruct((8, 16, LANES), F32),
        ),
        in_specs=[vmem, vmem, vmem, pl.BlockSpec(memory_space=pltpu.SMEM), vmem],
        out_specs=(vmem,) * 4,
        scratch_shapes=[
            pltpu.VMEM((4, CHUNKS, SHARDS, 16, LANES), BF16),
            pltpu.VMEM((2, CHUNKS, SHARDS, 16, LANES), F32),
            pltpu.VMEM((CHUNKS, SHARDS, 16, LANES), BF16),
            pltpu.VMEM((512, LANES), F32),
            pltpu.VMEM((8, LANES, LANES + 8192), BF16),
            pltpu.VMEM((8, LANES + 8192), F32),
            pltpu.VMEM((6, 16, LANES), BF16),
            pltpu.VMEM((6, 16, LANES), BF16),
            pltpu.VMEM((6, 16, LANES), F32),
            pltpu.VMEM((256, 256), BF16),
            pltpu.VMEM((LANES, 9 * LANES), BF16),
            pltpu.VMEM((256, 256), BF16),
            pltpu.VMEM((256, 256), BF16),
            pltpu.VMEM((256, LANES), BF16),
            pltpu.VMEM((18 * LANES, LANES), BF16),
            message, message, message, message,
            pltpu.VMEM((2, 1024, LANES), F32),
            pltpu.VMEM((2, 512, LANES), F32),
            pltpu.VMEM((2, 576, LANES), F32),
            pltpu.VMEM((QUAD, 2, 512, 256), BF16),
            pltpu.VMEM((QUAD, 256, 256), F32),
            pltpu.VMEM((2, 1024, LANES), F32),
            pltpu.VMEM((QUAD, 2, 4, 256, LANES), BF16),
            pltpu.VMEM((QUAD, LANES, 256), BF16),
            pltpu.VMEM((2, 4, LANES, 256), F32),
            pltpu.VMEM((QUAD, LAGS, 8, LANES), F32),
            pltpu.VMEM((QUAD, LAGS + 1, 8, LANES), F32),
            pltpu.VMEM((QUAD, 4, 16, LANES), F32),
            pltpu.VMEM((REPS, 8, 16, LANES), BF16),
            pltpu.VMEM((REPS, 8, 16, LANES), BF16),
            pltpu.VMEM((CHUNKS, 3, SHARDS, 16, LANES), F32),
            pltpu.VMEM((CHUNKS, 3, SHARDS, 16, LANES), BF16),
            pltpu.VMEM((CHUNKS, 3, 16, LANES), F32),
            pltpu.VMEM((CHUNKS, 3, 16, LANES), F32),
            pltpu.VMEM((SHARDS, 8, LANES), F32),
            pltpu.VMEM((SHARDS, 8, LANES), F32),
            pltpu.SemaphoreType.DMA((2,)),
            pltpu.SemaphoreType.DMA((2, CHUNKS)),
            pltpu.SemaphoreType.DMA((2, CHUNKS)),
            pltpu.SemaphoreType.DMA((2, CHUNKS)),
            pltpu.SemaphoreType.DMA((2,)),
            pltpu.SemaphoreType.DMA((2,)),
        ],
        compiler_params=pltpu.CompilerParams(
            collective_id=0, has_side_effects=True, vmem_limit_bytes=60 * 2**20
        ),
    )(features, cotangent, tap_rows, skip_gain, filters)
    short = d_short[:, :36].reshape(2, 4, 2, 2, 3, 3)
    short = jnp.transpose(short, (4, 3, 0, 2, 1, 5)).reshape(3, 4, 8, 3)
    skips = jnp.transpose(d_skip[:, 0].reshape(2, 4, 4), (1, 0, 2)).reshape(4, 8)
    return (d_feat, short, skips, d_filt.reshape(8, 2048))


def solution(mesh):
    placed = (
        P(None, "rep", None, "ctx"),
        P(None, "rep", None, None),
        P("rep", "ctx"),
        P("ctx", None),
        P("rep", None, "ctx"),
    )
    return jax.shard_map(
        per_device,
        mesh=mesh,
        in_specs=placed,
        out_specs=(
            P(None, "rep", None, "ctx"),
            P(None, "rep", "ctx", None),
            P("rep", "ctx"),
            P("ctx", "rep"),
        ),
        check_vma=False,
    )
```

```python
import functools

import jax
import jax.numpy as jnp
from jax import lax
from jax.experimental import pallas as pl
from jax.experimental.pallas import tpu as pltpu
from jax.sharding import PartitionSpec as P

MESH = pl.DeviceIdType.MESH
F32 = jnp.float32
BF16 = jnp.bfloat16

SHARDS = 64
REPS = 4
LANES = 128
CHUNKS = 2
QUAD = 4
GROUP = 8
LAGS = 64
WIDE = 32


def lane_ids():
    return lax.broadcasted_iota(jnp.int32, (8, LANES), 1)


def row_ids():
    return lax.broadcasted_iota(jnp.int32, (8, LANES), 0)


def swap_halves(first, second):
    upper = row_ids() < QUAD
    return (
        jnp.where(upper, first, pltpu.roll(second, QUAD, 0)),
        jnp.where(upper, pltpu.roll(first, QUAD, 0), second),
    )


def flip_matrix():
    rows = lax.broadcasted_iota(jnp.int32, (LANES, LANES), 0)
    cols = lax.broadcasted_iota(jnp.int32, (LANES, LANES), 1)
    return jnp.where(rows + cols == LANES - 1, 1.0, 0.0).astype(BF16)


def ids(rows, cols):
    shape = (rows, cols)
    return (
        lax.broadcasted_iota(jnp.int32, shape, 0),
        lax.broadcasted_iota(jnp.int32, shape, 1),
    )


def ones_where(condition):
    return jnp.where(condition, 1.0, 0.0).astype(BF16)


def product_of(left, right):
    return jnp.dot(left, right, preferred_element_type=F32)


def kernel(
    feat, cot, taps, skip, filt,
    d_rows, d_short, d_skip, d_filt,
    sig, mixed, wts, tcol, strip, base, front, front_in, halo,
    m_early, m_col, m_late, m_first, m_sum,
    send_in, recv_in, send_out, recv_out,
    spread, prod_nat, grad_nat, xs, conv, merged,
    shifted, prod_t, prod_half, cross, low, high, lagrow, lag_send, lag_recv,
    grads, early, back, back_out, back_in, taps_all, near_send, near_recv, far_send, far_recv,
    front_sem, in_sem, out_sem, out_recv_sem, back_sem, near_sem, far_sem, lag_sem,
):
    me = lax.axis_index("ctx")
    rep = lax.axis_index("rep")
    lane = lane_ids()

    barrier = pltpu.get_barrier_semaphore()

    def greet(k, _):
        pl.semaphore_signal(
            barrier, inc=1, device_id=(lax.rem(me + k, SHARDS), rep), device_id_type=MESH
        )
        return 0

    lax.fori_loop(1, SHARDS, greet, 0)
    for k in range(1, REPS):
        pl.semaphore_signal(
            barrier, inc=1, device_id=(me, lax.rem(rep + k, REPS)), device_id_type=MESH
        )

    row, col = ids(LANES, LANES)
    last = ones_where(row - (LANES - 2) == col % 2)
    m_early[0:LANES, 0:LANES] = ones_where(col == row + 1)
    m_early[0:LANES, LANES:] = ones_where(col == row + 2)
    m_early[LANES:, 0:LANES] = ones_where((col == 0) & (row % 2 == 1))
    m_early[LANES:, LANES:] = ones_where((col < 2) & (col == row % 2))
    for k in range(9):
        m_col[:, k * LANES : (k + 1) * LANES] = ones_where((row < 27) & (row % 9 == k))

    def arrange(step, _):
        for half in range(4):
            pair = step * 4 + half
            rows = pl.ds(pl.multiple_of(pair * 16, 16), 16)
            for j in range(4):
                wide = []
                for g in range(4):
                    block = feat[j, g, rows, :] if j < 3 else cot[g, rows, :]
                    wide.append(block.astype(F32))
                for u in range(2):
                    both = [
                        swap_halves(
                            wide[2 * gp][8 * u : 8 * u + 8], wide[2 * gp + 1][8 * u : 8 * u + 8]
                        )
                        for gp in range(2)
                    ]
                    for c in range(CHUNKS):
                        sig[j, c, pair * 2 + u] = jnp.concatenate(
                            [both[0][c], both[1][c]], axis=0
                        ).astype(BF16)
        return 0

    zero = jnp.zeros((8, LANES), F32)
    lax.fori_loop(0, SHARDS // 8, arrange, 0)

    def eight(ref, *at):
        return ref[at].reshape(8 * 16, LANES)

    def own_lanes(step):
        rows, cols = ids(8 * 16, LANES)
        return cols // 2 == step * 8 + rows // 16

    def gather(values):
        total = values[0:16]
        for u in range(1, 8):
            total = total + values[16 * u : 16 * u + 16]
        return total

    def pack_front(c, step, _):
        mine = own_lanes(step)
        shards = pl.ds(pl.multiple_of(step * 8, 8), 8)
        for j in range(3):
            spread_out = product_of(eight(sig, j, c, shards), last)
            halo[c, j] += gather(jnp.where(mine, spread_out, 0.0))
        return 0

    halo[...] = jnp.zeros(halo.shape, F32)

    def front_copy(c):
        return pltpu.make_async_remote_copy(
            src_ref=front.at[c], dst_ref=front_in.at[c], send_sem=front_sem.at[0, c],
            recv_sem=front_sem.at[1, c], device_id=(lax.rem(me + 1, SHARDS), rep),
            device_id_type=MESH,
        )

    @pl.when(me == 0)
    def _():
        front_in[...] = jnp.zeros(front_in.shape, BF16)

    @pl.when(me == SHARDS - 1)
    def _():
        back_in[...] = jnp.zeros(back_in.shape, BF16)

    for c in range(CHUNKS):
        lax.fori_loop(0, SHARDS // 8, functools.partial(pack_front, c), 0)
        front[c] = halo[c].astype(BF16)
        if c == 0:
            pl.semaphore_wait(barrier, SHARDS - 1 + REPS - 1)

        @pl.when(me < SHARDS - 1)
        def _():
            front_copy(c).start()

    for part in range(4):
        cols = slice(part * LANES, (part + 1) * LANES)
        rows = [taps[j, i, g : g + 1, cols] for g in range(4) for j in range(3) for i in range(3)]
        tcol[cols, :] = jnp.concatenate(
            rows + [jnp.zeros((LANES - 36, LANES), F32)], axis=0
        ).T

    def arrange_taps(step, _):
        for u in range(8):
            shard = step * 8 + u
            tile = tcol[pl.ds(pl.multiple_of(shard * 8, 8), 8), :]
            made = ([], [])
            for gp in range(2):
                first = tile if gp == 0 else pltpu.roll(tile, LANES - 18 * gp, 1)
                second = pltpu.roll(tile, LANES - 18 * gp - 9, 1)
                for c, weight in enumerate(swap_halves(first, second)):
                    high_part = weight.astype(BF16).astype(F32)
                    rest = weight - high_part
                    mid_part = rest.astype(BF16).astype(F32)
                    rest = rest - mid_part
                    three = jnp.where(
                        lane < 9,
                        high_part,
                        jnp.where(lane < 18, pltpu.roll(mid_part, 9, 1), pltpu.roll(rest, 18, 1)),
                    )
                    made[c].append(jnp.where(lane < 27, three, 0.0))
            for c in range(CHUNKS):
                wts[c, shard] = jnp.concatenate(made[c], axis=0).astype(BF16)
        return 0

    lax.fori_loop(0, SHARDS // 8, arrange_taps, 0)

    def in_copy(c, peer):
        return pltpu.make_async_remote_copy(
            src_ref=send_in.at[c, peer], dst_ref=recv_in.at[c, me], send_sem=in_sem.at[0, c],
            recv_sem=in_sem.at[1, c], device_id=(peer, rep), device_id_type=MESH,
        )

    def out_copy(c, peer):
        return pltpu.make_async_remote_copy(
            src_ref=send_out.at[c, peer], dst_ref=recv_out.at[c, me], send_sem=out_sem.at[c],
            recv_sem=out_recv_sem.at[c, me // GROUP], device_id=(peer, rep), device_id_type=MESH,
        )

    def in_copies(c):
        others = pl.ds(0, SHARDS - 1)
        return pltpu.make_async_remote_copy(
            src_ref=send_in.at[c, others], dst_ref=recv_in.at[c, others], send_sem=in_sem.at[0, c],
            recv_sem=in_sem.at[1, c], device_id=(lax.rem(me + 1, SHARDS), rep), device_id_type=MESH,
        )

    def out_copies(c, group, count):
        some = pl.ds(0, count)
        return pltpu.make_async_remote_copy(
            src_ref=send_out.at[c, some], dst_ref=recv_out.at[c, some], send_sem=out_sem.at[c],
            recv_sem=out_recv_sem.at[c, group], device_id=(lax.rem(me + 1, SHARDS), rep),
            device_id_type=MESH,
        )

    def send_results(c):
        def one(k, _):
            out_copy(c, lax.rem(me + k, SHARDS)).start()
            return 0

        lax.fori_loop(1, SHARDS, one, 0)
        recv_out[c, me] = send_out[c, me]

    def short_conv(c, step, _):
        group = lax.rem(me // GROUP + step, SHARDS // GROUP)
        shards = pl.ds(pl.multiple_of(group * GROUP, GROUP), GROUP)
        mine = own_lanes(group)
        weight = product_of(eight(wts, c, shards), m_col[...])
        mix = []
        for j in range(3):
            here = eight(sig, j, c, shards)
            before = jnp.concatenate([front_in[c, j].astype(F32)] * 8, axis=0)
            before = jnp.where(mine, before, 0.0).astype(BF16)
            moved = product_of(jnp.concatenate([here, before], axis=1), m_early[...])
            for i in range(2):
                early[c, j, i, shards] = (
                    moved[:, i * LANES : (i + 1) * LANES].astype(BF16).reshape(8, 16, LANES)
                )
            three = [weight[:, (3 * j + i) * LANES : (3 * j + i + 1) * LANES] for i in range(3)]
            mix.append(
                three[0] * here.astype(F32)
                + three[1] * moved[:, 0:LANES]
                + three[2] * moved[:, LANES:]
            )
        mixed[0, c, shards] = mix[1].reshape(8, 16, LANES)
        mixed[1, c, shards] = mix[2].reshape(8, 16, LANES)
        send_in[c, shards, 0:16, :] = (mix[1] * mix[2]).astype(BF16).reshape(8, 16, LANES)
        gated = eight(sig, 3, c, shards).astype(F32) * mix[0]
        send_in[c, shards, 16:32, :] = gated.astype(BF16).reshape(8, 16, LANES)
        for u in range(GROUP):
            shard = group * GROUP + lax.rem(me + u, GROUP)

            @pl.when(shard != me)
            def _():
                in_copy(c, shard).start()

        return 0

    for c in range(CHUNKS):

        @pl.when(me > 0)
        def _():
            front_copy(c).wait_recv()

        lax.fori_loop(0, SHARDS // GROUP, functools.partial(short_conv, c), 0)
        recv_in[c, me] = send_in[c, me]

    strip[:, :, 0:LANES] = jnp.zeros((8, LANES, LANES), BF16)
    base[:, 0:LANES] = zero

    def make_strip(f, _):
        row = filt[pl.ds(f, 1), :]
        for part in range(8):
            cols = slice(LANES + part * 1024, LANES + part * 1024 + 1024)
            base[:, cols] = jnp.broadcast_to(row[:, part * 1024 : part * 1024 + 1024], (8, 1024))
        for part in reversed(range(8)):
            wide = base[:, part * 1024 : part * 1024 + 1152]
            base[:, LANES + part * 1024 : LANES + part * 1024 + 1024] = pltpu.roll(
                wide, 0, 1, stride=1, stride_axis=0
            )[:, LANES:]
        for part in range(8):
            wide = base[:, part * 1024 : part * 1024 + 1152]
            for k in range(8):
                upper = wide if k == 0 else pltpu.roll(wide, 16 * k, 1)
                lower = pltpu.roll(wide, 16 * k + 8, 1)
                strip[f, 16 * k : 16 * k + 16, LANES + part * 1024 : LANES + part * 1024 + 1024] = (
                    jnp.concatenate([upper[:, LANES:], lower[:, LANES:]], axis=0).astype(BF16)
                )
        return 0

    lax.fori_loop(0, 8, make_strip, 0)

    m_late[0:LANES, 0:LANES] = ones_where(col == row - 1)
    m_late[0:LANES, LANES:] = ones_where(col == row - 2)
    m_late[LANES:, 0:LANES] = ones_where((col == LANES - 1) & (row % 2 == 0))
    m_late[LANES:, LANES:] = ones_where((col >= LANES - 2) & (col % 2 == row % 2))
    m_first[...] = ones_where(row == col % 2)
    for k in range(9):
        m_sum[k * LANES : (k + 1) * LANES, :] = ones_where(col == k)

    for q in range(QUAD):
        for u in range(2):
            xs[q, u, 0:256, :] = jnp.zeros((256, 256), BF16)
        for e in range(2):
            for k in range(4):
                shifted[q, e, k, 128:256, :] = jnp.zeros((128, LANES), BF16)
        high[q, LAGS] = zero
    for e in range(2):
        grad_nat[e, 512:576, :] = jnp.zeros((64, LANES), F32)

    flip = flip_matrix()
    sign_row = lax.broadcasted_iota(jnp.int32, (8, 256), 0) % 4

    def unpack(c, step, total):
        first = pl.ds(pl.multiple_of(step * WIDE, WIDE), WIDE)
        turned = product_of(recv_in[c, first, 16:32, :].reshape(WIDE * 16, LANES), flip)
        for u in range(WIDE):
            shard = step * WIDE + u
            place = step * (WIDE // 2) + u // 2
            e = u % 2
            product = recv_in[c, shard, 0:16, :].astype(F32)
            gated = recv_in[c, shard, 16:32, :].astype(F32)
            total = total + product * gated
            spread[e, pl.ds(pl.multiple_of(place * 32, 32), 16), :] = product
            prod_nat[e, pl.ds(pl.multiple_of(place * 16, 16), 16), :] = product
            reverse = turned[16 * u : 16 * u + 16]
            mirror = 31 - place
            spread[1 - e, pl.ds(pl.multiple_of(mirror * 32 + 16, 16), 16), :] = reverse
            grad_nat[e, pl.ds(pl.multiple_of(place * 16, 16), 16), :] = reverse
        return total

    def long_conv(c, q, _):
        f = QUAD * c + q
        for group in range(4):
            skip_rows = 64 * group
            acc = jnp.zeros((256 - skip_rows, 256), F32)
            for lag in range(8 * group, 8 * group + 8):
                even = lag - lag % 2
                lhs = xs[q, lag % 2, 256 + skip_rows - 8 * even : 512 - 8 * even, :]
                at = LANES + 256 * lag
                rhs = jnp.concatenate(
                    [strip[f, :, at : at + 256], strip[f, :, at - LANES : at + LANES]], axis=0
                )
                acc = acc + jnp.dot(lhs, rhs, preferred_element_type=F32)
            if group == 0:
                conv[q] = acc
            else:
                conv[q, skip_rows:256, :] += acc
        gain = jnp.where(
            sign_row == 0,
            skip[0, f],
            jnp.where(sign_row == 1, skip[1, f], jnp.where(sign_row == 2, skip[2, f], skip[3, f])),
        )
        for part in range(4):
            rows = slice(64 * part, 64 * part + 64)
            own = xs[q, 0, 256 + 64 * part : 320 + 64 * part, :].astype(F32)
            conv[q, rows, :] += own * jnp.concatenate([gain] * 8, axis=0)
        return 0

    def pack(c, step, _):
        half = WIDE // 2
        rows = pl.ds(pl.multiple_of(step * half * 32, 32), half * 32)
        both = [merged[e, rows, :].astype(BF16).reshape(half, 32, LANES) for e in range(2)]
        turned = product_of(
            jnp.concatenate([b[:, 16:32].reshape(half * 16, LANES) for b in both], axis=0), flip
        ).astype(BF16)
        for u in range(WIDE):
            shard = step * WIDE + u
            at = (u % 2) * half + u // 2
            send_out[c, shard, 0:16, :] = both[u % 2][u // 2, 0:16]
            send_out[c, SHARDS - 1 - shard, 16:32, :] = turned[16 * at : 16 * at + 16]
        return 0

    def owner_conv(c):
        in_copies(c).wait_recv()
        total = lax.fori_loop(0, SHARDS // WIDE, functools.partial(unpack, c), jnp.zeros((16, LANES), F32))
        d_skip[16 * c : 16 * c + 16, :] = jnp.broadcast_to(
            jnp.sum(total, axis=1, keepdims=True), (16, LANES)
        )
        for q in range(QUAD):
            tile = jnp.concatenate(
                [spread[e, pl.ds(q, 256, stride=4), :] for e in range(2)], axis=1
            )
            xs[q, 0, 256:512, :] = tile.astype(BF16)
            xs[q, 1, 256:512, :] = jnp.concatenate(
                [jnp.zeros((8, 256), F32), tile[0:248]], axis=0
            ).astype(BF16)
        lax.fori_loop(0, QUAD, functools.partial(long_conv, c), 0)
        for q in range(QUAD):
            for e in range(2):
                merged[e, pl.ds(q, 256, stride=4), :] = conv[q, :, LANES * e : LANES * e + LANES]
        lax.fori_loop(0, SHARDS // WIDE, functools.partial(pack, c), 0)
        send_results(c)

    def cross_dots(q, m, slot):
        rows = 128 if m < 4 else 64
        left = prod_t if m < 4 else prod_half
        for pair in range(4):
            sides = []
            for odd in range(2):
                parts = []
                for e in range(2):
                    carry = pair + (1 if e == 1 and odd == 1 else 0)
                    at = 16 * m + 16 * (carry // 4)
                    parts.append(shifted[q, (e + odd) % 2, carry % 4, at : at + rows, :])
                sides.append(jnp.concatenate(parts, axis=0))
            cross[slot, pair] = product_of(left[q], jnp.concatenate(sides, axis=1))

    def diagonals(q, m, slot):
        for lag in range(8):
            cols = slice((lag % 2) * LANES, (lag % 2) * LANES + LANES)
            total = cross[slot, lag // 2, 0:8, cols]
            kept = total
            for k in range(1, 16):
                moved = pltpu.roll(cross[slot, lag // 2, 8 * k : 8 * k + 8, cols], 8 * k, 1)
                total = total + moved
                kept = kept + jnp.where(lane >= 8 * k, moved, 0.0)
            low[q, 8 * m + lag] = kept
            high[q, 8 * m + lag] = total - kept

    def owner_lags(c):
        for q in range(QUAD):
            for e in range(2):
                prod_t[q, :, LANES * e : LANES * e + LANES] = (
                    prod_nat[e, pl.ds(q, 128, stride=4), :].T.astype(BF16)
                )
                prod_half[q, :, 64 * e : 64 * e + 64] = (
                    prod_nat[e, pl.ds(q, 64, stride=4), :].T.astype(BF16)
                )
                for k in range(4):
                    shifted[q, e, k, 0:128, :] = grad_nat[
                        e, pl.ds(q + 16 * k, 128, stride=4), :
                    ].astype(BF16)
        cross_dots(0, 0, 0)

        def one_filter(q, _):
            for m in range(8):
                if m < 7:
                    cross_dots(q, m + 1, (m + 1) % 2)
                else:
                    cross_dots(jnp.minimum(q + 1, QUAD - 1), 0, 0)
                diagonals(q, m, m % 2)
            return 0

        lax.fori_loop(0, QUAD, one_filter, 0)

        def turn(step, _):
            q = step // 4
            first = 16 * (step % 4)
            rolled = []
            for k in range(17):
                at = jnp.minimum(first + k, LAGS - 1)
                tile = low[q, at] + high[q, at + 1]
                rolled.append(pltpu.roll(tile, 0, 1, stride=1, stride_axis=0))
            rolled[16] = jnp.where(first == 48, 0.0, rolled[16])
            rows = [
                jnp.sum(jnp.where(lane >= row_ids(), rolled[k], rolled[k + 1]), axis=0, keepdims=True)
                for k in range(16)
            ]
            lagrow[q, step % 4] = jnp.concatenate(rows, axis=0)
            return 0

        lax.fori_loop(0, 16, turn, 0)
        for q in range(QUAD):
            turned = jnp.dot(
                jnp.concatenate([lagrow[q, r] for r in range(4)], axis=0).astype(BF16),
                flip,
                preferred_element_type=F32,
            ).astype(BF16)
            for r in range(REPS):
                lag_send[r, QUAD * c + q] = turned[16 * r : 16 * r + 16]

    owner_conv(0)
    owner_lags(0)
    owner_conv(1)
    owner_lags(1)

    def lag_copy(peer):
        return pltpu.make_async_remote_copy(
            src_ref=lag_send.at[peer], dst_ref=lag_recv.at[rep], send_sem=lag_sem.at[0],
            recv_sem=lag_sem.at[1], device_id=(me, peer), device_id_type=MESH,
        )

    for k in range(1, REPS):
        lag_copy(lax.rem(rep + k, REPS)).start()
    lag_recv[rep] = lag_send[rep]

    def make_grads(c, step, _):
        own = me // GROUP
        group = lax.rem(own + GROUP - 1 - step, GROUP)

        @pl.when(group == own)
        def _():
            out_copies(c, group, GROUP - 1).wait_recv()

        @pl.when(group != own)
        def _():
            out_copies(c, group, GROUP).wait_recv()

        shards = pl.ds(pl.multiple_of(group * 8, 8), 8)
        mine = own_lanes(group)
        value = recv_out[c, shards, 16:32, :].astype(F32)
        three = (
            sig[3, c, shards].astype(F32) * recv_out[c, shards, 0:16, :].astype(F32),
            value * mixed[1, c, shards],
            value * mixed[0, c, shards],
        )
        terms = []
        for j in range(3):
            narrow = three[j].astype(BF16)
            grads[c, j, shards] = narrow
            spread_out = product_of(narrow.reshape(8 * 16, LANES), m_first[...])
            back[c, j] += gather(jnp.where(mine, spread_out, 0.0))
            wide = three[j].reshape(8 * 16, LANES)
            terms.append((wide * eight(sig, j, c, shards).astype(F32)).astype(BF16))
            for i in range(2):
                terms.append((wide * eight(early, c, j, i, shards).astype(F32)).astype(BF16))
        sums = product_of(jnp.concatenate(terms, axis=1), m_sum[...])
        for u in range(8):
            first = sums[16 * u : 16 * u + 8]
            second = pltpu.roll(sums[16 * u + 8 : 16 * u + 16], 18 * c + 9, 1)
            if c == 0:
                taps_all[group * 8 + u] = first + second
            else:
                taps_all[group * 8 + u] += pltpu.roll(first, 18 * c, 1) + second
        return 0

    def back_copy(c):
        return pltpu.make_async_remote_copy(
            src_ref=back_out.at[c], dst_ref=back_in.at[c], send_sem=back_sem.at[0, c],
            recv_sem=back_sem.at[1, c],
            device_id=(lax.rem(me + SHARDS - 1, SHARDS), rep), device_id_type=MESH,
        )

    def grads_of(c):
        back[c] = jnp.zeros(back.shape[1:], F32)
        lax.fori_loop(0, SHARDS // GROUP, functools.partial(make_grads, c), 0)
        back_out[c] = back[c].astype(BF16)

        @pl.when(me > 0)
        def _():
            back_copy(c).start()

    def short_back(c, step, _):
        shards = pl.ds(pl.multiple_of(step * 8, 8), 8)
        mine = own_lanes(step)
        weight = product_of(eight(wts, c, shards), m_col[...])
        for j in range(3):
            here = eight(grads, c, j, shards)
            after = jnp.concatenate([back_in[c, j].astype(F32)] * 8, axis=0)
            after = jnp.where(mine, after, 0.0).astype(BF16)
            moved = product_of(jnp.concatenate([here, after], axis=1), m_late[...])
            at = 3 * j * LANES
            total = (
                weight[:, at : at + LANES] * here.astype(F32)
                + weight[:, at + LANES : at + 2 * LANES] * moved[:, 0:LANES]
                + weight[:, at + 2 * LANES : at + 3 * LANES] * moved[:, LANES:]
            )
            d_rows[c, j, shards] = total.astype(BF16).reshape(8, 16, LANES)
        return 0

    def features_of(c):
        @pl.when(me < SHARDS - 1)
        def _():
            back_copy(c).wait_recv()

        lax.fori_loop(0, SHARDS // GROUP, functools.partial(short_back, c), 0)

    grads_of(0)
    features_of(0)
    grads_of(1)

    own_group = me // GROUP
    own_place = lax.rem(me, GROUP)

    def near_copy(place):
        return pltpu.make_async_remote_copy(
            src_ref=near_send.at[place], dst_ref=near_recv.at[own_place], send_sem=near_sem.at[0],
            recv_sem=near_sem.at[1], device_id=(own_group * GROUP + place, rep),
            device_id_type=MESH,
        )

    def far_copy(group):
        return pltpu.make_async_remote_copy(
            src_ref=far_send.at[group], dst_ref=far_recv.at[own_group], send_sem=far_sem.at[0],
            recv_sem=far_sem.at[1], device_id=(group * GROUP + own_place, rep),
            device_id_type=MESH,
        )

    for place in range(GROUP):
        for m in range(3):
            tile = taps_all[3 * m * GROUP + place]
            for n in range(1, 3 if m < 2 else 2):
                tile = tile + pltpu.roll(taps_all[(3 * m + n) * GROUP + place], 36 * n, 1)
            near_send[place, 8 * m : 8 * m + 8, :] = tile
    for k in range(1, GROUP):
        near_copy(lax.rem(own_place + k, GROUP)).start()
    near_recv[own_place] = near_send[own_place]

    features_of(1)

    seven = pl.ds(0, GROUP - 1)
    near_all = pltpu.make_async_remote_copy(
        src_ref=near_send.at[seven], dst_ref=near_recv.at[seven], send_sem=near_sem.at[0],
        recv_sem=near_sem.at[1], device_id=(lax.rem(me + 1, SHARDS), rep), device_id_type=MESH,
    )
    far_all = pltpu.make_async_remote_copy(
        src_ref=far_send.at[seven], dst_ref=far_recv.at[seven], send_sem=far_sem.at[0],
        recv_sem=far_sem.at[1], device_id=(lax.rem(me + 1, SHARDS), rep), device_id_type=MESH,
    )
    near_all.wait_recv()
    packed = jnp.sum(near_recv[...], axis=0)
    for group in range(GROUP):
        tile = packed[8 * (group // 3) : 8 * (group // 3) + 8]
        if group % 3:
            tile = pltpu.roll(tile, LANES - 36 * (group % 3), 1)
        far_send[group] = jnp.where(lane < 36, tile, 0.0)
    for k in range(1, GROUP):
        far_copy(lax.rem(own_group + k, GROUP)).start()
    far_recv[own_group] = far_send[own_group]

    lag_all = pltpu.make_async_remote_copy(
        src_ref=lag_send.at[pl.ds(0, REPS - 1)], dst_ref=lag_recv.at[pl.ds(0, REPS - 1)],
        send_sem=lag_sem.at[0], recv_sem=lag_sem.at[1],
        device_id=(me, lax.rem(rep + 1, REPS)), device_id_type=MESH,
    )
    lag_all.wait_recv()
    for f in range(8):
        d_filt[16 * f : 16 * f + 16, :] = (
            lag_recv[0, f].astype(F32)
            + lag_recv[1, f].astype(F32)
            + lag_recv[2, f].astype(F32)
            + lag_recv[3, f].astype(F32)
        )

    far_all.wait_recv()
    d_short[...] = jnp.sum(far_recv[...], axis=0)

    for c in range(CHUNKS):
        in_copies(c).wait_send()
        out_copies(c, 0, SHARDS - 1).wait_send()

        @pl.when(me < SHARDS - 1)
        def _():
            front_copy(c).wait_send()

        @pl.when(me > 0)
        def _():
            back_copy(c).wait_send()

    lag_all.wait_send()
    near_all.wait_send()
    far_all.wait_send()


def finish(d_rows, short, skips, lags, d_feat, d_short, d_skip, d_filt):
    for pair in range(d_rows.shape[2] // 2):
        rows = slice(16 * pair, 16 * pair + 16)
        for j in range(3):
            chunk = [
                [d_rows[c, j, pair * 2 + u].astype(F32) for u in range(2)] for c in range(CHUNKS)
            ]
            for gp in range(2):
                at = slice(8 * gp, 8 * gp + 8)
                tiles = [swap_halves(chunk[0][u][at], chunk[1][u][at]) for u in range(2)]
                for g in range(2):
                    d_feat[j, 2 * gp + g, rows, :] = jnp.concatenate(
                        [tiles[0][g], tiles[1][g]], axis=0
                    ).astype(BF16)

    @pl.when(pl.program_id(0) == 0)
    def _():
        turned = jnp.concatenate(
            [short[...], jnp.zeros((LANES - 8, LANES), F32)], axis=0
        ).T
        wide = lax.broadcasted_iota(jnp.int32, (18, LANES), 1)
        upper, lower = turned[0:18], turned[18:36]
        members = (
            jnp.where(wide < QUAD, upper, pltpu.roll(lower, QUAD, 1)),
            jnp.where(wide < QUAD, pltpu.roll(upper, LANES - QUAD, 1), lower),
        )
        for j in range(3):
            for i in range(3):
                k = 3 * j + i
                four = [members[g % 2][9 * (g // 2) + k : 9 * (g // 2) + k + 1] for g in range(4)]
                d_short[j, i] = jnp.concatenate(four, axis=0)[:, 0:8]
        flat = jnp.concatenate([skips[...], jnp.zeros((LANES - 32, LANES), F32)], axis=0).T[0:8]
        four = []
        for g in range(4):
            first = flat if g == 0 else pltpu.roll(flat, LANES - 4 * g, 1)
            second = pltpu.roll(flat, LANES - 12 - 4 * g, 1)
            four.append(jnp.where(lane_ids() < QUAD, first, second)[0:1])
        d_skip[...] = jnp.concatenate(four, axis=0)[:, 0:8]
        for k in range(16):
            d_filt[:, k * LANES : (k + 1) * LANES] = lags[pl.ds(k, 8, stride=16), :]


def per_device(features, short_taps, skip_gain, filters, cotangent):
    tap_rows = jnp.transpose(short_taps, (0, 3, 1, 2))
    vmem = pl.BlockSpec(memory_space=pltpu.VMEM)
    message = pltpu.VMEM((CHUNKS, SHARDS, 32, LANES), BF16)
    parts = pl.pallas_call(
        kernel,
        out_shape=(
            jax.ShapeDtypeStruct((CHUNKS, 3, SHARDS, 16, LANES), BF16),
            jax.ShapeDtypeStruct((8, LANES), F32),
            jax.ShapeDtypeStruct((32, LANES), F32),
            jax.ShapeDtypeStruct((128, LANES), F32),
        ),
        in_specs=[vmem, vmem, vmem, pl.BlockSpec(memory_space=pltpu.SMEM), vmem],
        out_specs=(vmem,) * 4,
        scratch_shapes=[
            pltpu.VMEM((4, CHUNKS, SHARDS, 16, LANES), BF16),
            pltpu.VMEM((2, CHUNKS, SHARDS, 16, LANES), F32),
            pltpu.VMEM((CHUNKS, SHARDS, 16, LANES), BF16),
            pltpu.VMEM((512, LANES), F32),
            pltpu.VMEM((8, LANES, LANES + 8192), BF16),
            pltpu.VMEM((8, LANES + 8192), F32),
            pltpu.VMEM((CHUNKS, 3, 16, LANES), BF16),
            pltpu.VMEM((CHUNKS, 3, 16, LANES), BF16),
            pltpu.VMEM((CHUNKS, 3, 16, LANES), F32),
            pltpu.VMEM((256, 256), BF16),
            pltpu.VMEM((LANES, 9 * LANES), BF16),
            pltpu.VMEM((256, 256), BF16),
            pltpu.VMEM((LANES, LANES), BF16),
            pltpu.VMEM((9 * LANES, LANES), BF16),
            message, message, message, message,
            pltpu.VMEM((2, 1024, LANES), F32),
            pltpu.VMEM((2, 512, LANES), F32),
            pltpu.VMEM((2, 576, LANES), F32),
            pltpu.VMEM((QUAD, 2, 512, 256), BF16),
            pltpu.VMEM((QUAD, 256, 256), F32),
            pltpu.VMEM((2, 1024, LANES), F32),
            pltpu.VMEM((QUAD, 2, 4, 256, LANES), BF16),
            pltpu.VMEM((QUAD, LANES, 256), BF16),
            pltpu.VMEM((QUAD, LANES, LANES), BF16),
            pltpu.VMEM((2, 4, LANES, 256), F32),
            pltpu.VMEM((QUAD, LAGS, 8, LANES), F32),
            pltpu.VMEM((QUAD, LAGS + 1, 8, LANES), F32),
            pltpu.VMEM((QUAD, 4, 16, LANES), F32),
            pltpu.VMEM((REPS, 8, 16, LANES), BF16),
            pltpu.VMEM((REPS, 8, 16, LANES), BF16),
            pltpu.VMEM((CHUNKS, 3, SHARDS, 16, LANES), BF16),
            pltpu.VMEM((CHUNKS, 3, 2, SHARDS, 16, LANES), BF16),
            pltpu.VMEM((CHUNKS, 3, 16, LANES), F32),
            pltpu.VMEM((CHUNKS, 3, 16, LANES), BF16),
            pltpu.VMEM((CHUNKS, 3, 16, LANES), BF16),
            pltpu.VMEM((SHARDS, 8, LANES), F32),
            pltpu.VMEM((GROUP, 24, LANES), F32),
            pltpu.VMEM((GROUP, 24, LANES), F32),
            pltpu.VMEM((GROUP, 8, LANES), F32),
            pltpu.VMEM((GROUP, 8, LANES), F32),
            pltpu.SemaphoreType.DMA((2, CHUNKS)),
            pltpu.SemaphoreType.DMA((2, CHUNKS)),
            pltpu.SemaphoreType.DMA((CHUNKS,)),
            pltpu.SemaphoreType.DMA((CHUNKS, GROUP)),
            pltpu.SemaphoreType.DMA((2, CHUNKS)),
            pltpu.SemaphoreType.DMA((2,)),
            pltpu.SemaphoreType.DMA((2,)),
            pltpu.SemaphoreType.DMA((2,)),
        ],
        compiler_params=pltpu.CompilerParams(
            collective_id=0, has_side_effects=True, vmem_limit_bytes=60 * 2**20
        ),
    )(features, cotangent, tap_rows, skip_gain, filters)
    steps = 4
    fixed = lambda *shape: pl.BlockSpec(shape, lambda i: (0,) * len(shape))
    d_feat, short, skips, lags = pl.pallas_call(
        finish,
        grid=(steps,),
        out_shape=(
            jax.ShapeDtypeStruct((3, 4, 512, LANES), BF16),
            jax.ShapeDtypeStruct((3, 3, 4, 8), F32),
            jax.ShapeDtypeStruct((4, 8), F32),
            jax.ShapeDtypeStruct((8, 2048), F32),
        ),
        in_specs=[
            pl.BlockSpec((CHUNKS, 3, SHARDS // steps, 16, LANES), lambda i: (0, 0, i, 0, 0)),
            fixed(8, LANES),
            fixed(32, LANES),
            fixed(128, LANES),
        ],
        out_specs=(
            pl.BlockSpec((3, 4, 512 // steps, LANES), lambda i: (0, 0, i, 0)),
            fixed(3, 3, 4, 8),
            fixed(4, 8),
            fixed(8, 2048),
        ),
    )(*parts)
    return (d_feat, jnp.transpose(short, (0, 2, 3, 1)), skips, lags)


def solution(mesh):
    placed = (
        P(None, "rep", None, "ctx"),
        P(None, "rep", None, None),
        P("rep", "ctx"),
        P("ctx", None),
        P("rep", None, "ctx"),
    )
    return jax.shard_map(
        per_device,
        mesh=mesh,
        in_specs=placed,
        out_specs=(
            P(None, "rep", None, "ctx"),
            P(None, "rep", "ctx", None),
            P("rep", "ctx"),
            P("ctx", "rep"),
        ),
        check_vma=False,
    )
```

```python
import functools

import jax
import jax.numpy as jnp
from jax import lax
from jax.experimental import pallas as pl
from jax.experimental.pallas import tpu as pltpu
from jax.sharding import PartitionSpec as P

MESH = pl.DeviceIdType.MESH
F32 = jnp.float32
BF16 = jnp.bfloat16

SHARDS = 64
REPS = 4
LANES = 128
CHUNKS = 2
QUAD = 4
GROUP = 8
LAGS = 64
WIDE = 32


def lane_ids():
    return lax.broadcasted_iota(jnp.int32, (8, LANES), 1)


def row_ids():
    return lax.broadcasted_iota(jnp.int32, (8, LANES), 0)


def swap_halves(first, second):
    upper = row_ids() < QUAD
    return (
        jnp.where(upper, first, pltpu.roll(second, QUAD, 0)),
        jnp.where(upper, pltpu.roll(first, QUAD, 0), second),
    )


def flip_matrix():
    rows = lax.broadcasted_iota(jnp.int32, (LANES, LANES), 0)
    cols = lax.broadcasted_iota(jnp.int32, (LANES, LANES), 1)
    return jnp.where(rows + cols == LANES - 1, 1.0, 0.0).astype(BF16)


def ids(rows, cols):
    shape = (rows, cols)
    return (
        lax.broadcasted_iota(jnp.int32, shape, 0),
        lax.broadcasted_iota(jnp.int32, shape, 1),
    )


def ones_where(condition):
    return jnp.where(condition, 1.0, 0.0).astype(BF16)


def product_of(left, right):
    return jnp.dot(left, right, preferred_element_type=F32)


def kernel(
    feat, cot, taps, skip, filt,
    d_out, d_short, d_skip, d_filt,
    d_rows, sig, mixed, wts, tcol, strip, base, front, front_in, before_rows,
    m_early, m_col, m_late, m_first, m_sum,
    send_in, recv_in, send_out, recv_out,
    spread, prod_nat, grad_nat, xs, conv, merged,
    shifted, prod_t, prod_half, cross, low, high, lagrow, lag_send, lag_recv,
    grads, early, back, back_out, back_in, taps_all, tap_send, tap_recv,
    front_sem, in_sem, out_sem, out_recv_sem, back_sem, tap_sem, lag_sem, rows_sem,
):
    me = lax.axis_index("ctx")
    rep = lax.axis_index("rep")
    lane = lane_ids()

    barrier = pltpu.get_barrier_semaphore()

    def greet(k, _):
        pl.semaphore_signal(
            barrier, inc=1, device_id=(lax.rem(me + k, SHARDS), rep), device_id_type=MESH
        )
        return 0

    lax.fori_loop(1, SHARDS, greet, 0)
    for k in range(1, REPS):
        pl.semaphore_signal(
            barrier, inc=1, device_id=(me, lax.rem(rep + k, REPS)), device_id_type=MESH
        )

    zero = jnp.zeros((8, LANES), F32)
    row, col = ids(LANES, LANES)
    last = ones_where(row - (LANES - 2) == col % 2)

    owner = lax.shift_right_logical(ids(16, LANES)[1], 1)

    def pack_front(j, _):
        for gp in range(2):
            tiles = []
            for g in range(2):
                spread_out = product_of(feat[j, 2 * gp + g], last)
                tile = zero
                for shard in range(SHARDS):
                    tile = jnp.where(
                        owner[0:8] == shard, spread_out[8 * shard : 8 * shard + 8], tile
                    )
                tiles.append(tile)
            front[2 * j + gp] = jnp.concatenate(tiles, axis=0).astype(BF16)
        return 0

    lax.fori_loop(0, 3, pack_front, 0)

    @pl.when(me == 0)
    def _():
        front_in[...] = jnp.zeros(front_in.shape, BF16)

    @pl.when(me == SHARDS - 1)
    def _():
        back_in[...] = jnp.zeros(back_in.shape, BF16)

    pl.semaphore_wait(barrier, SHARDS - 1 + REPS - 1)

    def front_copy():
        return pltpu.make_async_remote_copy(
            src_ref=front, dst_ref=front_in, send_sem=front_sem.at[0], recv_sem=front_sem.at[1],
            device_id=(lax.rem(me + 1, SHARDS), rep), device_id_type=MESH,
        )

    @pl.when(me < SHARDS - 1)
    def _():
        front_copy().start()

    def arrange(step, _):
        for half in range(4):
            pair = step * 4 + half
            rows = pl.ds(pl.multiple_of(pair * 16, 16), 16)
            for j in range(4):
                wide = []
                for g in range(4):
                    block = feat[j, g, rows, :] if j < 3 else cot[g, rows, :]
                    wide.append(block.astype(F32))
                for u in range(2):
                    both = [
                        swap_halves(
                            wide[2 * gp][8 * u : 8 * u + 8], wide[2 * gp + 1][8 * u : 8 * u + 8]
                        )
                        for gp in range(2)
                    ]
                    for c in range(CHUNKS):
                        sig[j, c, pair * 2 + u] = jnp.concatenate(
                            [both[0][c], both[1][c]], axis=0
                        ).astype(BF16)
        return 0


    m_early[0:LANES, 0:LANES] = ones_where(col == row + 1)
    m_early[0:LANES, LANES:] = ones_where(col == row + 2)
    m_early[LANES:, 0:LANES] = ones_where((col == 0) & (row % 2 == 1))
    m_early[LANES:, LANES:] = ones_where((col < 2) & (col == row % 2))
    for k in range(9):
        m_col[:, k * LANES : (k + 1) * LANES] = ones_where((row < 27) & (row % 9 == k))

    def eight(ref, *at):
        return ref[at].reshape(8 * 16, LANES)

    def scatter(block, first):
        return jnp.concatenate(
            [jnp.where(owner == first + u, block, 0.0) for u in range(8)], axis=0
        ).astype(BF16)

    def gather(values, first, block):
        for u in range(values.shape[0] // 16):
            block = jnp.where(owner == first + u, values[16 * u : 16 * u + 16], block)
        return block

    for part in range(4):
        cols = slice(part * LANES, (part + 1) * LANES)
        rows = [taps[j, i, g : g + 1, cols] for g in range(4) for j in range(3) for i in range(3)]
        tcol[cols, :] = jnp.concatenate(
            rows + [jnp.zeros((LANES - 36, LANES), F32)], axis=0
        ).T

    def arrange_taps(step, _):
        for u in range(8):
            shard = step * 8 + u
            tile = tcol[pl.ds(pl.multiple_of(shard * 8, 8), 8), :]
            made = ([], [])
            for gp in range(2):
                first = tile if gp == 0 else pltpu.roll(tile, LANES - 18 * gp, 1)
                second = pltpu.roll(tile, LANES - 18 * gp - 9, 1)
                for c, weight in enumerate(swap_halves(first, second)):
                    high_part = weight.astype(BF16).astype(F32)
                    rest = weight - high_part
                    mid_part = rest.astype(BF16).astype(F32)
                    rest = rest - mid_part
                    three = jnp.where(
                        lane < 9,
                        high_part,
                        jnp.where(lane < 18, pltpu.roll(mid_part, 9, 1), pltpu.roll(rest, 18, 1)),
                    )
                    made[c].append(jnp.where(lane < 27, three, 0.0))
            for c in range(CHUNKS):
                wts[c, shard] = jnp.concatenate(made[c], axis=0).astype(BF16)
        return 0


    def in_copy(c, peer):
        return pltpu.make_async_remote_copy(
            src_ref=send_in.at[c, peer], dst_ref=recv_in.at[c, me], send_sem=in_sem.at[0, c],
            recv_sem=in_sem.at[1, c], device_id=(peer, rep), device_id_type=MESH,
        )

    def out_copy(c, peer):
        return pltpu.make_async_remote_copy(
            src_ref=send_out.at[c, peer], dst_ref=recv_out.at[c, me], send_sem=out_sem.at[c],
            recv_sem=out_recv_sem.at[c, me // GROUP], device_id=(peer, rep), device_id_type=MESH,
        )

    def in_copies(c):
        others = pl.ds(0, SHARDS - 1)
        return pltpu.make_async_remote_copy(
            src_ref=send_in.at[c, others], dst_ref=recv_in.at[c, others], send_sem=in_sem.at[0, c],
            recv_sem=in_sem.at[1, c], device_id=(lax.rem(me + 1, SHARDS), rep), device_id_type=MESH,
        )

    def out_copies(c, group, count):
        some = pl.ds(0, count)
        return pltpu.make_async_remote_copy(
            src_ref=send_out.at[c, some], dst_ref=recv_out.at[c, some], send_sem=out_sem.at[c],
            recv_sem=out_recv_sem.at[c, group], device_id=(lax.rem(me + 1, SHARDS), rep),
            device_id_type=MESH,
        )

    def send_results(c):
        def one(k, _):
            out_copy(c, lax.rem(me + k, SHARDS)).start()
            return 0

        lax.fori_loop(1, SHARDS, one, 0)
        recv_out[c, me] = send_out[c, me]

    def short_conv(c, step, _):
        group = lax.rem(me // GROUP + step, SHARDS // GROUP)
        shards = pl.ds(pl.multiple_of(group * GROUP, GROUP), GROUP)
        weight = product_of(eight(wts, c, shards), m_col[...])
        mix = []
        for j in range(3):
            here = eight(sig, j, c, shards)
            before = scatter(before_rows[c, j], group * GROUP)
            moved = product_of(jnp.concatenate([here, before], axis=1), m_early[...])
            for i in range(2):
                early[c, j, i, shards] = (
                    moved[:, i * LANES : (i + 1) * LANES].astype(BF16).reshape(8, 16, LANES)
                )
            three = [weight[:, (3 * j + i) * LANES : (3 * j + i + 1) * LANES] for i in range(3)]
            mix.append(
                three[0] * here.astype(F32)
                + three[1] * moved[:, 0:LANES]
                + three[2] * moved[:, LANES:]
            )
        mixed[0, c, shards] = mix[1].reshape(8, 16, LANES)
        mixed[1, c, shards] = mix[2].reshape(8, 16, LANES)
        send_in[c, shards, 0:16, :] = (mix[1] * mix[2]).astype(BF16).reshape(8, 16, LANES)
        gated = eight(sig, 3, c, shards).astype(F32) * mix[0]
        send_in[c, shards, 16:32, :] = gated.astype(BF16).reshape(8, 16, LANES)
        for u in range(GROUP):
            shard = group * GROUP + lax.rem(me + u, GROUP)

            @pl.when(shard != me)
            def _():
                in_copy(c, shard).start()

        return 0

    @pl.when(me > 0)
    def _():
        front_copy().wait_recv()

    for j in range(3):
        pairs = [front_in[2 * j + gp].astype(F32) for gp in range(2)]
        pairs = [swap_halves(pair[0:8], pair[8:16]) for pair in pairs]
        for c in range(CHUNKS):
            before_rows[c, j] = jnp.concatenate([pairs[0][c], pairs[1][c]], axis=0)

    def first_pass(step, _):
        group = lax.rem(me // GROUP + step, SHARDS // GROUP)
        arrange(group, 0)
        arrange_taps(group, 0)
        return short_conv(0, step, 0)

    lax.fori_loop(0, SHARDS // GROUP, first_pass, 0)
    lax.fori_loop(0, SHARDS // GROUP, functools.partial(short_conv, 1), 0)
    for c in range(CHUNKS):
        recv_in[c, me] = send_in[c, me]

    strip[:, :, 0:LANES] = jnp.zeros((8, LANES, LANES), BF16)
    base[:, 0:LANES] = zero

    def make_strip(f, _):
        row = filt[pl.ds(f, 1), :]
        for part in range(8):
            cols = slice(LANES + part * 1024, LANES + part * 1024 + 1024)
            base[:, cols] = jnp.broadcast_to(row[:, part * 1024 : part * 1024 + 1024], (8, 1024))
        for part in reversed(range(8)):
            wide = base[:, part * 1024 : part * 1024 + 1152]
            base[:, LANES + part * 1024 : LANES + part * 1024 + 1024] = pltpu.roll(
                wide, 0, 1, stride=1, stride_axis=0
            )[:, LANES:]
        for part in range(8):
            wide = base[:, part * 1024 : part * 1024 + 1152]
            for k in range(8):
                upper = wide if k == 0 else pltpu.roll(wide, 16 * k, 1)
                lower = pltpu.roll(wide, 16 * k + 8, 1)
                strip[f, 16 * k : 16 * k + 16, LANES + part * 1024 : LANES + part * 1024 + 1024] = (
                    jnp.concatenate([upper[:, LANES:], lower[:, LANES:]], axis=0).astype(BF16)
                )
        return 0

    lax.fori_loop(0, 8, make_strip, 0)

    m_late[0:LANES, 0:LANES] = ones_where(col == row - 1)
    m_late[0:LANES, LANES:] = ones_where(col == row - 2)
    m_late[LANES:, 0:LANES] = ones_where((col == LANES - 1) & (row % 2 == 0))
    m_late[LANES:, LANES:] = ones_where((col >= LANES - 2) & (col % 2 == row % 2))
    m_first[...] = ones_where(row == col % 2)
    for k in range(9):
        m_sum[k * LANES : (k + 1) * LANES, :] = ones_where(col == k)

    for q in range(QUAD):
        for u in range(2):
            xs[q, u, 0:256, :] = jnp.zeros((256, 256), BF16)
        for e in range(2):
            for k in range(4):
                shifted[q, e, k, 128:256, :] = jnp.zeros((128, LANES), BF16)
        high[q, LAGS] = zero
    for e in range(2):
        grad_nat[e, 512:576, :] = jnp.zeros((64, LANES), F32)

    flip = flip_matrix()
    sign_row = lax.broadcasted_iota(jnp.int32, (8, 256), 0) % 4

    def unpack(c, step, total):
        first = pl.ds(pl.multiple_of(step * WIDE, WIDE), WIDE)
        turned = product_of(recv_in[c, first, 16:32, :].reshape(WIDE * 16, LANES), flip)
        for u in range(WIDE):
            shard = step * WIDE + u
            place = step * (WIDE // 2) + u // 2
            e = u % 2
            product = recv_in[c, shard, 0:16, :].astype(F32)
            gated = recv_in[c, shard, 16:32, :].astype(F32)
            total = total + product * gated
            spread[e, pl.ds(pl.multiple_of(place * 32, 32), 16), :] = product
            prod_nat[e, pl.ds(pl.multiple_of(place * 16, 16), 16), :] = product
            reverse = turned[16 * u : 16 * u + 16]
            mirror = 31 - place
            spread[1 - e, pl.ds(pl.multiple_of(mirror * 32 + 16, 16), 16), :] = reverse
            grad_nat[e, pl.ds(pl.multiple_of(place * 16, 16), 16), :] = reverse
        return total

    def long_conv(c, q, _):
        f = QUAD * c + q
        for group in range(4):
            skip_rows = 64 * group
            acc = jnp.zeros((256 - skip_rows, 256), F32)
            for lag in range(8 * group, 8 * group + 8):
                even = lag - lag % 2
                lhs = xs[q, lag % 2, 256 + skip_rows - 8 * even : 512 - 8 * even, :]
                at = LANES + 256 * lag
                rhs = jnp.concatenate(
                    [strip[f, :, at : at + 256], strip[f, :, at - LANES : at + LANES]], axis=0
                )
                acc = acc + jnp.dot(lhs, rhs, preferred_element_type=F32)
            if group == 0:
                conv[q] = acc
            else:
                conv[q, skip_rows:256, :] += acc
        gain = jnp.where(
            sign_row == 0,
            skip[0, f],
            jnp.where(sign_row == 1, skip[1, f], jnp.where(sign_row == 2, skip[2, f], skip[3, f])),
        )
        for part in range(4):
            rows = slice(64 * part, 64 * part + 64)
            own = xs[q, 0, 256 + 64 * part : 320 + 64 * part, :].astype(F32)
            conv[q, rows, :] += own * jnp.concatenate([gain] * 8, axis=0)
        return 0

    def pack(c, step, _):
        half = WIDE // 2
        rows = pl.ds(pl.multiple_of(step * half * 32, 32), half * 32)
        both = [merged[e, rows, :].astype(BF16).reshape(half, 32, LANES) for e in range(2)]
        turned = product_of(
            jnp.concatenate([b[:, 16:32].reshape(half * 16, LANES) for b in both], axis=0), flip
        ).astype(BF16)
        for u in range(WIDE):
            shard = step * WIDE + u
            at = (u % 2) * half + u // 2
            send_out[c, shard, 0:16, :] = both[u % 2][u // 2, 0:16]
            send_out[c, SHARDS - 1 - shard, 16:32, :] = turned[16 * at : 16 * at + 16]
        return 0

    def owner_conv(c):
        in_copies(c).wait_recv()
        total = lax.fori_loop(0, SHARDS // WIDE, functools.partial(unpack, c), jnp.zeros((16, LANES), F32))
        d_skip[16 * c : 16 * c + 16, :] = jnp.broadcast_to(
            jnp.sum(total, axis=1, keepdims=True), (16, LANES)
        )
        for q in range(QUAD):
            tile = jnp.concatenate(
                [spread[e, pl.ds(q, 256, stride=4), :] for e in range(2)], axis=1
            )
            xs[q, 0, 256:512, :] = tile.astype(BF16)
            xs[q, 1, 256:512, :] = jnp.concatenate(
                [jnp.zeros((8, 256), F32), tile[0:248]], axis=0
            ).astype(BF16)
        lax.fori_loop(0, QUAD, functools.partial(long_conv, c), 0)
        for q in range(QUAD):
            for e in range(2):
                merged[e, pl.ds(q, 256, stride=4), :] = conv[q, :, LANES * e : LANES * e + LANES]
        lax.fori_loop(0, SHARDS // WIDE, functools.partial(pack, c), 0)
        send_results(c)

    def cross_dots(q, m, slot):
        rows = 128 if m < 4 else 64
        left = prod_t if m < 4 else prod_half
        for pair in range(4):
            sides = []
            for odd in range(2):
                parts = []
                for e in range(2):
                    carry = pair + (1 if e == 1 and odd == 1 else 0)
                    at = 16 * m + 16 * (carry // 4)
                    parts.append(shifted[q, (e + odd) % 2, carry % 4, at : at + rows, :])
                sides.append(jnp.concatenate(parts, axis=0))
            cross[slot, pair] = product_of(left[q], jnp.concatenate(sides, axis=1))

    def diagonals(q, m, slot):
        for lag in range(8):
            cols = slice((lag % 2) * LANES, (lag % 2) * LANES + LANES)
            total = cross[slot, lag // 2, 0:8, cols]
            kept = total
            for k in range(1, 16):
                moved = pltpu.roll(cross[slot, lag // 2, 8 * k : 8 * k + 8, cols], 8 * k, 1)
                total = total + moved
                kept = kept + jnp.where(lane >= 8 * k, moved, 0.0)
            low[q, 8 * m + lag] = kept
            high[q, 8 * m + lag] = total - kept

    def owner_lags(c):
        for q in range(QUAD):
            for e in range(2):
                prod_t[q, :, LANES * e : LANES * e + LANES] = (
                    prod_nat[e, pl.ds(q, 128, stride=4), :].T.astype(BF16)
                )
                prod_half[q, :, 64 * e : 64 * e + 64] = (
                    prod_nat[e, pl.ds(q, 64, stride=4), :].T.astype(BF16)
                )
                for k in range(4):
                    shifted[q, e, k, 0:128, :] = grad_nat[
                        e, pl.ds(q + 16 * k, 128, stride=4), :
                    ].astype(BF16)
        cross_dots(0, 0, 0)

        def one_filter(q, _):
            for m in range(8):
                if m < 7:
                    cross_dots(q, m + 1, (m + 1) % 2)
                else:
                    cross_dots(jnp.minimum(q + 1, QUAD - 1), 0, 0)
                diagonals(q, m, m % 2)
            return 0

        lax.fori_loop(0, QUAD, one_filter, 0)

        def turn(step, _):
            q = step // 4
            first = 16 * (step % 4)
            rolled = []
            for k in range(17):
                at = jnp.minimum(first + k, LAGS - 1)
                tile = low[q, at] + high[q, at + 1]
                rolled.append(pltpu.roll(tile, 0, 1, stride=1, stride_axis=0))
            rolled[16] = jnp.where(first == 48, 0.0, rolled[16])
            rows = [
                jnp.sum(jnp.where(lane >= row_ids(), rolled[k], rolled[k + 1]), axis=0, keepdims=True)
                for k in range(16)
            ]
            lagrow[q, step % 4] = jnp.concatenate(rows, axis=0)
            return 0

        lax.fori_loop(0, 16, turn, 0)
        for q in range(QUAD):
            turned = jnp.dot(
                jnp.concatenate([lagrow[q, r] for r in range(4)], axis=0).astype(BF16),
                flip,
                preferred_element_type=F32,
            ).astype(BF16)
            for r in range(REPS):
                lag_send[r, QUAD * c + q] = turned[16 * r : 16 * r + 16]

    owner_conv(0)
    owner_lags(0)
    owner_conv(1)
    owner_lags(1)

    def lag_copy(peer):
        return pltpu.make_async_remote_copy(
            src_ref=lag_send.at[peer], dst_ref=lag_recv.at[rep], send_sem=lag_sem.at[0],
            recv_sem=lag_sem.at[1], device_id=(me, peer), device_id_type=MESH,
        )

    for k in range(1, REPS):
        lag_copy(lax.rem(rep + k, REPS)).start()
    lag_recv[rep] = lag_send[rep]

    def make_grads(c, step, _):
        own = me // GROUP
        pair = lax.rem(own // 2 + GROUP // 2 - 1 - step, GROUP // 2)
        for half in range(2):
            group = 2 * pair + half

            @pl.when(group == own)
            def _():
                out_copies(c, group, GROUP - 1).wait_recv()

            @pl.when(group != own)
            def _():
                out_copies(c, group, GROUP).wait_recv()

        shards = pl.ds(pl.multiple_of(pair * 16, 16), 16)
        value = recv_out[c, shards, 16:32, :].astype(F32)
        three = (
            sig[3, c, shards].astype(F32) * recv_out[c, shards, 0:16, :].astype(F32),
            value * mixed[1, c, shards],
            value * mixed[0, c, shards],
        )
        terms = []
        for j in range(3):
            narrow = three[j].astype(BF16)
            grads[c, j, shards] = narrow
            spread_out = product_of(narrow.reshape(16 * 16, LANES), m_first[...])
            back[c, j] = gather(spread_out, pair * 16, back[c, j])
            terms.append((three[j] * sig[j, c, shards].astype(F32)).astype(BF16))
            for i in range(2):
                terms.append((three[j] * early[c, j, i, shards].astype(F32)).astype(BF16))
        terms = [term.reshape(16 * 16, LANES) for term in terms]
        sums = product_of(jnp.concatenate(terms, axis=1), m_sum[...])
        for u in range(16):
            first = sums[16 * u : 16 * u + 8]
            second = pltpu.roll(sums[16 * u + 8 : 16 * u + 16], 18 * c + 9, 1)
            at = pl.ds(pl.multiple_of((pair * 16 + u) * 8, 8), 8)
            if c == 0:
                taps_all[at, :] = first + second
            else:
                taps_all[at, :] += pltpu.roll(first, 18 * c, 1) + second
        return 0

    def back_copy(c):
        return pltpu.make_async_remote_copy(
            src_ref=back_out.at[c], dst_ref=back_in.at[c], send_sem=back_sem.at[0, c],
            recv_sem=back_sem.at[1, c],
            device_id=(lax.rem(me + SHARDS - 1, SHARDS), rep), device_id_type=MESH,
        )

    def grads_of(c):
        back[c] = jnp.zeros(back.shape[1:], F32)
        lax.fori_loop(0, GROUP // 2, functools.partial(make_grads, c), 0)
        back_out[c] = back[c].astype(BF16)

        @pl.when(me > 0)
        def _():
            back_copy(c).start()

    def short_back(c, step, _):
        shards = pl.ds(pl.multiple_of(step * 8, 8), 8)
        weight = product_of(eight(wts, c, shards), m_col[...])
        for j in range(3):
            here = eight(grads, c, j, shards)
            after = scatter(back_in[c, j].astype(F32), step * 8)
            moved = product_of(jnp.concatenate([here, after], axis=1), m_late[...])
            at = 3 * j * LANES
            total = (
                weight[:, at : at + LANES] * here.astype(F32)
                + weight[:, at + LANES : at + 2 * LANES] * moved[:, 0:LANES]
                + weight[:, at + 2 * LANES : at + 3 * LANES] * moved[:, LANES:]
            )
            d_rows[c, j, shards] = total.astype(BF16).reshape(8, 16, LANES)
        return 0

    def features_of(c):
        @pl.when(me < SHARDS - 1)
        def _():
            back_copy(c).wait_recv()

        lax.fori_loop(0, SHARDS // GROUP, functools.partial(short_back, c), 0)

    def rows_copy(c):
        return pltpu.make_async_copy(d_rows.at[c], d_out.at[c], rows_sem.at[c])

    grads_of(0)
    features_of(0)
    rows_copy(0).start()
    grads_of(1)

    def tap_copy(peer):
        return pltpu.make_async_remote_copy(
            src_ref=tap_send.at[peer], dst_ref=tap_recv.at[me], send_sem=tap_sem.at[0],
            recv_sem=tap_sem.at[1], device_id=(peer, rep), device_id_type=MESH,
        )

    for m in range(3):
        total = taps_all[pl.ds(3 * m, SHARDS, stride=8), :]
        for n in range(1, 3 if m < 2 else 2):
            total = total + pltpu.roll(taps_all[pl.ds(3 * m + n, SHARDS, stride=8), :], 36 * n, 1)
        tap_send[:, m, :] = total
    tap_send[:, 3, :] = jnp.zeros((SHARDS, LANES), F32)

    def send_taps(k, _):
        tap_copy(lax.rem(me + k, SHARDS)).start()
        return 0

    lax.fori_loop(1, SHARDS, send_taps, 0)
    tap_recv[me] = tap_send[me]

    features_of(1)
    rows_copy(1).start()

    lag_all = pltpu.make_async_remote_copy(
        src_ref=lag_send.at[pl.ds(0, REPS - 1)], dst_ref=lag_recv.at[pl.ds(0, REPS - 1)],
        send_sem=lag_sem.at[0], recv_sem=lag_sem.at[1],
        device_id=(me, lax.rem(rep + 1, REPS)), device_id_type=MESH,
    )
    lag_all.wait_recv()
    for f in range(8):
        d_filt[16 * f : 16 * f + 16, :] = (
            lag_recv[0, f].astype(F32)
            + lag_recv[1, f].astype(F32)
            + lag_recv[2, f].astype(F32)
            + lag_recv[3, f].astype(F32)
        )

    others = pl.ds(0, SHARDS - 1)
    tap_all = pltpu.make_async_remote_copy(
        src_ref=tap_send.at[others], dst_ref=tap_recv.at[others], send_sem=tap_sem.at[0],
        recv_sem=tap_sem.at[1], device_id=(lax.rem(me + 1, SHARDS), rep), device_id_type=MESH,
    )
    tap_all.wait_recv()
    d_short[0:4, :] = jnp.sum(tap_recv[...], axis=0)
    d_short[4:8, :] = jnp.zeros((4, LANES), F32)

    for c in range(CHUNKS):
        rows_copy(c).wait()
        in_copies(c).wait_send()
        out_copies(c, 0, SHARDS - 1).wait_send()

        @pl.when(me > 0)
        def _():
            back_copy(c).wait_send()

    lag_all.wait_send()
    tap_all.wait_send()

    @pl.when(me < SHARDS - 1)
    def _():
        front_copy().wait_send()


def finish(d_rows, short, skips, lags, d_feat, d_short, d_skip, d_filt):
    for pair in range(d_rows.shape[2] // 2):
        rows = slice(16 * pair, 16 * pair + 16)
        for j in range(3):
            chunk = [
                [d_rows[c, j, pair * 2 + u].astype(F32) for u in range(2)] for c in range(CHUNKS)
            ]
            for gp in range(2):
                at = slice(8 * gp, 8 * gp + 8)
                tiles = [swap_halves(chunk[0][u][at], chunk[1][u][at]) for u in range(2)]
                for g in range(2):
                    d_feat[j, 2 * gp + g, rows, :] = jnp.concatenate(
                        [tiles[0][g], tiles[1][g]], axis=0
                    ).astype(BF16)

    @pl.when(pl.program_id(0) == 0)
    def _():
        moved = [short[...]] + [pltpu.roll(short[...], LANES - 36 * n, 1) for n in (1, 2)]
        eight_rows = [moved[r % 3][r // 3 : r // 3 + 1] for r in range(8)]
        turned = jnp.concatenate(
            eight_rows + [jnp.zeros((LANES - 8, LANES), F32)], axis=0
        ).T
        wide = lax.broadcasted_iota(jnp.int32, (18, LANES), 1)
        upper, lower = turned[0:18], turned[18:36]
        members = (
            jnp.where(wide < QUAD, upper, pltpu.roll(lower, QUAD, 1)),
            jnp.where(wide < QUAD, pltpu.roll(upper, LANES - QUAD, 1), lower),
        )
        for j in range(3):
            for i in range(3):
                k = 3 * j + i
                four = [members[g % 2][9 * (g // 2) + k : 9 * (g // 2) + k + 1] for g in range(4)]
                d_short[j, i] = jnp.concatenate(four, axis=0)[:, 0:8]
        flat = jnp.concatenate([skips[...], jnp.zeros((LANES - 32, LANES), F32)], axis=0).T[0:8]
        four = []
        for g in range(4):
            first = flat if g == 0 else pltpu.roll(flat, LANES - 4 * g, 1)
            second = pltpu.roll(flat, LANES - 12 - 4 * g, 1)
            four.append(jnp.where(lane_ids() < QUAD, first, second)[0:1])
        d_skip[...] = jnp.concatenate(four, axis=0)[:, 0:8]
        for k in range(16):
            d_filt[:, k * LANES : (k + 1) * LANES] = lags[pl.ds(k, 8, stride=16), :]


def per_device(features, short_taps, skip_gain, filters, cotangent):
    tap_rows = jnp.transpose(short_taps, (0, 3, 1, 2))
    vmem = pl.BlockSpec(memory_space=pltpu.VMEM)
    message = pltpu.VMEM((CHUNKS, SHARDS, 32, LANES), BF16)
    parts = pl.pallas_call(
        kernel,
        out_shape=(
            jax.ShapeDtypeStruct((CHUNKS, 3, SHARDS, 16, LANES), BF16),
            jax.ShapeDtypeStruct((8, LANES), F32),
            jax.ShapeDtypeStruct((32, LANES), F32),
            jax.ShapeDtypeStruct((128, LANES), F32),
        ),
        in_specs=[vmem, vmem, vmem, pl.BlockSpec(memory_space=pltpu.SMEM), vmem],
        out_specs=(pl.BlockSpec(memory_space=pl.ANY), vmem, vmem, vmem),
        scratch_shapes=[
            pltpu.VMEM((CHUNKS, 3, SHARDS, 16, LANES), BF16),
            pltpu.VMEM((4, CHUNKS, SHARDS, 16, LANES), BF16),
            pltpu.VMEM((2, CHUNKS, SHARDS, 16, LANES), F32),
            pltpu.VMEM((CHUNKS, SHARDS, 16, LANES), BF16),
            pltpu.VMEM((512, LANES), F32),
            pltpu.VMEM((8, LANES, LANES + 8192), BF16),
            pltpu.VMEM((8, LANES + 8192), F32),
            pltpu.VMEM((6, 16, LANES), BF16),
            pltpu.VMEM((6, 16, LANES), BF16),
            pltpu.VMEM((CHUNKS, 3, 16, LANES), F32),
            pltpu.VMEM((256, 256), BF16),
            pltpu.VMEM((LANES, 9 * LANES), BF16),
            pltpu.VMEM((256, 256), BF16),
            pltpu.VMEM((LANES, LANES), BF16),
            pltpu.VMEM((9 * LANES, LANES), BF16),
            message, message, message, message,
            pltpu.VMEM((2, 1024, LANES), F32),
            pltpu.VMEM((2, 512, LANES), F32),
            pltpu.VMEM((2, 576, LANES), F32),
            pltpu.VMEM((QUAD, 2, 512, 256), BF16),
            pltpu.VMEM((QUAD, 256, 256), F32),
            pltpu.VMEM((2, 1024, LANES), F32),
            pltpu.VMEM((QUAD, 2, 4, 256, LANES), BF16),
            pltpu.VMEM((QUAD, LANES, 256), BF16),
            pltpu.VMEM((QUAD, LANES, LANES), BF16),
            pltpu.VMEM((2, 4, LANES, 256), F32),
            pltpu.VMEM((QUAD, LAGS, 8, LANES), F32),
            pltpu.VMEM((QUAD, LAGS + 1, 8, LANES), F32),
            pltpu.VMEM((QUAD, 4, 16, LANES), F32),
            pltpu.VMEM((REPS, 8, 16, LANES), BF16),
            pltpu.VMEM((REPS, 8, 16, LANES), BF16),
            pltpu.VMEM((CHUNKS, 3, SHARDS, 16, LANES), BF16),
            pltpu.VMEM((CHUNKS, 3, 2, SHARDS, 16, LANES), BF16),
            pltpu.VMEM((CHUNKS, 3, 16, LANES), F32),
            pltpu.VMEM((CHUNKS, 3, 16, LANES), BF16),
            pltpu.VMEM((CHUNKS, 3, 16, LANES), BF16),
            pltpu.VMEM((SHARDS * 8, LANES), F32),
            pltpu.VMEM((SHARDS, 4, LANES), F32),
            pltpu.VMEM((SHARDS, 4, LANES), F32),
            pltpu.SemaphoreType.DMA((2,)),
            pltpu.SemaphoreType.DMA((2, CHUNKS)),
            pltpu.SemaphoreType.DMA((CHUNKS,)),
            pltpu.SemaphoreType.DMA((CHUNKS, GROUP)),
            pltpu.SemaphoreType.DMA((2, CHUNKS)),
            pltpu.SemaphoreType.DMA((2,)),
            pltpu.SemaphoreType.DMA((2,)),
            pltpu.SemaphoreType.DMA((CHUNKS,)),
        ],
        compiler_params=pltpu.CompilerParams(
            collective_id=0, has_side_effects=True, vmem_limit_bytes=60 * 2**20
        ),
    )(features, cotangent, tap_rows, skip_gain, filters)
    steps = 2
    fixed = lambda *shape: pl.BlockSpec(shape, lambda i: (0,) * len(shape))
    d_feat, short, skips, lags = pl.pallas_call(
        finish,
        grid=(steps,),
        out_shape=(
            jax.ShapeDtypeStruct((3, 4, 512, LANES), BF16),
            jax.ShapeDtypeStruct((3, 3, 4, 8), F32),
            jax.ShapeDtypeStruct((4, 8), F32),
            jax.ShapeDtypeStruct((8, 2048), F32),
        ),
        in_specs=[
            pl.BlockSpec((CHUNKS, 3, SHARDS // steps, 16, LANES), lambda i: (0, 0, i, 0, 0)),
            fixed(8, LANES),
            fixed(32, LANES),
            fixed(128, LANES),
        ],
        out_specs=(
            pl.BlockSpec((3, 4, 512 // steps, LANES), lambda i: (0, 0, i, 0)),
            fixed(3, 3, 4, 8),
            fixed(4, 8),
            fixed(8, 2048),
        ),
    )(*parts)
    return (d_feat, jnp.transpose(short, (0, 2, 3, 1)), skips, lags)


def solution(mesh):
    placed = (
        P(None, "rep", None, "ctx"),
        P(None, "rep", None, None),
        P("rep", "ctx"),
        P("ctx", None),
        P("rep", None, "ctx"),
    )
    return jax.shard_map(
        per_device,
        mesh=mesh,
        in_specs=placed,
        out_specs=(
            P(None, "rep", None, "ctx"),
            P(None, "rep", "ctx", None),
            P("rep", "ctx"),
            P("ctx", "rep"),
        ),
        check_vma=False,
    )
```

```python
import functools

import jax
import jax.numpy as jnp
from jax import lax
from jax.experimental import pallas as pl
from jax.experimental.pallas import tpu as pltpu
from jax.sharding import PartitionSpec as P

MESH = pl.DeviceIdType.MESH
F32 = jnp.float32
BF16 = jnp.bfloat16

SHARDS = 64
REPS = 4
LANES = 128
CHUNKS = 2
QUAD = 4
GROUP = 8
LAGS = 64
WIDE = 32


def lane_ids():
    return lax.broadcasted_iota(jnp.int32, (8, LANES), 1)


def row_ids():
    return lax.broadcasted_iota(jnp.int32, (8, LANES), 0)


def swap_halves(first, second):
    upper = row_ids() < QUAD
    return (
        jnp.where(upper, first, pltpu.roll(second, QUAD, 0)),
        jnp.where(upper, pltpu.roll(first, QUAD, 0), second),
    )


def flip_matrix():
    rows = lax.broadcasted_iota(jnp.int32, (LANES, LANES), 0)
    cols = lax.broadcasted_iota(jnp.int32, (LANES, LANES), 1)
    return jnp.where(rows + cols == LANES - 1, 1.0, 0.0).astype(BF16)


def ids(rows, cols):
    shape = (rows, cols)
    return (
        lax.broadcasted_iota(jnp.int32, shape, 0),
        lax.broadcasted_iota(jnp.int32, shape, 1),
    )


def ones_where(condition):
    return jnp.where(condition, 1.0, 0.0).astype(BF16)


def product_of(left, right):
    return jnp.dot(left, right, preferred_element_type=F32)


def kernel(
    feat, cot, taps, skip, filt,
    d_out, d_short, d_skip, d_filt,
    d_rows, sig, mixed, wts, tcol, strip, base, front, front_in, before_rows,
    m_early, m_col, m_late, m_first, m_sum,
    send_in, recv_in, send_out, recv_out,
    spread, prod_nat, grad_nat, xs, conv, merged,
    shifted, prod_t, prod_half, cross, low, high, lagrow, lag_send, lag_recv,
    grads, early, back, back_out, back_in, taps_all, tap_send, tap_recv,
    front_sem, in_sem, out_sem, out_recv_sem, back_sem, tap_sem, lag_sem, rows_sem,
):
    me = lax.axis_index("ctx")
    rep = lax.axis_index("rep")
    lane = lane_ids()

    barrier = pltpu.get_barrier_semaphore()

    def greet(k, _):
        pl.semaphore_signal(
            barrier, inc=1, device_id=(lax.rem(me + k, SHARDS), rep), device_id_type=MESH
        )
        return 0

    lax.fori_loop(1, SHARDS, greet, 0)
    for k in range(1, REPS):
        pl.semaphore_signal(
            barrier, inc=1, device_id=(me, lax.rem(rep + k, REPS)), device_id_type=MESH
        )

    zero = jnp.zeros((8, LANES), F32)
    row, col = ids(LANES, LANES)
    last = ones_where(row - (LANES - 2) == col % 2)

    owner = lax.shift_right_logical(ids(16, LANES)[1], 1)

    def pack_front(j, _):
        for gp in range(2):
            tiles = []
            for g in range(2):
                spread_out = product_of(feat[j, 2 * gp + g], last)
                tile = zero
                for shard in range(SHARDS):
                    tile = jnp.where(
                        owner[0:8] == shard, spread_out[8 * shard : 8 * shard + 8], tile
                    )
                tiles.append(tile)
            front[2 * j + gp] = jnp.concatenate(tiles, axis=0).astype(BF16)
        return 0

    lax.fori_loop(0, 3, pack_front, 0)

    @pl.when(me == 0)
    def _():
        front_in[...] = jnp.zeros(front_in.shape, BF16)

    @pl.when(me == SHARDS - 1)
    def _():
        back_in[...] = jnp.zeros(back_in.shape, BF16)

    pl.semaphore_wait(barrier, SHARDS - 1 + REPS - 1)

    def front_copy():
        return pltpu.make_async_remote_copy(
            src_ref=front, dst_ref=front_in, send_sem=front_sem.at[0], recv_sem=front_sem.at[1],
            device_id=(lax.rem(me + 1, SHARDS), rep), device_id_type=MESH,
        )

    @pl.when(me < SHARDS - 1)
    def _():
        front_copy().start()

    def arrange(step, _):
        for half in range(4):
            pair = step * 4 + half
            rows = pl.ds(pl.multiple_of(pair * 16, 16), 16)
            for j in range(4):
                wide = []
                for g in range(4):
                    block = feat[j, g, rows, :] if j < 3 else cot[g, rows, :]
                    wide.append(block.astype(F32))
                for u in range(2):
                    both = [
                        swap_halves(
                            wide[2 * gp][8 * u : 8 * u + 8], wide[2 * gp + 1][8 * u : 8 * u + 8]
                        )
                        for gp in range(2)
                    ]
                    for c in range(CHUNKS):
                        sig[j, c, pair * 2 + u] = jnp.concatenate(
                            [both[0][c], both[1][c]], axis=0
                        ).astype(BF16)
        return 0


    m_early[0:LANES, 0:LANES] = ones_where(col == row + 1)
    m_early[0:LANES, LANES:] = ones_where(col == row + 2)
    m_early[LANES:, 0:LANES] = ones_where((col == 0) & (row % 2 == 1))
    m_early[LANES:, LANES:] = ones_where((col < 2) & (col == row % 2))
    for k in range(9):
        m_col[:, k * LANES : (k + 1) * LANES] = ones_where((row < 27) & (row % 9 == k))

    def eight(ref, *at):
        return ref[at].reshape(8 * 16, LANES)

    def scatter(block, first):
        return jnp.concatenate(
            [jnp.where(owner == first + u, block, 0.0) for u in range(8)], axis=0
        ).astype(BF16)

    def gather(values, first, block):
        for u in range(values.shape[0] // 16):
            block = jnp.where(owner == first + u, values[16 * u : 16 * u + 16], block)
        return block

    for part in range(4):
        cols = slice(part * LANES, (part + 1) * LANES)
        rows = [taps[j, i, g : g + 1, cols] for g in range(4) for j in range(3) for i in range(3)]
        tcol[cols, :] = jnp.concatenate(
            rows + [jnp.zeros((LANES - 36, LANES), F32)], axis=0
        ).T

    def arrange_taps(step, _):
        for u in range(8):
            shard = step * 8 + u
            tile = tcol[pl.ds(pl.multiple_of(shard * 8, 8), 8), :]
            made = ([], [])
            for gp in range(2):
                first = tile if gp == 0 else pltpu.roll(tile, LANES - 18 * gp, 1)
                second = pltpu.roll(tile, LANES - 18 * gp - 9, 1)
                for c, weight in enumerate(swap_halves(first, second)):
                    high_part = weight.astype(BF16).astype(F32)
                    rest = weight - high_part
                    mid_part = rest.astype(BF16).astype(F32)
                    rest = rest - mid_part
                    three = jnp.where(
                        lane < 9,
                        high_part,
                        jnp.where(lane < 18, pltpu.roll(mid_part, 9, 1), pltpu.roll(rest, 18, 1)),
                    )
                    made[c].append(jnp.where(lane < 27, three, 0.0))
            for c in range(CHUNKS):
                wts[c, shard] = jnp.concatenate(made[c], axis=0).astype(BF16)
        return 0


    def in_copy(c, peer):
        return pltpu.make_async_remote_copy(
            src_ref=send_in.at[c, peer], dst_ref=recv_in.at[c, me], send_sem=in_sem.at[0, c],
            recv_sem=in_sem.at[1, c], device_id=(peer, rep), device_id_type=MESH,
        )

    def out_copy(c, peer):
        return pltpu.make_async_remote_copy(
            src_ref=send_out.at[c, peer], dst_ref=recv_out.at[c, me], send_sem=out_sem.at[c],
            recv_sem=out_recv_sem.at[c, me // GROUP], device_id=(peer, rep), device_id_type=MESH,
        )

    def in_copies(c):
        others = pl.ds(0, SHARDS - 1)
        return pltpu.make_async_remote_copy(
            src_ref=send_in.at[c, others], dst_ref=recv_in.at[c, others], send_sem=in_sem.at[0, c],
            recv_sem=in_sem.at[1, c], device_id=(lax.rem(me + 1, SHARDS), rep), device_id_type=MESH,
        )

    def out_copies(c, group, count):
        some = pl.ds(0, count)
        return pltpu.make_async_remote_copy(
            src_ref=send_out.at[c, some], dst_ref=recv_out.at[c, some], send_sem=out_sem.at[c],
            recv_sem=out_recv_sem.at[c, group], device_id=(lax.rem(me + 1, SHARDS), rep),
            device_id_type=MESH,
        )

    def send_results(c):
        def one(k, _):
            out_copy(c, lax.rem(me + k, SHARDS)).start()
            return 0

        lax.fori_loop(1, SHARDS, one, 0)
        recv_out[c, me] = send_out[c, me]

    def short_conv(c, step, _):
        group = lax.rem(me // GROUP + step, SHARDS // GROUP)
        shards = pl.ds(pl.multiple_of(group * GROUP, GROUP), GROUP)
        weight = product_of(eight(wts, c, shards), m_col[...])
        mix = []
        for j in range(3):
            here = eight(sig, j, c, shards)
            before = scatter(before_rows[c, j], group * GROUP)
            moved = product_of(jnp.concatenate([here, before], axis=1), m_early[...])
            for i in range(2):
                early[c, j, i, shards] = (
                    moved[:, i * LANES : (i + 1) * LANES].astype(BF16).reshape(8, 16, LANES)
                )
            three = [weight[:, (3 * j + i) * LANES : (3 * j + i + 1) * LANES] for i in range(3)]
            mix.append(
                three[0] * here.astype(F32)
                + three[1] * moved[:, 0:LANES]
                + three[2] * moved[:, LANES:]
            )
        mixed[0, c, shards] = mix[1].reshape(8, 16, LANES)
        mixed[1, c, shards] = mix[2].reshape(8, 16, LANES)
        send_in[c, shards, 0:16, :] = (mix[1] * mix[2]).astype(BF16).reshape(8, 16, LANES)
        gated = eight(sig, 3, c, shards).astype(F32) * mix[0]
        send_in[c, shards, 16:32, :] = gated.astype(BF16).reshape(8, 16, LANES)
        for u in range(GROUP):
            shard = group * GROUP + lax.rem(me + u, GROUP)

            @pl.when(shard != me)
            def _():
                in_copy(c, shard).start()

        return 0

    @pl.when(me > 0)
    def _():
        front_copy().wait_recv()

    for j in range(3):
        pairs = [front_in[2 * j + gp].astype(F32) for gp in range(2)]
        pairs = [swap_halves(pair[0:8], pair[8:16]) for pair in pairs]
        for c in range(CHUNKS):
            before_rows[c, j] = jnp.concatenate([pairs[0][c], pairs[1][c]], axis=0)

    def first_pass(step, _):
        group = lax.rem(me // GROUP + step, SHARDS // GROUP)
        arrange(group, 0)
        arrange_taps(group, 0)
        return short_conv(0, step, 0)

    lax.fori_loop(0, SHARDS // GROUP, first_pass, 0)
    lax.fori_loop(0, SHARDS // GROUP, functools.partial(short_conv, 1), 0)
    for c in range(CHUNKS):
        recv_in[c, me] = send_in[c, me]

    strip[:, :, 0:LANES] = jnp.zeros((8, LANES, LANES), BF16)
    base[:, 0:LANES] = zero

    def make_strip(f, _):
        row = filt[pl.ds(f, 1), :]
        for part in range(8):
            cols = slice(LANES + part * 1024, LANES + part * 1024 + 1024)
            base[:, cols] = jnp.broadcast_to(row[:, part * 1024 : part * 1024 + 1024], (8, 1024))
        for part in reversed(range(8)):
            wide = base[:, part * 1024 : part * 1024 + 1152]
            base[:, LANES + part * 1024 : LANES + part * 1024 + 1024] = pltpu.roll(
                wide, 0, 1, stride=1, stride_axis=0
            )[:, LANES:]
        for part in range(8):
            wide = base[:, part * 1024 : part * 1024 + 1152]
            for k in range(8):
                upper = wide if k == 0 else pltpu.roll(wide, 16 * k, 1)
                lower = pltpu.roll(wide, 16 * k + 8, 1)
                strip[f, 16 * k : 16 * k + 16, LANES + part * 1024 : LANES + part * 1024 + 1024] = (
                    jnp.concatenate([upper[:, LANES:], lower[:, LANES:]], axis=0).astype(BF16)
                )
        return 0

    lax.fori_loop(0, 8, make_strip, 0)

    m_late[0:LANES, 0:LANES] = ones_where(col == row - 1)
    m_late[0:LANES, LANES:] = ones_where(col == row - 2)
    m_late[LANES:, 0:LANES] = ones_where((col == LANES - 1) & (row % 2 == 0))
    m_late[LANES:, LANES:] = ones_where((col >= LANES - 2) & (col % 2 == row % 2))
    m_first[...] = ones_where(row == col % 2)
    for k in range(9):
        m_sum[k * LANES : (k + 1) * LANES, :] = ones_where(col == k)

    for q in range(QUAD):
        for u in range(2):
            xs[q, u, 0:256, :] = jnp.zeros((256, 256), BF16)
        for e in range(2):
            for k in range(4):
                shifted[q, e, k, 128:256, :] = jnp.zeros((128, LANES), BF16)
        high[q, LAGS] = zero
    for e in range(2):
        grad_nat[e, 512:576, :] = jnp.zeros((64, LANES), F32)

    flip = flip_matrix()
    sign_row = lax.broadcasted_iota(jnp.int32, (8, 256), 0) % 4

    def unpack(c, step, total):
        first = pl.ds(pl.multiple_of(step * WIDE, WIDE), WIDE)
        turned = product_of(recv_in[c, first, 16:32, :].reshape(WIDE * 16, LANES), flip)
        for u in range(WIDE):
            shard = step * WIDE + u
            place = step * (WIDE // 2) + u // 2
            e = u % 2
            product = recv_in[c, shard, 0:16, :].astype(F32)
            gated = recv_in[c, shard, 16:32, :].astype(F32)
            total = total + product * gated
            spread[e, pl.ds(pl.multiple_of(place * 32, 32), 16), :] = product
            prod_nat[e, pl.ds(pl.multiple_of(place * 16, 16), 16), :] = product
            reverse = turned[16 * u : 16 * u + 16]
            mirror = 31 - place
            spread[1 - e, pl.ds(pl.multiple_of(mirror * 32 + 16, 16), 16), :] = reverse
            grad_nat[e, pl.ds(pl.multiple_of(place * 16, 16), 16), :] = reverse
        return total

    def long_conv(c, q, _):
        f = QUAD * c + q
        for group in range(4):
            skip_rows = 64 * group
            acc = jnp.zeros((256 - skip_rows, 256), F32)
            for lag in range(8 * group, 8 * group + 8):
                even = lag - lag % 2
                lhs = xs[q, lag % 2, 256 + skip_rows - 8 * even : 512 - 8 * even, :]
                at = LANES + 256 * lag
                rhs = jnp.concatenate(
                    [strip[f, :, at : at + 256], strip[f, :, at - LANES : at + LANES]], axis=0
                )
                acc = acc + jnp.dot(lhs, rhs, preferred_element_type=F32)
            if group == 0:
                conv[q] = acc
            else:
                conv[q, skip_rows:256, :] += acc
        gain = jnp.where(
            sign_row == 0,
            skip[0, f],
            jnp.where(sign_row == 1, skip[1, f], jnp.where(sign_row == 2, skip[2, f], skip[3, f])),
        )
        for part in range(4):
            rows = slice(64 * part, 64 * part + 64)
            own = xs[q, 0, 256 + 64 * part : 320 + 64 * part, :].astype(F32)
            conv[q, rows, :] += own * jnp.concatenate([gain] * 8, axis=0)
        return 0

    def pack(c, step, _):
        half = WIDE // 2
        rows = pl.ds(pl.multiple_of(step * half * 32, 32), half * 32)
        both = [merged[e, rows, :].astype(BF16).reshape(half, 32, LANES) for e in range(2)]
        turned = product_of(
            jnp.concatenate([b[:, 16:32].reshape(half * 16, LANES) for b in both], axis=0), flip
        ).astype(BF16)
        for u in range(WIDE):
            shard = step * WIDE + u
            at = (u % 2) * half + u // 2
            send_out[c, shard, 0:16, :] = both[u % 2][u // 2, 0:16]
            send_out[c, SHARDS - 1 - shard, 16:32, :] = turned[16 * at : 16 * at + 16]
        return 0

    def owner_conv(c):
        in_copies(c).wait_recv()
        total = lax.fori_loop(0, SHARDS // WIDE, functools.partial(unpack, c), jnp.zeros((16, LANES), F32))
        d_skip[16 * c : 16 * c + 16, :] = jnp.broadcast_to(
            jnp.sum(total, axis=1, keepdims=True), (16, LANES)
        )
        for q in range(QUAD):
            tile = jnp.concatenate(
                [spread[e, pl.ds(q, 256, stride=4), :] for e in range(2)], axis=1
            )
            xs[q, 0, 256:512, :] = tile.astype(BF16)
            xs[q, 1, 256:512, :] = jnp.concatenate(
                [jnp.zeros((8, 256), F32), tile[0:248]], axis=0
            ).astype(BF16)
        lax.fori_loop(0, QUAD, functools.partial(long_conv, c), 0)
        for q in range(QUAD):
            for e in range(2):
                merged[e, pl.ds(q, 256, stride=4), :] = conv[q, :, LANES * e : LANES * e + LANES]
        lax.fori_loop(0, SHARDS // WIDE, functools.partial(pack, c), 0)
        send_results(c)

    def cross_dots(q, m, slot):
        rows = 128 if m < 4 else 64
        left = prod_t if m < 4 else prod_half
        for pair in range(4):
            sides = []
            for odd in range(2):
                parts = []
                for e in range(2):
                    carry = pair + (1 if e == 1 and odd == 1 else 0)
                    at = 16 * m + 16 * (carry // 4)
                    parts.append(shifted[q, (e + odd) % 2, carry % 4, at : at + rows, :])
                sides.append(jnp.concatenate(parts, axis=0))
            cross[slot, pair] = product_of(left[q], jnp.concatenate(sides, axis=1))

    def diagonals(q, m, slot):
        for lag in range(8):
            cols = slice((lag % 2) * LANES, (lag % 2) * LANES + LANES)
            total = cross[slot, lag // 2, 0:8, cols]
            kept = total
            for k in range(1, 16):
                moved = pltpu.roll(cross[slot, lag // 2, 8 * k : 8 * k + 8, cols], 8 * k, 1)
                total = total + moved
                kept = kept + jnp.where(lane >= 8 * k, moved, 0.0)
            low[q, 8 * m + lag] = kept
            high[q, 8 * m + lag] = total - kept

    def owner_lags(c):
        for q in range(QUAD):
            for e in range(2):
                prod_t[q, :, LANES * e : LANES * e + LANES] = (
                    prod_nat[e, pl.ds(q, 128, stride=4), :].T.astype(BF16)
                )
                prod_half[q, :, 64 * e : 64 * e + 64] = (
                    prod_nat[e, pl.ds(q, 64, stride=4), :].T.astype(BF16)
                )
                for k in range(4):
                    shifted[q, e, k, 0:128, :] = grad_nat[
                        e, pl.ds(q + 16 * k, 128, stride=4), :
                    ].astype(BF16)
        cross_dots(0, 0, 0)

        def one_filter(q, _):
            for m in range(8):
                if m < 7:
                    cross_dots(q, m + 1, (m + 1) % 2)
                else:
                    cross_dots(jnp.minimum(q + 1, QUAD - 1), 0, 0)
                diagonals(q, m, m % 2)
            return 0

        lax.fori_loop(0, QUAD, one_filter, 0)

        def turn(step, _):
            q = step // 4
            first = 16 * (step % 4)
            rolled = []
            for k in range(17):
                at = jnp.minimum(first + k, LAGS - 1)
                tile = low[q, at] + high[q, at + 1]
                rolled.append(pltpu.roll(tile, 0, 1, stride=1, stride_axis=0))
            rolled[16] = jnp.where(first == 48, 0.0, rolled[16])
            rows = [
                jnp.sum(jnp.where(lane >= row_ids(), rolled[k], rolled[k + 1]), axis=0, keepdims=True)
                for k in range(16)
            ]
            lagrow[q, step % 4] = jnp.concatenate(rows, axis=0)
            return 0

        lax.fori_loop(0, 16, turn, 0)
        for q in range(QUAD):
            turned = jnp.dot(
                jnp.concatenate([lagrow[q, r] for r in range(4)], axis=0).astype(BF16),
                flip,
                preferred_element_type=F32,
            ).astype(BF16)
            for r in range(REPS):
                lag_send[r, QUAD * c + q] = turned[16 * r : 16 * r + 16]

    owner_conv(0)
    owner_lags(0)
    owner_conv(1)
    owner_lags(1)

    def lag_copy(peer):
        return pltpu.make_async_remote_copy(
            src_ref=lag_send.at[peer], dst_ref=lag_recv.at[rep], send_sem=lag_sem.at[0],
            recv_sem=lag_sem.at[1], device_id=(me, peer), device_id_type=MESH,
        )

    for k in range(1, REPS):
        lag_copy(lax.rem(rep + k, REPS)).start()
    lag_recv[rep] = lag_send[rep]

    def make_grads(c, step, _):
        own = me // GROUP
        pair = lax.rem(own // 2 + GROUP // 2 - 1 - step, GROUP // 2)
        for half in range(2):
            group = 2 * pair + half

            @pl.when(group == own)
            def _():
                out_copies(c, group, GROUP - 1).wait_recv()

            @pl.when(group != own)
            def _():
                out_copies(c, group, GROUP).wait_recv()

        shards = pl.ds(pl.multiple_of(pair * 16, 16), 16)
        value = recv_out[c, shards, 16:32, :].astype(F32)
        three = (
            sig[3, c, shards].astype(F32) * recv_out[c, shards, 0:16, :].astype(F32),
            value * mixed[1, c, shards],
            value * mixed[0, c, shards],
        )
        terms = []
        for j in range(3):
            narrow = three[j].astype(BF16)
            grads[c, j, shards] = narrow
            spread_out = product_of(narrow.reshape(16 * 16, LANES), m_first[...])
            back[c, j] = gather(spread_out, pair * 16, back[c, j])
            terms.append((three[j] * sig[j, c, shards].astype(F32)).astype(BF16))
            for i in range(2):
                terms.append((three[j] * early[c, j, i, shards].astype(F32)).astype(BF16))
        terms = [term.reshape(16 * 16, LANES) for term in terms]
        sums = product_of(jnp.concatenate(terms, axis=1), m_sum[...])
        for u in range(16):
            first = sums[16 * u : 16 * u + 8]
            second = pltpu.roll(sums[16 * u + 8 : 16 * u + 16], 18 * c + 9, 1)
            at = pl.ds(pl.multiple_of((pair * 16 + u) * 8, 8), 8)
            if c == 0:
                taps_all[at, :] = first + second
            else:
                taps_all[at, :] += pltpu.roll(first, 18 * c, 1) + second
        return 0

    def back_copy(c):
        return pltpu.make_async_remote_copy(
            src_ref=back_out.at[c], dst_ref=back_in.at[c], send_sem=back_sem.at[0, c],
            recv_sem=back_sem.at[1, c],
            device_id=(lax.rem(me + SHARDS - 1, SHARDS), rep), device_id_type=MESH,
        )

    def grads_of(c):
        back[c] = jnp.zeros(back.shape[1:], F32)
        lax.fori_loop(0, GROUP // 2, functools.partial(make_grads, c), 0)
        back_out[c] = back[c].astype(BF16)

        @pl.when(me > 0)
        def _():
            back_copy(c).start()

    def short_back(c, step, _):
        shards = pl.ds(pl.multiple_of(step * 8, 8), 8)
        weight = product_of(eight(wts, c, shards), m_col[...])
        for j in range(3):
            here = eight(grads, c, j, shards)
            after = scatter(back_in[c, j].astype(F32), step * 8)
            moved = product_of(jnp.concatenate([here, after], axis=1), m_late[...])
            at = 3 * j * LANES
            total = (
                weight[:, at : at + LANES] * here.astype(F32)
                + weight[:, at + LANES : at + 2 * LANES] * moved[:, 0:LANES]
                + weight[:, at + 2 * LANES : at + 3 * LANES] * moved[:, LANES:]
            )
            d_rows[c, j, shards] = total.astype(BF16).reshape(8, 16, LANES)
        return 0

    def features_of(c):
        @pl.when(me < SHARDS - 1)
        def _():
            back_copy(c).wait_recv()

        lax.fori_loop(0, SHARDS // GROUP, functools.partial(short_back, c), 0)

    def rows_copy(c):
        return pltpu.make_async_copy(d_rows.at[c], d_out.at[c], rows_sem.at[c])

    grads_of(0)
    grads_of(1)

    def tap_copy(peer):
        return pltpu.make_async_remote_copy(
            src_ref=tap_send.at[peer], dst_ref=tap_recv.at[me], send_sem=tap_sem.at[0],
            recv_sem=tap_sem.at[1], device_id=(peer, rep), device_id_type=MESH,
        )

    for m in range(3):
        total = taps_all[pl.ds(3 * m, SHARDS, stride=8), :]
        for n in range(1, 3 if m < 2 else 2):
            total = total + pltpu.roll(taps_all[pl.ds(3 * m + n, SHARDS, stride=8), :], 36 * n, 1)
        tap_send[:, m, :] = total
    tap_send[:, 3, :] = jnp.zeros((SHARDS, LANES), F32)

    def send_taps(k, _):
        tap_copy(lax.rem(me + k, SHARDS)).start()
        return 0

    lax.fori_loop(1, SHARDS, send_taps, 0)
    tap_recv[me] = tap_send[me]

    for c in range(CHUNKS):
        features_of(c)
        rows_copy(c).start()

    lag_all = pltpu.make_async_remote_copy(
        src_ref=lag_send.at[pl.ds(0, REPS - 1)], dst_ref=lag_recv.at[pl.ds(0, REPS - 1)],
        send_sem=lag_sem.at[0], recv_sem=lag_sem.at[1],
        device_id=(me, lax.rem(rep + 1, REPS)), device_id_type=MESH,
    )
    lag_all.wait_recv()
    for f in range(8):
        d_filt[16 * f : 16 * f + 16, :] = (
            lag_recv[0, f].astype(F32)
            + lag_recv[1, f].astype(F32)
            + lag_recv[2, f].astype(F32)
            + lag_recv[3, f].astype(F32)
        )

    others = pl.ds(0, SHARDS - 1)
    tap_all = pltpu.make_async_remote_copy(
        src_ref=tap_send.at[others], dst_ref=tap_recv.at[others], send_sem=tap_sem.at[0],
        recv_sem=tap_sem.at[1], device_id=(lax.rem(me + 1, SHARDS), rep), device_id_type=MESH,
    )
    tap_all.wait_recv()
    d_short[0:4, :] = jnp.sum(tap_recv[...], axis=0)
    d_short[4:8, :] = jnp.zeros((4, LANES), F32)

    for c in range(CHUNKS):
        rows_copy(c).wait()
        in_copies(c).wait_send()
        out_copies(c, 0, SHARDS - 1).wait_send()

        @pl.when(me > 0)
        def _():
            back_copy(c).wait_send()

    lag_all.wait_send()
    tap_all.wait_send()

    @pl.when(me < SHARDS - 1)
    def _():
        front_copy().wait_send()


def finish(d_rows, short, skips, lags, d_feat, d_short, d_skip, d_filt):
    for pair in range(d_rows.shape[2] // 2):
        rows = slice(16 * pair, 16 * pair + 16)
        for j in range(3):
            chunk = [
                [d_rows[c, j, pair * 2 + u].astype(F32) for u in range(2)] for c in range(CHUNKS)
            ]
            for gp in range(2):
                at = slice(8 * gp, 8 * gp + 8)
                tiles = [swap_halves(chunk[0][u][at], chunk[1][u][at]) for u in range(2)]
                for g in range(2):
                    d_feat[j, 2 * gp + g, rows, :] = jnp.concatenate(
                        [tiles[0][g], tiles[1][g]], axis=0
                    ).astype(BF16)

    @pl.when(pl.program_id(0) == 0)
    def _():
        moved = [short[...]] + [pltpu.roll(short[...], LANES - 36 * n, 1) for n in (1, 2)]
        eight_rows = [moved[r % 3][r // 3 : r // 3 + 1] for r in range(8)]
        turned = jnp.concatenate(
            eight_rows + [jnp.zeros((LANES - 8, LANES), F32)], axis=0
        ).T
        wide = lax.broadcasted_iota(jnp.int32, (18, LANES), 1)
        upper, lower = turned[0:18], turned[18:36]
        members = (
            jnp.where(wide < QUAD, upper, pltpu.roll(lower, QUAD, 1)),
            jnp.where(wide < QUAD, pltpu.roll(upper, LANES - QUAD, 1), lower),
        )
        for j in range(3):
            for i in range(3):
                k = 3 * j + i
                four = [members[g % 2][9 * (g // 2) + k : 9 * (g // 2) + k + 1] for g in range(4)]
                d_short[j, i] = jnp.concatenate(four, axis=0)[:, 0:8]
        flat = jnp.concatenate([skips[...], jnp.zeros((LANES - 32, LANES), F32)], axis=0).T[0:8]
        four = []
        for g in range(4):
            first = flat if g == 0 else pltpu.roll(flat, LANES - 4 * g, 1)
            second = pltpu.roll(flat, LANES - 12 - 4 * g, 1)
            four.append(jnp.where(lane_ids() < QUAD, first, second)[0:1])
        d_skip[...] = jnp.concatenate(four, axis=0)[:, 0:8]
        for k in range(16):
            d_filt[:, k * LANES : (k + 1) * LANES] = lags[pl.ds(k, 8, stride=16), :]


def per_device(features, short_taps, skip_gain, filters, cotangent):
    tap_rows = jnp.transpose(short_taps, (0, 3, 1, 2))
    vmem = pl.BlockSpec(memory_space=pltpu.VMEM)
    message = pltpu.VMEM((CHUNKS, SHARDS, 32, LANES), BF16)
    parts = pl.pallas_call(
        kernel,
        out_shape=(
            jax.ShapeDtypeStruct((CHUNKS, 3, SHARDS, 16, LANES), BF16),
            jax.ShapeDtypeStruct((8, LANES), F32),
            jax.ShapeDtypeStruct((32, LANES), F32),
            jax.ShapeDtypeStruct((128, LANES), F32),
        ),
        in_specs=[vmem, vmem, vmem, pl.BlockSpec(memory_space=pltpu.SMEM), vmem],
        out_specs=(pl.BlockSpec(memory_space=pl.ANY), vmem, vmem, vmem),
        scratch_shapes=[
            pltpu.VMEM((CHUNKS, 3, SHARDS, 16, LANES), BF16),
            pltpu.VMEM((4, CHUNKS, SHARDS, 16, LANES), BF16),
            pltpu.VMEM((2, CHUNKS, SHARDS, 16, LANES), F32),
            pltpu.VMEM((CHUNKS, SHARDS, 16, LANES), BF16),
            pltpu.VMEM((512, LANES), F32),
            pltpu.VMEM((8, LANES, LANES + 8192), BF16),
            pltpu.VMEM((8, LANES + 8192), F32),
            pltpu.VMEM((6, 16, LANES), BF16),
            pltpu.VMEM((6, 16, LANES), BF16),
            pltpu.VMEM((CHUNKS, 3, 16, LANES), F32),
            pltpu.VMEM((256, 256), BF16),
            pltpu.VMEM((LANES, 9 * LANES), BF16),
            pltpu.VMEM((256, 256), BF16),
            pltpu.VMEM((LANES, LANES), BF16),
            pltpu.VMEM((9 * LANES, LANES), BF16),
            message, message, message, message,
            pltpu.VMEM((2, 1024, LANES), F32),
            pltpu.VMEM((2, 512, LANES), F32),
            pltpu.VMEM((2, 576, LANES), F32),
            pltpu.VMEM((QUAD, 2, 512, 256), BF16),
            pltpu.VMEM((QUAD, 256, 256), F32),
            pltpu.VMEM((2, 1024, LANES), F32),
            pltpu.VMEM((QUAD, 2, 4, 256, LANES), BF16),
            pltpu.VMEM((QUAD, LANES, 256), BF16),
            pltpu.VMEM((QUAD, LANES, LANES), BF16),
            pltpu.VMEM((2, 4, LANES, 256), F32),
            pltpu.VMEM((QUAD, LAGS, 8, LANES), F32),
            pltpu.VMEM((QUAD, LAGS + 1, 8, LANES), F32),
            pltpu.VMEM((QUAD, 4, 16, LANES), F32),
            pltpu.VMEM((REPS, 8, 16, LANES), BF16),
            pltpu.VMEM((REPS, 8, 16, LANES), BF16),
            pltpu.VMEM((CHUNKS, 3, SHARDS, 16, LANES), BF16),
            pltpu.VMEM((CHUNKS, 3, 2, SHARDS, 16, LANES), BF16),
            pltpu.VMEM((CHUNKS, 3, 16, LANES), F32),
            pltpu.VMEM((CHUNKS, 3, 16, LANES), BF16),
            pltpu.VMEM((CHUNKS, 3, 16, LANES), BF16),
            pltpu.VMEM((SHARDS * 8, LANES), F32),
            pltpu.VMEM((SHARDS, 4, LANES), F32),
            pltpu.VMEM((SHARDS, 4, LANES), F32),
            pltpu.SemaphoreType.DMA((2,)),
            pltpu.SemaphoreType.DMA((2, CHUNKS)),
            pltpu.SemaphoreType.DMA((CHUNKS,)),
            pltpu.SemaphoreType.DMA((CHUNKS, GROUP)),
            pltpu.SemaphoreType.DMA((2, CHUNKS)),
            pltpu.SemaphoreType.DMA((2,)),
            pltpu.SemaphoreType.DMA((2,)),
            pltpu.SemaphoreType.DMA((CHUNKS,)),
        ],
        compiler_params=pltpu.CompilerParams(
            collective_id=0, has_side_effects=True, vmem_limit_bytes=60 * 2**20
        ),
    )(features, cotangent, tap_rows, skip_gain, filters)
    steps = 2
    fixed = lambda *shape: pl.BlockSpec(shape, lambda i: (0,) * len(shape))
    d_feat, short, skips, lags = pl.pallas_call(
        finish,
        grid=(steps,),
        out_shape=(
            jax.ShapeDtypeStruct((3, 4, 512, LANES), BF16),
            jax.ShapeDtypeStruct((3, 3, 4, 8), F32),
            jax.ShapeDtypeStruct((4, 8), F32),
            jax.ShapeDtypeStruct((8, 2048), F32),
        ),
        in_specs=[
            pl.BlockSpec((CHUNKS, 3, SHARDS // steps, 16, LANES), lambda i: (0, 0, i, 0, 0)),
            fixed(8, LANES),
            fixed(32, LANES),
            fixed(128, LANES),
        ],
        out_specs=(
            pl.BlockSpec((3, 4, 512 // steps, LANES), lambda i: (0, 0, i, 0)),
            fixed(3, 3, 4, 8),
            fixed(4, 8),
            fixed(8, 2048),
        ),
    )(*parts)
    return (d_feat, jnp.transpose(short, (0, 2, 3, 1)), skips, lags)


def solution(mesh):
    placed = (
        P(None, "rep", None, "ctx"),
        P(None, "rep", None, None),
        P("rep", "ctx"),
        P("ctx", None),
        P("rep", None, "ctx"),
    )
    return jax.shard_map(
        per_device,
        mesh=mesh,
        in_specs=placed,
        out_specs=(
            P(None, "rep", None, "ctx"),
            P(None, "rep", "ctx", None),
            P("rep", "ctx"),
            P("ctx", "rep"),
        ),
        check_vma=False,
    )
```

```python
import functools

import jax
import jax.numpy as jnp
from jax import lax
from jax.experimental import pallas as pl
from jax.experimental.pallas import tpu as pltpu
from jax.sharding import PartitionSpec as P

MESH = pl.DeviceIdType.MESH
F32 = jnp.float32
BF16 = jnp.bfloat16

SHARDS = 64
REPS = 4
LANES = 128
CHUNKS = 2
QUAD = 4
GROUP = 8
LAGS = 64
WIDE = 32


def lane_ids():
    return lax.broadcasted_iota(jnp.int32, (8, LANES), 1)


def row_ids():
    return lax.broadcasted_iota(jnp.int32, (8, LANES), 0)


def swap_halves(first, second):
    upper = row_ids() < QUAD
    return (
        jnp.where(upper, first, pltpu.roll(second, QUAD, 0)),
        jnp.where(upper, pltpu.roll(first, QUAD, 0), second),
    )


def flip_matrix():
    rows = lax.broadcasted_iota(jnp.int32, (LANES, LANES), 0)
    cols = lax.broadcasted_iota(jnp.int32, (LANES, LANES), 1)
    return jnp.where(rows + cols == LANES - 1, 1.0, 0.0).astype(BF16)


def ids(rows, cols):
    shape = (rows, cols)
    return (
        lax.broadcasted_iota(jnp.int32, shape, 0),
        lax.broadcasted_iota(jnp.int32, shape, 1),
    )


def ones_where(condition):
    return jnp.where(condition, 1.0, 0.0).astype(BF16)


def product_of(left, right):
    return jnp.dot(left, right, preferred_element_type=F32)


def kernel(
    feat, cot, taps, skip, filt,
    d_out, d_short, d_skip, d_filt,
    d_rows, sig, mixed, wts, tcol, strip, base, front, front_in, before_rows,
    m_early, m_col, m_late, m_first, m_sum,
    send_in, recv_in, send_out, recv_out,
    spread, prod_nat, grad_nat, xs, conv, merged,
    shifted, prod_t, prod_half, cross, low, high, lagrow, lag_send, lag_recv,
    grads, early, back, back_out, back_in, taps_all, tap_send, tap_recv,
    front_sem, in_sem, out_sem, out_recv_sem, back_sem, tap_sem, lag_sem, rows_sem,
):
    me = lax.axis_index("ctx")
    rep = lax.axis_index("rep")
    lane = lane_ids()

    barrier = pltpu.get_barrier_semaphore()

    def greet(k, _):
        pl.semaphore_signal(
            barrier, inc=1, device_id=(lax.rem(me + k, SHARDS), rep), device_id_type=MESH
        )
        return 0

    lax.fori_loop(1, SHARDS, greet, 0)
    for k in range(1, REPS):
        pl.semaphore_signal(
            barrier, inc=1, device_id=(me, lax.rem(rep + k, REPS)), device_id_type=MESH
        )

    zero = jnp.zeros((8, LANES), F32)
    row, col = ids(LANES, LANES)
    last = ones_where(row - (LANES - 2) == col % 2)

    owner = lax.shift_right_logical(ids(16, LANES)[1], 1)

    def pack_front(j, _):
        for gp in range(2):
            tiles = []
            for g in range(2):
                spread_out = product_of(feat[j, 2 * gp + g], last)
                tile = zero
                for shard in range(SHARDS):
                    tile = jnp.where(
                        owner[0:8] == shard, spread_out[8 * shard : 8 * shard + 8], tile
                    )
                tiles.append(tile)
            front[2 * j + gp] = jnp.concatenate(tiles, axis=0).astype(BF16)
        return 0

    lax.fori_loop(0, 3, pack_front, 0)

    @pl.when(me == 0)
    def _():
        front_in[...] = jnp.zeros(front_in.shape, BF16)

    @pl.when(me == SHARDS - 1)
    def _():
        back_in[...] = jnp.zeros(back_in.shape, BF16)

    pl.semaphore_wait(barrier, SHARDS - 1 + REPS - 1)

    def front_copy():
        return pltpu.make_async_remote_copy(
            src_ref=front, dst_ref=front_in, send_sem=front_sem.at[0], recv_sem=front_sem.at[1],
            device_id=(lax.rem(me + 1, SHARDS), rep), device_id_type=MESH,
        )

    @pl.when(me < SHARDS - 1)
    def _():
        front_copy().start()

    def arrange(step, _):
        for half in range(4):
            pair = step * 4 + half
            rows = pl.ds(pl.multiple_of(pair * 16, 16), 16)
            for j in range(4):
                wide = []
                for g in range(4):
                    block = feat[j, g, rows, :] if j < 3 else cot[g, rows, :]
                    wide.append(block.astype(F32))
                for u in range(2):
                    both = [
                        swap_halves(
                            wide[2 * gp][8 * u : 8 * u + 8], wide[2 * gp + 1][8 * u : 8 * u + 8]
                        )
                        for gp in range(2)
                    ]
                    for c in range(CHUNKS):
                        sig[j, c, pair * 2 + u] = jnp.concatenate(
                            [both[0][c], both[1][c]], axis=0
                        ).astype(BF16)
        return 0


    m_early[0:LANES, 0:LANES] = ones_where(col == row + 1)
    m_early[0:LANES, LANES:] = ones_where(col == row + 2)
    m_early[LANES:, 0:LANES] = ones_where((col == 0) & (row % 2 == 1))
    m_early[LANES:, LANES:] = ones_where((col < 2) & (col == row % 2))
    for k in range(9):
        m_col[:, k * LANES : (k + 1) * LANES] = ones_where((row < 27) & (row % 9 == k))

    def eight(ref, *at):
        return ref[at].reshape(8 * 16, LANES)

    def scatter(block, first):
        return jnp.concatenate(
            [jnp.where(owner == first + u, block, 0.0) for u in range(8)], axis=0
        ).astype(BF16)

    def gather(values, first, block):
        for u in range(values.shape[0] // 16):
            block = jnp.where(owner == first + u, values[16 * u : 16 * u + 16], block)
        return block

    for part in range(4):
        cols = slice(part * LANES, (part + 1) * LANES)
        rows = [taps[j, i, g : g + 1, cols] for g in range(4) for j in range(3) for i in range(3)]
        tcol[cols, :] = jnp.concatenate(
            rows + [jnp.zeros((LANES - 36, LANES), F32)], axis=0
        ).T

    def arrange_taps(step, _):
        for u in range(8):
            shard = step * 8 + u
            tile = tcol[pl.ds(pl.multiple_of(shard * 8, 8), 8), :]
            made = ([], [])
            for gp in range(2):
                first = tile if gp == 0 else pltpu.roll(tile, LANES - 18 * gp, 1)
                second = pltpu.roll(tile, LANES - 18 * gp - 9, 1)
                for c, weight in enumerate(swap_halves(first, second)):
                    high_part = weight.astype(BF16).astype(F32)
                    rest = weight - high_part
                    mid_part = rest.astype(BF16).astype(F32)
                    rest = rest - mid_part
                    three = jnp.where(
                        lane < 9,
                        high_part,
                        jnp.where(lane < 18, pltpu.roll(mid_part, 9, 1), pltpu.roll(rest, 18, 1)),
                    )
                    made[c].append(jnp.where(lane < 27, three, 0.0))
            for c in range(CHUNKS):
                wts[c, shard] = jnp.concatenate(made[c], axis=0).astype(BF16)
        return 0


    def in_copy(c, peer):
        return pltpu.make_async_remote_copy(
            src_ref=send_in.at[c, peer], dst_ref=recv_in.at[c, me], send_sem=in_sem.at[0, c],
            recv_sem=in_sem.at[1, c], device_id=(peer, rep), device_id_type=MESH,
        )

    def out_copy(c, peer):
        return pltpu.make_async_remote_copy(
            src_ref=send_out.at[c, peer], dst_ref=recv_out.at[c, me], send_sem=out_sem.at[c],
            recv_sem=out_recv_sem.at[c, me // GROUP], device_id=(peer, rep), device_id_type=MESH,
        )

    def in_copies(c):
        others = pl.ds(0, SHARDS - 1)
        return pltpu.make_async_remote_copy(
            src_ref=send_in.at[c, others], dst_ref=recv_in.at[c, others], send_sem=in_sem.at[0, c],
            recv_sem=in_sem.at[1, c], device_id=(lax.rem(me + 1, SHARDS), rep), device_id_type=MESH,
        )

    def out_copies(c, group, count):
        some = pl.ds(0, count)
        return pltpu.make_async_remote_copy(
            src_ref=send_out.at[c, some], dst_ref=recv_out.at[c, some], send_sem=out_sem.at[c],
            recv_sem=out_recv_sem.at[c, group], device_id=(lax.rem(me + 1, SHARDS), rep),
            device_id_type=MESH,
        )

    def send_results(c):
        def one(k, _):
            out_copy(c, lax.rem(me + k, SHARDS)).start()
            return 0

        lax.fori_loop(1, SHARDS, one, 0)
        recv_out[c, me] = send_out[c, me]

    def short_conv(c, step, _):
        group = lax.rem(me // GROUP + step, SHARDS // GROUP)
        shards = pl.ds(pl.multiple_of(group * GROUP, GROUP), GROUP)
        weight = product_of(eight(wts, c, shards), m_col[...])
        mix = []
        for j in range(3):
            here = eight(sig, j, c, shards)
            before = scatter(before_rows[c, j], group * GROUP)
            moved = product_of(jnp.concatenate([here, before], axis=1), m_early[...])
            for i in range(2):
                early[c, j, i, shards] = (
                    moved[:, i * LANES : (i + 1) * LANES].astype(BF16).reshape(8, 16, LANES)
                )
            three = [weight[:, (3 * j + i) * LANES : (3 * j + i + 1) * LANES] for i in range(3)]
            mix.append(
                three[0] * here.astype(F32)
                + three[1] * moved[:, 0:LANES]
                + three[2] * moved[:, LANES:]
            )
        mixed[0, c, shards] = mix[1].reshape(8, 16, LANES)
        mixed[1, c, shards] = mix[2].reshape(8, 16, LANES)
        send_in[c, shards, 0:16, :] = (mix[1] * mix[2]).astype(BF16).reshape(8, 16, LANES)
        gated = eight(sig, 3, c, shards).astype(F32) * mix[0]
        send_in[c, shards, 16:32, :] = gated.astype(BF16).reshape(8, 16, LANES)
        for u in range(GROUP):
            shard = group * GROUP + lax.rem(me + u, GROUP)

            @pl.when(shard != me)
            def _():
                in_copy(c, shard).start()

        return 0

    @pl.when(me > 0)
    def _():
        front_copy().wait_recv()

    for j in range(3):
        pairs = [front_in[2 * j + gp].astype(F32) for gp in range(2)]
        pairs = [swap_halves(pair[0:8], pair[8:16]) for pair in pairs]
        for c in range(CHUNKS):
            before_rows[c, j] = jnp.concatenate([pairs[0][c], pairs[1][c]], axis=0)

    def first_pass(step, _):
        group = lax.rem(me // GROUP + step, SHARDS // GROUP)
        arrange(group, 0)
        arrange_taps(group, 0)
        return short_conv(0, step, 0)

    lax.fori_loop(0, SHARDS // GROUP, first_pass, 0)
    lax.fori_loop(0, SHARDS // GROUP, functools.partial(short_conv, 1), 0)
    for c in range(CHUNKS):
        recv_in[c, me] = send_in[c, me]

    strip[:, :, 0:LANES] = jnp.zeros((8, LANES, LANES), BF16)
    base[:, 0:LANES] = zero

    def make_strip(f, _):
        row = filt[pl.ds(f, 1), :]
        for part in range(8):
            cols = slice(LANES + part * 1024, LANES + part * 1024 + 1024)
            base[:, cols] = jnp.broadcast_to(row[:, part * 1024 : part * 1024 + 1024], (8, 1024))
        for part in reversed(range(8)):
            wide = base[:, part * 1024 : part * 1024 + 1152]
            base[:, LANES + part * 1024 : LANES + part * 1024 + 1024] = pltpu.roll(
                wide, 0, 1, stride=1, stride_axis=0
            )[:, LANES:]
        for part in range(8):
            wide = base[:, part * 1024 : part * 1024 + 1152]
            for k in range(8):
                upper = wide if k == 0 else pltpu.roll(wide, 16 * k, 1)
                lower = pltpu.roll(wide, 16 * k + 8, 1)
                strip[f, 16 * k : 16 * k + 16, LANES + part * 1024 : LANES + part * 1024 + 1024] = (
                    jnp.concatenate([upper[:, LANES:], lower[:, LANES:]], axis=0).astype(BF16)
                )
        return 0

    lax.fori_loop(0, 8, make_strip, 0)

    m_late[0:LANES, 0:LANES] = ones_where(col == row - 1)
    m_late[0:LANES, LANES:] = ones_where(col == row - 2)
    m_late[LANES:, 0:LANES] = ones_where((col == LANES - 1) & (row % 2 == 0))
    m_late[LANES:, LANES:] = ones_where((col >= LANES - 2) & (col % 2 == row % 2))
    m_first[...] = ones_where(row == col % 2)
    for k in range(9):
        m_sum[k * LANES : (k + 1) * LANES, :] = ones_where(col == k)

    for q in range(QUAD):
        for u in range(2):
            xs[q, u, 0:256, :] = jnp.zeros((256, 256), BF16)
        for e in range(2):
            for k in range(4):
                shifted[q, e, k, 128:256, :] = jnp.zeros((128, LANES), BF16)
        high[q, LAGS] = zero
    for e in range(2):
        grad_nat[e, 512:576, :] = jnp.zeros((64, LANES), F32)

    flip = flip_matrix()
    sign_row = lax.broadcasted_iota(jnp.int32, (8, 256), 0) % 4

    def unpack(c, step, total):
        first = pl.ds(pl.multiple_of(step * WIDE, WIDE), WIDE)
        turned = product_of(recv_in[c, first, 16:32, :].reshape(WIDE * 16, LANES), flip)
        for u in range(WIDE):
            shard = step * WIDE + u
            place = step * (WIDE // 2) + u // 2
            e = u % 2
            product = recv_in[c, shard, 0:16, :].astype(F32)
            gated = recv_in[c, shard, 16:32, :].astype(F32)
            total = total + product * gated
            spread[e, pl.ds(pl.multiple_of(place * 32, 32), 16), :] = product
            prod_nat[e, pl.ds(pl.multiple_of(place * 16, 16), 16), :] = product
            reverse = turned[16 * u : 16 * u + 16]
            mirror = 31 - place
            spread[1 - e, pl.ds(pl.multiple_of(mirror * 32 + 16, 16), 16), :] = reverse
            grad_nat[e, pl.ds(pl.multiple_of(place * 16, 16), 16), :] = reverse
        return total

    def long_conv(c, q, _):
        f = QUAD * c + q
        for group in range(4):
            skip_rows = 64 * group
            acc = jnp.zeros((256 - skip_rows, 256), F32)
            for lag in range(8 * group, 8 * group + 8):
                even = lag - lag % 2
                lhs = xs[q, lag % 2, 256 + skip_rows - 8 * even : 512 - 8 * even, :]
                at = LANES + 256 * lag
                rhs = jnp.concatenate(
                    [strip[f, :, at : at + 256], strip[f, :, at - LANES : at + LANES]], axis=0
                )
                acc = acc + jnp.dot(lhs, rhs, preferred_element_type=F32)
            if group == 0:
                conv[q] = acc
            else:
                conv[q, skip_rows:256, :] += acc
        gain = jnp.where(
            sign_row == 0,
            skip[0, f],
            jnp.where(sign_row == 1, skip[1, f], jnp.where(sign_row == 2, skip[2, f], skip[3, f])),
        )
        for part in range(4):
            rows = slice(64 * part, 64 * part + 64)
            own = xs[q, 0, 256 + 64 * part : 320 + 64 * part, :].astype(F32)
            conv[q, rows, :] += own * jnp.concatenate([gain] * 8, axis=0)
        return 0

    def pack(c, step, _):
        half = WIDE // 2
        rows = pl.ds(pl.multiple_of(step * half * 32, 32), half * 32)
        both = [merged[e, rows, :].astype(BF16).reshape(half, 32, LANES) for e in range(2)]
        turned = product_of(
            jnp.concatenate([b[:, 16:32].reshape(half * 16, LANES) for b in both], axis=0), flip
        ).astype(BF16)
        for u in range(WIDE):
            shard = step * WIDE + u
            at = (u % 2) * half + u // 2
            send_out[c, shard, 0:16, :] = both[u % 2][u // 2, 0:16]
            send_out[c, SHARDS - 1 - shard, 16:32, :] = turned[16 * at : 16 * at + 16]
        return 0

    def owner_conv(c):
        in_copies(c).wait_recv()
        total = lax.fori_loop(0, SHARDS // WIDE, functools.partial(unpack, c), jnp.zeros((16, LANES), F32))
        d_skip[16 * c : 16 * c + 16, :] = jnp.broadcast_to(
            jnp.sum(total, axis=1, keepdims=True), (16, LANES)
        )
        for q in range(QUAD):
            tile = jnp.concatenate(
                [spread[e, pl.ds(q, 256, stride=4), :] for e in range(2)], axis=1
            )
            xs[q, 0, 256:512, :] = tile.astype(BF16)
            xs[q, 1, 256:512, :] = jnp.concatenate(
                [jnp.zeros((8, 256), F32), tile[0:248]], axis=0
            ).astype(BF16)
        lax.fori_loop(0, QUAD, functools.partial(long_conv, c), 0)
        for q in range(QUAD):
            for e in range(2):
                merged[e, pl.ds(q, 256, stride=4), :] = conv[q, :, LANES * e : LANES * e + LANES]
        lax.fori_loop(0, SHARDS // WIDE, functools.partial(pack, c), 0)
        send_results(c)

    def cross_dots(q, m, slot):
        rows = 128 if m < 4 else 64
        left = prod_t if m < 4 else prod_half
        for pair in range(4):
            sides = []
            for odd in range(2):
                parts = []
                for e in range(2):
                    carry = pair + (1 if e == 1 and odd == 1 else 0)
                    at = 16 * m + 16 * (carry // 4)
                    parts.append(shifted[q, (e + odd) % 2, carry % 4, at : at + rows, :])
                sides.append(jnp.concatenate(parts, axis=0))
            cross[slot, pair] = product_of(left[q], jnp.concatenate(sides, axis=1))

    def diagonals(q, m, slot):
        for lag in range(8):
            cols = slice((lag % 2) * LANES, (lag % 2) * LANES + LANES)
            total = cross[slot, lag // 2, 0:8, cols]
            kept = total
            for k in range(1, 16):
                moved = pltpu.roll(cross[slot, lag // 2, 8 * k : 8 * k + 8, cols], 8 * k, 1)
                total = total + moved
                kept = kept + jnp.where(lane >= 8 * k, moved, 0.0)
            low[q, 8 * m + lag] = kept
            high[q, 8 * m + lag] = total - kept

    def lag_blocks(c):
        for q in range(QUAD):
            for e in range(2):
                prod_t[q, :, LANES * e : LANES * e + LANES] = (
                    prod_nat[e, pl.ds(q, 128, stride=4), :].T.astype(BF16)
                )
                prod_half[q, :, 64 * e : 64 * e + 64] = (
                    prod_nat[e, pl.ds(q, 64, stride=4), :].T.astype(BF16)
                )
                for k in range(4):
                    shifted[q, e, k, 0:128, :] = grad_nat[
                        e, pl.ds(q + 16 * k, 128, stride=4), :
                    ].astype(BF16)

    def owner_lags(c):
        cross_dots(0, 0, 0)

        def one_filter(q, _):
            for m in range(8):
                if m < 7:
                    cross_dots(q, m + 1, (m + 1) % 2)
                else:
                    cross_dots(jnp.minimum(q + 1, QUAD - 1), 0, 0)
                diagonals(q, m, m % 2)
            return 0

        lax.fori_loop(0, QUAD, one_filter, 0)

        def turn(step, _):
            q = step // 4
            first = 16 * (step % 4)
            rolled = []
            for k in range(17):
                at = jnp.minimum(first + k, LAGS - 1)
                tile = low[q, at] + high[q, at + 1]
                rolled.append(pltpu.roll(tile, 0, 1, stride=1, stride_axis=0))
            rolled[16] = jnp.where(first == 48, 0.0, rolled[16])
            rows = [
                jnp.sum(jnp.where(lane >= row_ids(), rolled[k], rolled[k + 1]), axis=0, keepdims=True)
                for k in range(16)
            ]
            lagrow[q, step % 4] = jnp.concatenate(rows, axis=0)
            return 0

        lax.fori_loop(0, 16, turn, 0)
        for q in range(QUAD):
            turned = jnp.dot(
                jnp.concatenate([lagrow[q, r] for r in range(4)], axis=0).astype(BF16),
                flip,
                preferred_element_type=F32,
            ).astype(BF16)
            for r in range(REPS):
                lag_send[r, QUAD * c + q] = turned[16 * r : 16 * r + 16]

    owner_conv(0)
    lag_blocks(0)
    owner_conv(1)
    owner_lags(0)
    lag_blocks(1)
    owner_lags(1)

    def lag_copy(peer):
        return pltpu.make_async_remote_copy(
            src_ref=lag_send.at[peer], dst_ref=lag_recv.at[rep], send_sem=lag_sem.at[0],
            recv_sem=lag_sem.at[1], device_id=(me, peer), device_id_type=MESH,
        )

    for k in range(1, REPS):
        lag_copy(lax.rem(rep + k, REPS)).start()
    lag_recv[rep] = lag_send[rep]

    def make_grads(c, step, _):
        own = me // GROUP
        pair = lax.rem(own // 2 + GROUP // 2 - 1 - step, GROUP // 2)
        for half in range(2):
            group = 2 * pair + half

            @pl.when(group == own)
            def _():
                out_copies(c, group, GROUP - 1).wait_recv()

            @pl.when(group != own)
            def _():
                out_copies(c, group, GROUP).wait_recv()

        shards = pl.ds(pl.multiple_of(pair * 16, 16), 16)
        value = recv_out[c, shards, 16:32, :].astype(F32)
        three = (
            sig[3, c, shards].astype(F32) * recv_out[c, shards, 0:16, :].astype(F32),
            value * mixed[1, c, shards],
            value * mixed[0, c, shards],
        )
        terms = []
        for j in range(3):
            narrow = three[j].astype(BF16)
            grads[c, j, shards] = narrow
            spread_out = product_of(narrow.reshape(16 * 16, LANES), m_first[...])
            back[c, j] = gather(spread_out, pair * 16, back[c, j])
            terms.append((three[j] * sig[j, c, shards].astype(F32)).astype(BF16))
            for i in range(2):
                terms.append((three[j] * early[c, j, i, shards].astype(F32)).astype(BF16))
        terms = [term.reshape(16 * 16, LANES) for term in terms]
        sums = product_of(jnp.concatenate(terms, axis=1), m_sum[...])
        for u in range(16):
            first = sums[16 * u : 16 * u + 8]
            second = pltpu.roll(sums[16 * u + 8 : 16 * u + 16], 18 * c + 9, 1)
            at = pl.ds(pl.multiple_of((pair * 16 + u) * 8, 8), 8)
            if c == 0:
                taps_all[at, :] = first + second
            else:
                taps_all[at, :] += pltpu.roll(first, 18 * c, 1) + second
        return 0

    def back_copy(c):
        return pltpu.make_async_remote_copy(
            src_ref=back_out.at[c], dst_ref=back_in.at[c], send_sem=back_sem.at[0, c],
            recv_sem=back_sem.at[1, c],
            device_id=(lax.rem(me + SHARDS - 1, SHARDS), rep), device_id_type=MESH,
        )

    def grads_of(c):
        back[c] = jnp.zeros(back.shape[1:], F32)
        lax.fori_loop(0, GROUP // 2, functools.partial(make_grads, c), 0)
        back_out[c] = back[c].astype(BF16)

        @pl.when(me > 0)
        def _():
            back_copy(c).start()

    def short_back(c, step, _):
        shards = pl.ds(pl.multiple_of(step * 8, 8), 8)
        weight = product_of(eight(wts, c, shards), m_col[...])
        for j in range(3):
            here = eight(grads, c, j, shards)
            after = scatter(back_in[c, j].astype(F32), step * 8)
            moved = product_of(jnp.concatenate([here, after], axis=1), m_late[...])
            at = 3 * j * LANES
            total = (
                weight[:, at : at + LANES] * here.astype(F32)
                + weight[:, at + LANES : at + 2 * LANES] * moved[:, 0:LANES]
                + weight[:, at + 2 * LANES : at + 3 * LANES] * moved[:, LANES:]
            )
            d_rows[c, j, shards] = total.astype(BF16).reshape(8, 16, LANES)
        return 0

    def features_of(c):
        @pl.when(me < SHARDS - 1)
        def _():
            back_copy(c).wait_recv()

        lax.fori_loop(0, SHARDS // GROUP, functools.partial(short_back, c), 0)

    def rows_copy(c):
        return pltpu.make_async_copy(d_rows.at[c], d_out.at[c], rows_sem.at[c])

    grads_of(0)
    grads_of(1)

    def tap_copy(peer):
        return pltpu.make_async_remote_copy(
            src_ref=tap_send.at[peer], dst_ref=tap_recv.at[me], send_sem=tap_sem.at[0],
            recv_sem=tap_sem.at[1], device_id=(peer, rep), device_id_type=MESH,
        )

    for m in range(3):
        total = taps_all[pl.ds(3 * m, SHARDS, stride=8), :]
        for n in range(1, 3 if m < 2 else 2):
            total = total + pltpu.roll(taps_all[pl.ds(3 * m + n, SHARDS, stride=8), :], 36 * n, 1)
        tap_send[:, m, :] = total
    tap_send[:, 3, :] = jnp.zeros((SHARDS, LANES), F32)

    def send_taps(k, _):
        tap_copy(lax.rem(me + k, SHARDS)).start()
        return 0

    lax.fori_loop(1, SHARDS, send_taps, 0)
    tap_recv[me] = tap_send[me]

    for c in range(CHUNKS):
        features_of(c)
        rows_copy(c).start()

    lag_all = pltpu.make_async_remote_copy(
        src_ref=lag_send.at[pl.ds(0, REPS - 1)], dst_ref=lag_recv.at[pl.ds(0, REPS - 1)],
        send_sem=lag_sem.at[0], recv_sem=lag_sem.at[1],
        device_id=(me, lax.rem(rep + 1, REPS)), device_id_type=MESH,
    )
    lag_all.wait_recv()
    for f in range(8):
        d_filt[16 * f : 16 * f + 16, :] = (
            lag_recv[0, f].astype(F32)
            + lag_recv[1, f].astype(F32)
            + lag_recv[2, f].astype(F32)
            + lag_recv[3, f].astype(F32)
        )

    others = pl.ds(0, SHARDS - 1)
    tap_all = pltpu.make_async_remote_copy(
        src_ref=tap_send.at[others], dst_ref=tap_recv.at[others], send_sem=tap_sem.at[0],
        recv_sem=tap_sem.at[1], device_id=(lax.rem(me + 1, SHARDS), rep), device_id_type=MESH,
    )
    tap_all.wait_recv()
    d_short[0:4, :] = jnp.sum(tap_recv[...], axis=0)
    d_short[4:8, :] = jnp.zeros((4, LANES), F32)

    for c in range(CHUNKS):
        rows_copy(c).wait()
        in_copies(c).wait_send()
        out_copies(c, 0, SHARDS - 1).wait_send()

        @pl.when(me > 0)
        def _():
            back_copy(c).wait_send()

    lag_all.wait_send()
    tap_all.wait_send()

    @pl.when(me < SHARDS - 1)
    def _():
        front_copy().wait_send()


def finish(d_rows, short, skips, lags, d_feat, d_short, d_skip, d_filt):
    for pair in range(d_rows.shape[2] // 2):
        rows = slice(16 * pair, 16 * pair + 16)
        for j in range(3):
            chunk = [
                [d_rows[c, j, pair * 2 + u].astype(F32) for u in range(2)] for c in range(CHUNKS)
            ]
            for gp in range(2):
                at = slice(8 * gp, 8 * gp + 8)
                tiles = [swap_halves(chunk[0][u][at], chunk[1][u][at]) for u in range(2)]
                for g in range(2):
                    d_feat[j, 2 * gp + g, rows, :] = jnp.concatenate(
                        [tiles[0][g], tiles[1][g]], axis=0
                    ).astype(BF16)

    @pl.when(pl.program_id(0) == 0)
    def _():
        moved = [short[...]] + [pltpu.roll(short[...], LANES - 36 * n, 1) for n in (1, 2)]
        eight_rows = [moved[r % 3][r // 3 : r // 3 + 1] for r in range(8)]
        turned = jnp.concatenate(
            eight_rows + [jnp.zeros((LANES - 8, LANES), F32)], axis=0
        ).T
        wide = lax.broadcasted_iota(jnp.int32, (18, LANES), 1)
        upper, lower = turned[0:18], turned[18:36]
        members = (
            jnp.where(wide < QUAD, upper, pltpu.roll(lower, QUAD, 1)),
            jnp.where(wide < QUAD, pltpu.roll(upper, LANES - QUAD, 1), lower),
        )
        for j in range(3):
            for i in range(3):
                k = 3 * j + i
                four = [members[g % 2][9 * (g // 2) + k : 9 * (g // 2) + k + 1] for g in range(4)]
                d_short[j, i] = jnp.concatenate(four, axis=0)[:, 0:8]
        flat = jnp.concatenate([skips[...], jnp.zeros((LANES - 32, LANES), F32)], axis=0).T[0:8]
        four = []
        for g in range(4):
            first = flat if g == 0 else pltpu.roll(flat, LANES - 4 * g, 1)
            second = pltpu.roll(flat, LANES - 12 - 4 * g, 1)
            four.append(jnp.where(lane_ids() < QUAD, first, second)[0:1])
        d_skip[...] = jnp.concatenate(four, axis=0)[:, 0:8]
        for k in range(16):
            d_filt[:, k * LANES : (k + 1) * LANES] = lags[pl.ds(k, 8, stride=16), :]


def per_device(features, short_taps, skip_gain, filters, cotangent):
    tap_rows = jnp.transpose(short_taps, (0, 3, 1, 2))
    vmem = pl.BlockSpec(memory_space=pltpu.VMEM)
    message = pltpu.VMEM((CHUNKS, SHARDS, 32, LANES), BF16)
    parts = pl.pallas_call(
        kernel,
        out_shape=(
            jax.ShapeDtypeStruct((CHUNKS, 3, SHARDS, 16, LANES), BF16),
            jax.ShapeDtypeStruct((8, LANES), F32),
            jax.ShapeDtypeStruct((32, LANES), F32),
            jax.ShapeDtypeStruct((128, LANES), F32),
        ),
        in_specs=[vmem, vmem, vmem, pl.BlockSpec(memory_space=pltpu.SMEM), vmem],
        out_specs=(pl.BlockSpec(memory_space=pl.ANY), vmem, vmem, vmem),
        scratch_shapes=[
            pltpu.VMEM((CHUNKS, 3, SHARDS, 16, LANES), BF16),
            pltpu.VMEM((4, CHUNKS, SHARDS, 16, LANES), BF16),
            pltpu.VMEM((2, CHUNKS, SHARDS, 16, LANES), F32),
            pltpu.VMEM((CHUNKS, SHARDS, 16, LANES), BF16),
            pltpu.VMEM((512, LANES), F32),
            pltpu.VMEM((8, LANES, LANES + 8192), BF16),
            pltpu.VMEM((8, LANES + 8192), F32),
            pltpu.VMEM((6, 16, LANES), BF16),
            pltpu.VMEM((6, 16, LANES), BF16),
            pltpu.VMEM((CHUNKS, 3, 16, LANES), F32),
            pltpu.VMEM((256, 256), BF16),
            pltpu.VMEM((LANES, 9 * LANES), BF16),
            pltpu.VMEM((256, 256), BF16),
            pltpu.VMEM((LANES, LANES), BF16),
            pltpu.VMEM((9 * LANES, LANES), BF16),
            message, message, message, message,
            pltpu.VMEM((2, 1024, LANES), F32),
            pltpu.VMEM((2, 512, LANES), F32),
            pltpu.VMEM((2, 576, LANES), F32),
            pltpu.VMEM((QUAD, 2, 512, 256), BF16),
            pltpu.VMEM((QUAD, 256, 256), F32),
            pltpu.VMEM((2, 1024, LANES), F32),
            pltpu.VMEM((QUAD, 2, 4, 256, LANES), BF16),
            pltpu.VMEM((QUAD, LANES, 256), BF16),
            pltpu.VMEM((QUAD, LANES, LANES), BF16),
            pltpu.VMEM((2, 4, LANES, 256), F32),
            pltpu.VMEM((QUAD, LAGS, 8, LANES), F32),
            pltpu.VMEM((QUAD, LAGS + 1, 8, LANES), F32),
            pltpu.VMEM((QUAD, 4, 16, LANES), F32),
            pltpu.VMEM((REPS, 8, 16, LANES), BF16),
            pltpu.VMEM((REPS, 8, 16, LANES), BF16),
            pltpu.VMEM((CHUNKS, 3, SHARDS, 16, LANES), BF16),
            pltpu.VMEM((CHUNKS, 3, 2, SHARDS, 16, LANES), BF16),
            pltpu.VMEM((CHUNKS, 3, 16, LANES), F32),
            pltpu.VMEM((CHUNKS, 3, 16, LANES), BF16),
            pltpu.VMEM((CHUNKS, 3, 16, LANES), BF16),
            pltpu.VMEM((SHARDS * 8, LANES), F32),
            pltpu.VMEM((SHARDS, 4, LANES), F32),
            pltpu.VMEM((SHARDS, 4, LANES), F32),
            pltpu.SemaphoreType.DMA((2,)),
            pltpu.SemaphoreType.DMA((2, CHUNKS)),
            pltpu.SemaphoreType.DMA((CHUNKS,)),
            pltpu.SemaphoreType.DMA((CHUNKS, GROUP)),
            pltpu.SemaphoreType.DMA((2, CHUNKS)),
            pltpu.SemaphoreType.DMA((2,)),
            pltpu.SemaphoreType.DMA((2,)),
            pltpu.SemaphoreType.DMA((CHUNKS,)),
        ],
        compiler_params=pltpu.CompilerParams(
            collective_id=0, has_side_effects=True, vmem_limit_bytes=60 * 2**20
        ),
    )(features, cotangent, tap_rows, skip_gain, filters)
    steps = 2
    fixed = lambda *shape: pl.BlockSpec(shape, lambda i: (0,) * len(shape))
    d_feat, short, skips, lags = pl.pallas_call(
        finish,
        grid=(steps,),
        out_shape=(
            jax.ShapeDtypeStruct((3, 4, 512, LANES), BF16),
            jax.ShapeDtypeStruct((3, 3, 4, 8), F32),
            jax.ShapeDtypeStruct((4, 8), F32),
            jax.ShapeDtypeStruct((8, 2048), F32),
        ),
        in_specs=[
            pl.BlockSpec((CHUNKS, 3, SHARDS // steps, 16, LANES), lambda i: (0, 0, i, 0, 0)),
            fixed(8, LANES),
            fixed(32, LANES),
            fixed(128, LANES),
        ],
        out_specs=(
            pl.BlockSpec((3, 4, 512 // steps, LANES), lambda i: (0, 0, i, 0)),
            fixed(3, 3, 4, 8),
            fixed(4, 8),
            fixed(8, 2048),
        ),
    )(*parts)
    return (d_feat, jnp.transpose(short, (0, 2, 3, 1)), skips, lags)


def solution(mesh):
    placed = (
        P(None, "rep", None, "ctx"),
        P(None, "rep", None, None),
        P("rep", "ctx"),
        P("ctx", None),
        P("rep", None, "ctx"),
    )
    return jax.shard_map(
        per_device,
        mesh=mesh,
        in_specs=placed,
        out_specs=(
            P(None, "rep", None, "ctx"),
            P(None, "rep", "ctx", None),
            P("rep", "ctx"),
            P("ctx", "rep"),
        ),
        check_vma=False,
    )
```
